32 devices in a mesh: gx: 4 (over y, x), gy: 8 (over z, core).
Axes of the slice: x: 2, y: 2, z: 4, core: 2. Of those that a mesh axis runs over, the one named last changes fastest.
Arguments:
- image: float32 [512, 32768], P('gx', 'gy'), may hold values from -6 to 6
- psfs: bfloat16 [16, 16, 32, 1024], P('gx', 'gy'), may hold values from -0.11035156 to 0.11035156
Outputs:
- hessian_image: float32 [512, 32768], P('gx', 'gy')
The draws below stay inside these ranges and needn't reach their ends.
All inputs are finite; a program needn't handle non-finite values.
Results may differ from the reference program's by a relative error of at most 0.023.
Values may be sent and summed in bfloat16 or wider, within the bound.
No kernel may reach another device: no remote copies, remote signals or barrier semaphores. Data moves between devices by JAX's collectives and lax.ppermute only.
A program may use at most 128 MiB of HBM per device.

```python
import jax
import jax.numpy as jnp
from jax import lax

PATCH = 64
PSFW = 32
DEPTH = 64
FFTL = 96
NX = 512
NY = 512
GX = 16
GY = 16


def levels(own_key, extent, split, smallest, high):
    def one(dim, shards_of):
        steps = jax.random.uniform(jax.random.fold_in(jax.random.fold_in(own_key, 6), dim), (shards_of,), jnp.float32, smallest / len(split), high / len(split))
        return jnp.repeat(jnp.exp(steps), extent[dim] // shards_of).reshape((-1,) + (1,) * (len(extent) - dim - 1))

    factor_of = one(*split[0])
    for cut in split[1:]:
        factor_of = factor_of * one(*cut)
    return factor_of


def gaussian(rng, extent, scale, most, cuts=(), kind=jnp.bfloat16):
    factor_of = levels(rng, extent, cuts, -0.22, 0.18) if cuts else 1.0
    values = jax.random.normal(rng, extent, jnp.float32) * scale * factor_of
    return jnp.minimum(jnp.maximum(values, -most), most).astype(kind)


def setup_inputs(seed: int = 0) -> dict:
    splits = jax.random.split(jax.random.key(seed), 3)
    image = gaussian(splits[0], (NX, NY * DEPTH), 1.0, 6.0, ((0, 4), (1, 8)), jnp.float32)
    psfs = gaussian(splits[1], (GX, GY, PSFW, PSFW * PSFW), (3.2 / PSFW ** 1.5), 0.11035156, ((0, 4), (1, 8)))
    return dict(image=image, psfs=psfs)


BLEND = (0.125, 0.375, 0.375, 0.125)


def rounded(values):
    real_part = jnp.real(values).astype(jnp.bfloat16)
    imag_part = jnp.imag(values).astype(jnp.bfloat16)
    real_part, imag_part = lax.optimization_barrier((real_part, imag_part))
    return real_part.astype(jnp.float32) + 1j * imag_part.astype(jnp.float32)


def forward(cube):
    spectrum = rounded(jnp.fft.fft(cube, n=FFTL, axis=2))
    spectrum = rounded(jnp.fft.fft(spectrum, n=FFTL, axis=1))
    return rounded(jnp.fft.fft(spectrum, n=FFTL, axis=0))


def response(cells, psf):
    product = rounded(forward(cells) * forward(psf))
    back = rounded(jnp.fft.ifft(product, axis=0))
    back = rounded(jnp.fft.ifft(back, axis=1))
    whole = jnp.real(jnp.fft.ifft(back, axis=2))
    return whole[:, :, PSFW // 2:PSFW // 2 + DEPTH].astype(jnp.float32)


def reference(image, psfs):
    half = PSFW // 2
    field = image.reshape(NX, NY, DEPTH)
    padded_nodes = jnp.pad(psfs, ((1, 1), (1, 1), (0, 0), (0, 0)))
    weights = jnp.array(BLEND, jnp.float32)
    columns = NY // PATCH
    count = (NX // PATCH) * columns

    def step(total, index):
        row = index // columns
        column = index % columns
        zero = jnp.int32(0)
        cells = lax.dynamic_slice(field, (row * PATCH, column * PATCH, zero), (PATCH, PATCH, DEPTH))
        cells = lax.optimization_barrier(cells.astype(jnp.bfloat16)).astype(jnp.float32)
        window = lax.dynamic_slice(padded_nodes, (2 * row, 2 * column, zero, zero), (4, 4, PSFW, PSFW * PSFW))
        blended = jnp.einsum('a,b,abcd->cd', weights, weights, window.astype(jnp.float32))
        blended = lax.optimization_barrier(blended.astype(jnp.bfloat16)).astype(jnp.float32)
        part = response(cells, blended.reshape(PSFW, PSFW, PSFW))
        start = (row * PATCH, column * PATCH, zero)
        current = lax.dynamic_slice(total, start, (FFTL, FFTL, DEPTH))
        return lax.dynamic_update_slice(total, current + part, start), None

    total = jnp.zeros((NX + PSFW, NY + PSFW, DEPTH), jnp.float32)
    total, _ = lax.scan(step, total, jnp.arange(count, dtype=jnp.int32))
    return total[half:half + NX, half:half + NY].reshape(NX, NY * DEPTH)
```

```python
import math

import jax
import jax.numpy as jnp
import ml_dtypes
import numpy as np
from jax import lax
from jax.experimental import pallas as pl
from jax.experimental.pallas import tpu as pltpu
from jax.sharding import PartitionSpec as P

PATCH = 64
PSFW = 32
DEPTH = 64
BLEND = (0.125, 0.375, 0.375, 0.125)

HALF = PSFW // 2
LONG = PATCH + PSFW
KX = LONG // 2
KZ = DEPTH + HALF
LANES = 128
YPER = LANES // DEPTH
PPER = LANES // PSFW
YROWS = PATCH // YPER
PROWS = PSFW // PPER
OROWS = LONG // YPER
F32 = jnp.float32
BF16 = jnp.bfloat16


def constant(values):
    return jnp.asarray(np.asarray(values, np.float32).astype(ml_dtypes.bfloat16))


def angle(k, n, length):
    return 2.0 * math.pi * np.outer(k, n) / length


def complex_block(theta, sign):
    cosine, sine = np.cos(theta), sign * np.sin(theta)
    return np.stack([np.stack([cosine, -sine], 1), np.stack([sine, cosine], 1)], 0)


def x_forward(count):
    theta = angle(np.arange(KX) + 0.5, np.arange(count), LONG)
    return np.concatenate([np.cos(theta), -np.sin(theta)], 0)


def z_forward(count, per):
    block = complex_block(angle(np.arange(KZ), np.arange(count), KZ), -1.0)
    table = np.zeros((2, per, count, per, 2, LANES))
    for y in range(per):
        table[:, y, :, y, :, :KZ] = block.transpose(2, 3, 0, 1)
    return table.reshape(2 * per * count, per * 2 * LANES)


def y_forward(count, per):
    block = complex_block(angle(np.arange(LONG), np.arange(count), LONG), -1.0)
    block = block.reshape(2, LONG, 2, count // per, per).transpose(0, 1, 4, 2, 3)
    return block.reshape(2 * LONG, 2 * count)


def y_inverse():
    block = complex_block(angle(np.arange(LONG), np.arange(LONG), LONG).T, 1.0) / LONG
    block = block.reshape(2, OROWS, YPER, 2 * LONG).transpose(2, 0, 1, 3)
    return block.reshape(2 * LONG, 2 * LONG)


def z_inverse():
    block = complex_block(angle(np.arange(DEPTH) + HALF, np.arange(KZ), KZ), 1.0) / KZ
    table = np.zeros((YPER, 2, LANES, 2, YPER, DEPTH))
    for y in range(YPER):
        table[y, :, :KZ, :, y, :] = block.transpose(2, 3, 0, 1)
    return table.reshape(YPER * 2 * LANES, 2 * YPER * DEPTH)


def x_inverse(patches):
    theta = angle(np.arange(LONG), np.arange(KX) + 0.5, LONG)
    block = np.stack([np.cos(theta), -np.sin(theta)], 1) * (2.0 / LONG)
    rows = patches * PATCH
    table = np.zeros((rows + PSFW, patches, 2, KX))
    for p in range(patches):
        table[p * PATCH : p * PATCH + LONG, p] = block
    table = np.concatenate([table[HALF : HALF + rows], table[:HALF], table[HALF + rows :]], 0)
    return table.reshape(rows + PSFW, patches * 2 * KX)


def dot(a, b):
    return jnp.dot(a, b, preferred_element_type=F32)


def full(shape):
    return pl.BlockSpec(shape, lambda *_: (0,) * len(shape))


def image_kernel(image_ref, tx_ref, tz_ref, ty_ref, out_ref, swap, mid):
    tile = 2 * LANES
    rows = 2 * KX

    def along_x(t, _):
        cells = image_ref[:, pl.ds(pl.multiple_of(t * tile, tile), tile)].astype(BF16)
        result = dot(tx_ref[...], cells)
        for h in range(2):
            swap[pl.ds(2 * t + h, rows, stride=YROWS), :] = result[:, h * LANES : (h + 1) * LANES]
        return 0

    lax.fori_loop(0, PATCH * DEPTH // tile, along_x, 0, unroll=4)

    half = KX * YROWS
    chunk = 8 * YROWS

    def along_z(t, _):
        start = pl.multiple_of(t * chunk, chunk)
        left = jnp.concatenate(
            [swap[pl.ds(start, chunk), :], swap[pl.ds(half + start, chunk), :]], 1
        ).astype(BF16)
        mid[pl.ds(start, chunk), :] = dot(left, tz_ref[...]).astype(BF16)
        return 0

    lax.fori_loop(0, half // chunk, along_z, 0, unroll=2)

    def along_y(t, _):
        pieces = []
        for h in range(2):
            rows_at = pl.ds(pl.multiple_of((2 * t + h) * YROWS, YROWS), YROWS)
            pieces.append(
                jnp.concatenate(
                    [mid[rows_at, b * LANES : (b + 1) * LANES] for b in range(2 * YPER)], 0
                )
            )
        result = dot(ty_ref[...], jnp.concatenate(pieces, 1)).astype(BF16)
        for h in range(2):
            out_ref[2 * t + h] = result[:, h * LANES : (h + 1) * LANES]
        return 0

    lax.fori_loop(0, KX // 2, along_y, 0, unroll=2)


def image_forward(image, patch):
    tables = (
        constant(x_forward(PATCH)),
        constant(z_forward(DEPTH, YPER)),
        constant(y_forward(PATCH, YPER)),
    )
    return pl.pallas_call(
        image_kernel,
        grid=(1,),
        in_specs=[pl.BlockSpec((PATCH, image.shape[1]), lambda _: (patch, 0))]
        + [full(t.shape) for t in tables],
        out_specs=full((KX, 2 * LONG, LANES)),
        out_shape=jax.ShapeDtypeStruct((KX, 2 * LONG, LANES), BF16),
        scratch_shapes=[
            pltpu.VMEM((2 * KX * YROWS, LANES), F32),
            pltpu.VMEM((KX * YROWS, 2 * YPER * LANES), BF16),
        ],
        compiler_params=pltpu.CompilerParams(vmem_limit_bytes=24 << 20),
        cost_estimate=pl.CostEstimate(
            flops=4_000_000_000, bytes_accessed=4_000_000, transcendentals=0
        ),
        name="image_forward",
    )(image, *tables)


def blend_kernel(psfs_ref, before_ref, after_ref, first_ref, last_ref):
    count = psfs_ref.shape[0]
    for column, out in ((0, first_ref), (1, last_ref)):
        nodes = [before_ref[0, column]]
        nodes += [psfs_ref[i, column] for i in range(count)]
        nodes += [after_ref[0, column]]
        nodes = [n.astype(F32) for n in nodes]
        for p in range(count // 2):
            total = (nodes[2 * p] + nodes[2 * p + 3]) * BLEND[0]
            total += (nodes[2 * p + 1] + nodes[2 * p + 2]) * BLEND[1]
            out[p] = total.astype(BF16)


def blend_x(psfs, before, after):
    patches = psfs.shape[0] // 2
    shape = (patches,) + psfs.shape[2:]
    return pl.pallas_call(
        blend_kernel,
        out_shape=(jax.ShapeDtypeStruct(shape, BF16),) * 2,
        name="blend_x",
    )(psfs, before, after)


def respond_kernel(
    patches,
    *refs,
):
    spectra = refs[:patches]
    columns = refs[patches : patches + 4]
    tpx, tpz, tpy, tiy, tiz, tix = refs[patches + 4 : patches + 10]
    mid_ref, low_ref, high_ref = refs[patches + 10 : patches + 13]
    pswap, pmid, rows_y, grid_x = refs[patches + 13 :]
    tile = 2 * LANES

    for p in range(patches):
        for t in range(PSFW * PSFW // tile):
            data = jnp.concatenate([c[p, :, t * tile : (t + 1) * tile] for c in columns], 0)
            result = dot(tpx[...], data)
            for h in range(2):
                pswap[p, pl.ds(2 * t + h, 2 * KX, stride=PROWS), :] = result[
                    :, h * LANES : (h + 1) * LANES
                ]
    half = KX * PROWS
    for p in range(patches):
        left = jnp.concatenate([pswap[p, :half, :], pswap[p, half:, :]], 1).astype(BF16)
        for b in range(PPER):
            result = dot(left, tpz[:, b * tile : (b + 1) * tile])
            result = result.reshape(KX, PROWS, tile)
            both = jnp.concatenate([result[:, :, :LANES], result[:, :, LANES:]], 1)
            pmid[p, :, 2 * b * PROWS : 2 * (b + 1) * PROWS, :] = both.astype(BF16)

    def along_y(t, _):
        for p in range(patches):
            psf = dot(tpy[...], jnp.concatenate([pmid[p, 2 * t], pmid[p, 2 * t + 1]], 1))
            field = jnp.concatenate([spectra[p][2 * t], spectra[p][2 * t + 1]], 1).astype(F32)
            are, aim = field[:LONG], field[LONG:]
            bre, bim = psf[:LONG], psf[LONG:]
            product = jnp.concatenate([are * bre - aim * bim, are * bim + aim * bre], 0)
            back = dot(tiy[...], product.astype(BF16)).astype(BF16)
            for h in range(2):
                rows_at = pl.ds(pl.multiple_of((2 * t + h) * OROWS, OROWS), OROWS)
                for b in range(2 * YPER):
                    rows_y[p, rows_at, b * LANES : (b + 1) * LANES] = back[
                        b * OROWS : (b + 1) * OROWS, h * LANES : (h + 1) * LANES
                    ]
        return 0

    lax.fori_loop(0, KX // 2, along_y, 0, unroll=1)

    group = 8

    def along_z(t, _):
        for p in range(patches):
            start = pl.multiple_of(t * group * OROWS, group * OROWS)
            result = dot(rows_y[p, pl.ds(start, group * OROWS), :], tiz[...])
            for k in range(group):
                for c in range(2):
                    grid_x[p, c, pl.ds(t * group + k, OROWS, stride=KX), :] = result[
                        k * OROWS : (k + 1) * OROWS, c * LANES : (c + 1) * LANES
                    ]
        return 0

    lax.fori_loop(0, KX // group, along_z, 0)

    def along_x(t):
        pieces = []
        for p in range(patches):
            for c in range(2):
                parts = []
                for h in range(2):
                    start = (2 * t + h) * KX
                    if not isinstance(start, int):
                        start = pl.multiple_of(start, KX)
                    parts.append(grid_x[p, c, pl.ds(start, KX), :])
                pieces.append(jnp.concatenate(parts, 1).astype(BF16))
        return dot(tix[...], jnp.concatenate(pieces, 0))

    rim = HALF * DEPTH // tile
    inner = PATCH * DEPTH // tile
    for t in range(rim):
        low_ref[:, t * tile : (t + 1) * tile] = along_x(t).astype(BF16)
        high_ref[:, t * tile : (t + 1) * tile] = along_x(rim + inner + t).astype(BF16)

    def middle(t, _):
        mid_ref[:, pl.ds(pl.multiple_of(t * tile, tile), tile)] = along_x(rim + t)
        return 0

    lax.fori_loop(0, inner, middle, 0, unroll=2)


def respond(spectra, columns):
    patches = len(spectra)
    weighted = np.concatenate([w * x_forward(PSFW) for w in BLEND], 1)
    tables = (
        constant(weighted),
        constant(z_forward(PSFW, PPER)),
        constant(y_forward(PSFW, PPER)),
        constant(y_inverse()),
        constant(z_inverse()),
        constant(x_inverse(patches)),
    )
    rows = patches * PATCH + PSFW
    rim = (rows, HALF * DEPTH)
    operands = (*spectra, *columns, *tables)
    return pl.pallas_call(
        lambda *refs: respond_kernel(patches, *refs),
        out_shape=(
            jax.ShapeDtypeStruct((rows, PATCH * DEPTH), F32),
            jax.ShapeDtypeStruct(rim, BF16),
            jax.ShapeDtypeStruct(rim, BF16),
        ),
        scratch_shapes=[
            pltpu.VMEM((patches, 2 * KX * PROWS, LANES), F32),
            pltpu.VMEM((patches, KX, 2 * PSFW, LANES), BF16),
            pltpu.VMEM((patches, KX * OROWS, 2 * YPER * LANES), BF16),
            pltpu.VMEM((patches, 2, OROWS * KX, LANES), F32),
        ],
        compiler_params=pltpu.CompilerParams(vmem_limit_bytes=48 << 20),
        name="respond",
    )(*operands)


def rim_kernel(mid_ref, low_ref, high_ref, first_ref, last_ref):
    band = low_ref.shape[1]
    rows = mid_ref.shape[0] // 2
    for k, out in ((0, first_ref), (1, last_ref)):
        at = slice(k * rows, (k + 1) * rows)
        out[...] = mid_ref[at, :].astype(BF16)
        out[:, :band] = (mid_ref[at, :band] + low_ref[at, :].astype(F32)).astype(BF16)
        out[:, -band:] = (mid_ref[at, -band:] + high_ref[at, :].astype(F32)).astype(BF16)


def x_rims(mid, low, high):
    start = (mid.shape[0] - PSFW) // PSFW
    shape = jax.ShapeDtypeStruct((HALF, mid.shape[1]), BF16)
    return pl.pallas_call(
        rim_kernel,
        grid=(1,),
        in_specs=[
            pl.BlockSpec((PSFW, mid.shape[1]), lambda _: (start, 0)),
            pl.BlockSpec((PSFW, low.shape[1]), lambda _: (start, 0)),
            pl.BlockSpec((PSFW, high.shape[1]), lambda _: (start, 0)),
        ],
        out_specs=(full(shape.shape),) * 2,
        out_shape=(shape,) * 2,
        name="x_rims",
    )(mid, low, high)


def fold_kernel(mid_ref, low_ref, high_ref, before_ref, after_ref, out_ref):
    rows, band = out_ref.shape[0], low_ref.shape[1]
    out_ref[...] = mid_ref[...]
    out_ref[:, :band] += low_ref[...].astype(F32)
    out_ref[:, -band:] += high_ref[...].astype(F32)
    out_ref[:HALF, :] += before_ref[...].astype(F32)
    out_ref[rows - HALF :, :] += after_ref[...].astype(F32)


def fold(mid, low, high, before, after):
    rows = mid.shape[0] - PSFW
    return pl.pallas_call(
        fold_kernel,
        grid=(1,),
        in_specs=[
            pl.BlockSpec((rows, mid.shape[1]), lambda _: (0, 0)),
            pl.BlockSpec((rows, low.shape[1]), lambda _: (0, 0)),
            pl.BlockSpec((rows, high.shape[1]), lambda _: (0, 0)),
            full(before.shape),
            full(after.shape),
        ],
        out_specs=full((rows, mid.shape[1])),
        out_shape=jax.ShapeDtypeStruct((rows, mid.shape[1]), F32),
        compiler_params=pltpu.CompilerParams(vmem_limit_bytes=24 << 20),
        name="fold",
    )(mid, low, high, before, after)


def onward(value, axis):
    return lax.ppermute(value, axis, [(i, i + 1) for i in range(lax.axis_size(axis) - 1)])


def backward(value, axis):
    return lax.ppermute(value, axis, [(i + 1, i) for i in range(lax.axis_size(axis) - 1)])


def body(image, psfs):
    patches = image.shape[0] // PATCH
    before = onward(psfs[-1:], "gx")
    after = backward(psfs[:1], "gx")
    spectra = [image_forward(image, 0)]
    first, last = blend_x(psfs, before, after)
    left = onward(last, "gy")
    right = backward(first, "gy")
    spectra += [image_forward(image, p) for p in range(1, patches)]
    mid, low, high = respond(spectra, (left, first, last, right))
    from_left = onward(high, "gy")
    from_right = backward(low, "gy")
    first, last = x_rims(mid, from_left, from_right)
    before = onward(last, "gx")
    after = backward(first, "gx")
    return fold(mid, from_left, from_right, before, after)


def solution(mesh):
    placed = (P("gx", "gy"), P("gx", "gy", None, None))
    return jax.shard_map(body, mesh=mesh, in_specs=placed, out_specs=P("gx", "gy"), check_vma=False)
```

```python
import functools
import math

import jax
import jax.numpy as jnp
import ml_dtypes
import numpy as np
from jax import lax
from jax.experimental import pallas as pl
from jax.experimental.pallas import tpu as pltpu
from jax.sharding import PartitionSpec as P

PATCH = 64
PSFW = 32
DEPTH = 64
BLEND = (0.125, 0.375, 0.375, 0.125)

HALF = PSFW // 2
LONG = PATCH + PSFW
KX = LONG // 2
KZ = DEPTH + HALF
LANES = 128
YPER = LANES // DEPTH
PPER = LANES // PSFW
YROWS = PATCH // YPER
PROWS = PSFW // PPER
OROWS = LONG // YPER
F32 = jnp.float32
BF16 = jnp.bfloat16


def constant(values):
    return jnp.asarray(np.asarray(values, np.float32).astype(ml_dtypes.bfloat16))


def angle(k, n, length):
    return 2.0 * math.pi * np.outer(k, n) / length


def complex_block(theta, sign):
    cosine, sine = np.cos(theta), sign * np.sin(theta)
    return np.stack([np.stack([cosine, -sine], 1), np.stack([sine, cosine], 1)], 0)


def x_forward(count):
    theta = angle(np.arange(KX) + 0.5, np.arange(count), LONG)
    return np.concatenate([np.cos(theta), -np.sin(theta)], 0)


def z_forward(count, per):
    block = complex_block(angle(np.arange(KZ), np.arange(count), KZ), -1.0)
    table = np.zeros((2, per, count, per, 2, LANES))
    for y in range(per):
        table[:, y, :, y, :, :KZ] = block.transpose(2, 3, 0, 1)
    return table.reshape(2 * per * count, per * 2 * LANES)


def y_forward(count, per):
    block = complex_block(angle(np.arange(LONG), np.arange(count), LONG), -1.0)
    block = block.reshape(2, LONG, 2, count // per, per).transpose(0, 1, 4, 2, 3)
    return block.reshape(2 * LONG, 2 * count)


def y_inverse():
    block = complex_block(angle(np.arange(LONG), np.arange(LONG), LONG).T, 1.0) / LONG
    block = block.reshape(2, OROWS, YPER, 2 * LONG).transpose(2, 0, 1, 3)
    return block.reshape(2 * LONG, 2 * LONG)


def z_inverse():
    block = complex_block(angle(np.arange(DEPTH) + HALF, np.arange(KZ), KZ), 1.0) / KZ
    table = np.zeros((YPER, 2, LANES, 2, YPER, DEPTH))
    for y in range(YPER):
        table[y, :, :KZ, :, y, :] = block.transpose(2, 3, 0, 1)
    return table.reshape(YPER * 2 * LANES, 2 * YPER * DEPTH)


def x_inverse(patches):
    theta = angle(np.arange(LONG), np.arange(KX) + 0.5, LONG)
    block = np.stack([np.cos(theta), -np.sin(theta)], 1) * (2.0 / LONG)
    rows = patches * PATCH
    table = np.zeros((rows + PSFW, patches, 2, KX))
    for p in range(patches):
        table[p * PATCH : p * PATCH + LONG, p] = block
    table = np.concatenate([table[HALF : HALF + rows], table[:HALF], table[HALF + rows :]], 0)
    return table.reshape(rows + PSFW, patches * 2 * KX)


def dot(a, b):
    return jnp.dot(a, b, preferred_element_type=F32)


def full(shape):
    return pl.BlockSpec(shape, lambda *_: (0,) * len(shape))


def parity(axis):
    return lax.rem(lax.axis_index(axis), 2)


def pick(flag, even, odd):
    return jnp.where(flag == 0, even, odd)


def image_kernel(patch, image_ref, tx_ref, tz_ref, ty_ref, out_ref, swap, mid):
    tile = 2 * LANES
    rows = 2 * KX

    def along_x(t, _):
        at = pl.ds(pl.multiple_of(t * tile, tile), tile)
        cells = image_ref[patch * PATCH : (patch + 1) * PATCH, at].astype(BF16)
        result = dot(tx_ref[...], cells)
        for h in range(2):
            swap[pl.ds(2 * t + h, rows, stride=YROWS), :] = result[:, h * LANES : (h + 1) * LANES]
        return 0

    lax.fori_loop(0, PATCH * DEPTH // tile, along_x, 0, unroll=8)

    half = KX * YROWS
    chunk = 8 * YROWS

    def along_z(t, _):
        start = pl.multiple_of(t * chunk, chunk)
        left = jnp.concatenate(
            [swap[pl.ds(start, chunk), :], swap[pl.ds(half + start, chunk), :]], 1
        ).astype(BF16)
        mid[pl.ds(start, chunk), :] = dot(left, tz_ref[...]).astype(BF16)
        return 0

    lax.fori_loop(0, half // chunk, along_z, 0, unroll=3)

    def along_y(t, _):
        pieces = []
        for h in range(2):
            rows_at = pl.ds(pl.multiple_of((2 * t + h) * YROWS, YROWS), YROWS)
            pieces.append(
                jnp.concatenate(
                    [mid[rows_at, b * LANES : (b + 1) * LANES] for b in range(2 * YPER)], 0
                )
            )
        result = dot(ty_ref[...], jnp.concatenate(pieces, 1)).astype(BF16)
        for h in range(2):
            out_ref[2 * t + h] = result[:, h * LANES : (h + 1) * LANES]
        return 0

    lax.fori_loop(0, KX // 2, along_y, 0, unroll=8)


def image_forward(image, patch):
    tables = (
        constant(x_forward(PATCH)),
        constant(z_forward(DEPTH, YPER)),
        constant(y_forward(PATCH, YPER)),
    )
    return pl.pallas_call(
        functools.partial(image_kernel, patch),
        out_shape=jax.ShapeDtypeStruct((KX, 2 * LONG, LANES), BF16),
        scratch_shapes=[
            pltpu.VMEM((2 * KX * YROWS, LANES), F32),
            pltpu.VMEM((KX * YROWS, 2 * YPER * LANES), BF16),
        ],
        compiler_params=pltpu.CompilerParams(vmem_limit_bytes=16 << 20),
        cost_estimate=pl.CostEstimate(
            flops=4_000_000_000, bytes_accessed=4_000_000, transcendentals=0
        ),
        name="image_forward",
    )(image, *tables)


def blend_kernel(psfs_ref, even_ref, odd_ref, to_even_ref, to_odd_ref):
    count = psfs_ref.shape[0]
    gx, gy = parity("gx"), parity("gy")
    for out, column in ((to_even_ref, 1 - gy), (to_odd_ref, gy)):
        from_even = even_ref[0, column].astype(F32)
        from_odd = odd_ref[0, column].astype(F32)
        nodes = [pick(gx, from_odd, from_even)]
        nodes += [psfs_ref[i, column].astype(F32) for i in range(count)]
        nodes += [pick(gx, from_even, from_odd)]
        for p in range(count // 2):
            total = (nodes[2 * p] + nodes[2 * p + 3]) * BLEND[0]
            total += (nodes[2 * p + 1] + nodes[2 * p + 2]) * BLEND[1]
            out[p] = total.astype(BF16)


def blend_x(psfs, even, odd):
    shape = (psfs.shape[0] // 2,) + psfs.shape[2:]
    return pl.pallas_call(
        blend_kernel,
        out_shape=(jax.ShapeDtypeStruct(shape, BF16),) * 2,
        compiler_params=pltpu.CompilerParams(vmem_limit_bytes=16 << 20),
        name="blend_x",
    )(psfs, even, odd)


def respond_kernel(patches, *refs):
    spectra = refs[:patches]
    columns = refs[patches : patches + 4]
    tpx, tpz, tpy, tiy, tiz, tix = refs[patches + 4 : patches + 10]
    mid_ref, to_even_ref, to_odd_ref = refs[patches + 10 : patches + 13]
    pswap, pmid, rows_y, grid_x = refs[patches + 13 :]
    tile = 2 * LANES

    for p in range(patches):
        for t in range(PSFW * PSFW // tile):
            data = jnp.concatenate([c[p, :, t * tile : (t + 1) * tile] for c in columns], 0)
            result = dot(tpx[...], data)
            for h in range(2):
                pswap[p, pl.ds(2 * t + h, 2 * KX, stride=PROWS), :] = result[
                    :, h * LANES : (h + 1) * LANES
                ]
    half = KX * PROWS
    for p in range(patches):
        left = jnp.concatenate([pswap[p, :half, :], pswap[p, half:, :]], 1).astype(BF16)
        for b in range(PPER):
            result = dot(left, tpz[:, b * tile : (b + 1) * tile])
            result = result.reshape(KX, PROWS, tile)
            both = jnp.concatenate([result[:, :, :LANES], result[:, :, LANES:]], 1)
            pmid[p, :, 2 * b * PROWS : 2 * (b + 1) * PROWS, :] = both.astype(BF16)

    def along_y(t, _):
        for p in range(patches):
            psf = dot(tpy[...], jnp.concatenate([pmid[p, 2 * t], pmid[p, 2 * t + 1]], 1))
            field = jnp.concatenate([spectra[p][2 * t], spectra[p][2 * t + 1]], 1).astype(F32)
            are, aim = field[:LONG], field[LONG:]
            bre, bim = psf[:LONG], psf[LONG:]
            product = jnp.concatenate([are * bre - aim * bim, are * bim + aim * bre], 0)
            back = dot(tiy[...], product.astype(BF16)).astype(BF16)
            for h in range(2):
                rows_at = pl.ds(pl.multiple_of((2 * t + h) * OROWS, OROWS), OROWS)
                for b in range(2 * YPER):
                    rows_y[p, rows_at, b * LANES : (b + 1) * LANES] = back[
                        b * OROWS : (b + 1) * OROWS, h * LANES : (h + 1) * LANES
                    ]
        return 0

    lax.fori_loop(0, KX // 2, along_y, 0, unroll=8)

    group = 8

    def along_z(t, _):
        for p in range(patches):
            start = pl.multiple_of(t * group * OROWS, group * OROWS)
            result = dot(rows_y[p, pl.ds(start, group * OROWS), :], tiz[...])
            for k in range(group):
                for c in range(2):
                    grid_x[p, c, pl.ds(t * group + k, OROWS, stride=KX), :] = result[
                        k * OROWS : (k + 1) * OROWS, c * LANES : (c + 1) * LANES
                    ]
        return 0

    lax.fori_loop(0, KX // group, along_z, 0, unroll=2)

    def along_x(t):
        pieces = []
        for p in range(patches):
            for c in range(2):
                parts = []
                for h in range(2):
                    start = pl.multiple_of((2 * t + h) * KX, KX)
                    parts.append(grid_x[p, c, pl.ds(start, KX), :])
                pieces.append(jnp.concatenate(parts, 1).astype(BF16))
        return dot(tix[...], jnp.concatenate(pieces, 0))

    rim = HALF * DEPTH // tile
    inner = PATCH * DEPTH // tile
    flag = parity("gy")
    for out, first in ((to_even_ref, 1 - flag), (to_odd_ref, flag)):
        for t in range(rim):
            out[:, t * tile : (t + 1) * tile] = along_x(first * (rim + inner) + t).astype(BF16)

    def middle(t, _):
        mid_ref[:, pl.ds(pl.multiple_of(t * tile, tile), tile)] = along_x(rim + t)
        return 0

    lax.fori_loop(0, inner, middle, 0, unroll=4)


def respond(spectra, columns):
    patches = len(spectra)
    weighted = np.concatenate([w * x_forward(PSFW) for w in BLEND], 1)
    tables = (
        constant(weighted),
        constant(z_forward(PSFW, PPER)),
        constant(y_forward(PSFW, PPER)),
        constant(y_inverse()),
        constant(z_inverse()),
        constant(x_inverse(patches)),
    )
    rows = patches * PATCH + PSFW
    rim = (rows, HALF * DEPTH)
    operands = (*spectra, *columns, *tables)
    return pl.pallas_call(
        functools.partial(respond_kernel, patches),
        out_shape=(
            jax.ShapeDtypeStruct((rows, PATCH * DEPTH), F32),
            jax.ShapeDtypeStruct(rim, BF16),
            jax.ShapeDtypeStruct(rim, BF16),
        ),
        scratch_shapes=[
            pltpu.VMEM((patches, 2 * KX * PROWS, LANES), F32),
            pltpu.VMEM((patches, KX, 2 * PSFW, LANES), BF16),
            pltpu.VMEM((patches, KX * OROWS, 2 * YPER * LANES), BF16),
            pltpu.VMEM((patches, 2, OROWS * KX, LANES), F32),
        ],
        compiler_params=pltpu.CompilerParams(vmem_limit_bytes=32 << 20),
        name="respond",
    )(*operands)


def rim_kernel(mid_ref, even_ref, odd_ref, to_even_ref, to_odd_ref):
    band = even_ref.shape[1]
    rows = mid_ref.shape[0] - PSFW
    gx, gy = parity("gx"), parity("gy")
    for out, side in ((to_even_ref, 1 - gx), (to_odd_ref, gx)):
        at = pl.ds(pl.multiple_of(rows + side * HALF, HALF), HALF)
        low = pick(gy, odd_ref[at, :], even_ref[at, :]).astype(F32)
        high = pick(gy, even_ref[at, :], odd_ref[at, :]).astype(F32)
        out[:, band:-band] = mid_ref[at, band:-band].astype(BF16)
        out[:, :band] = (mid_ref[at, :band] + low).astype(BF16)
        out[:, -band:] = (mid_ref[at, -band:] + high).astype(BF16)


def x_rims(mid, even, odd):
    shape = jax.ShapeDtypeStruct((HALF, mid.shape[1]), BF16)
    return pl.pallas_call(
        rim_kernel,
        out_shape=(shape,) * 2,
        compiler_params=pltpu.CompilerParams(vmem_limit_bytes=16 << 20),
        name="x_rims",
    )(mid, even, odd)


def fold_kernel(mid_ref, even_y_ref, odd_y_ref, even_x_ref, odd_x_ref, out_ref):
    rows, columns = out_ref.shape
    band = even_y_ref.shape[1]
    gx, gy = parity("gx"), parity("gy")
    out_ref[...] = mid_ref[:rows, :]
    for ref, side in ((even_y_ref, 1 - gy), (odd_y_ref, gy)):
        at = pl.ds(pl.multiple_of(side * (columns - band), band), band)
        out_ref[:, at] += ref[:rows, :].astype(F32)
    for ref, side in ((even_x_ref, 1 - gx), (odd_x_ref, gx)):
        at = pl.ds(pl.multiple_of(side * (rows - HALF), HALF), HALF)
        out_ref[at, :] += ref[...].astype(F32)


def fold(mid, *received):
    rows = mid.shape[0] - PSFW
    return pl.pallas_call(
        fold_kernel,
        out_shape=jax.ShapeDtypeStruct((rows, mid.shape[1]), F32),
        compiler_params=pltpu.CompilerParams(vmem_limit_bytes=16 << 20),
        name="fold",
    )(mid, *received)


def swap_even(value, axis):
    count = lax.axis_size(axis)
    return lax.ppermute(value, axis, [(i, i ^ 1) for i in range(count) if i ^ 1 < count])


def swap_odd(value, axis):
    ends = [i + 1 if i % 2 else i - 1 for i in range(lax.axis_size(axis))]
    pairs = [(i, j) for i, j in enumerate(ends) if 0 <= j < len(ends)]
    return lax.ppermute(value, axis, pairs)


def body(image, psfs):
    patches = image.shape[0] // PATCH
    last = psfs.shape[0] - 1
    gx = parity("gx")
    to_odd = lax.dynamic_slice_in_dim(psfs, gx * last, 1, 0)
    to_even = lax.dynamic_slice_in_dim(psfs, (1 - gx) * last, 1, 0)
    odd = swap_odd(to_odd, "gx")
    even = swap_even(to_even, "gx")
    spectra = [image_forward(image, 0)]
    to_even, to_odd = blend_x(psfs, even, odd)
    odd = swap_odd(to_odd, "gy")
    even = swap_even(to_even, "gy")
    spectra += [image_forward(image, p) for p in range(1, patches)]
    mid, out_even, out_odd = respond(spectra, (odd, to_odd, to_even, even))
    odd_y = swap_odd(out_odd, "gy")
    even_y = swap_even(out_even, "gy")
    out_even, out_odd = x_rims(mid, even_y, odd_y)
    odd_x = swap_odd(out_odd, "gx")
    even_x = swap_even(out_even, "gx")
    return fold(mid, even_y, odd_y, even_x, odd_x)


def solution(mesh):
    placed = (P("gx", "gy"), P("gx", "gy", None, None))
    return jax.shard_map(body, mesh=mesh, in_specs=placed, out_specs=P("gx", "gy"), check_vma=False)
```

```python
import functools
import math

import jax
import jax.numpy as jnp
import ml_dtypes
import numpy as np
from jax import lax
from jax.experimental import pallas as pl
from jax.experimental.pallas import tpu as pltpu
from jax.sharding import PartitionSpec as P

PATCH = 64
PSFW = 32
DEPTH = 64
BLEND = (0.125, 0.375, 0.375, 0.125)

HALF = PSFW // 2
LONG = PATCH + PSFW
KX = LONG // 2
KZ = DEPTH + HALF
LANES = 128
YPER = LANES // DEPTH
PPER = LANES // PSFW
YROWS = PATCH // YPER
PROWS = PSFW // PPER
OROWS = LONG // YPER
RIM = HALF // YPER
EDGE = 2 * RIM
F32 = jnp.float32
BF16 = jnp.bfloat16


def constant(values):
    return jnp.asarray(np.asarray(values, np.float32).astype(ml_dtypes.bfloat16))


def angle(k, n, length):
    return 2.0 * math.pi * np.outer(k, n) / length


def complex_block(theta, sign):
    cosine, sine = np.cos(theta), sign * np.sin(theta)
    return np.stack([np.stack([cosine, -sine], 1), np.stack([sine, cosine], 1)], 0)


def x_forward(count):
    theta = angle(np.arange(KX) + 0.5, np.arange(count), LONG)
    return np.concatenate([np.cos(theta), -np.sin(theta)], 0)


def z_forward(count, per):
    block = complex_block(angle(np.arange(KZ), np.arange(count), KZ), -1.0)
    table = np.zeros((2, per, count, per, 2, LANES))
    for y in range(per):
        table[:, y, :, y, :, :KZ] = block.transpose(2, 3, 0, 1)
    return table.reshape(2 * per * count, per * 2 * LANES)


def y_forward(count, per):
    block = complex_block(angle(np.arange(LONG), np.arange(count), LONG), -1.0)
    block = block.reshape(2, LONG, 2, count // per, per).transpose(0, 1, 4, 2, 3)
    return block.reshape(2 * LONG, 2 * count)


def y_inverse():
    block = complex_block(angle(np.arange(LONG), np.arange(LONG), LONG).T, 1.0) / LONG
    block = block.reshape(2, OROWS, YPER, 2 * LONG).transpose(2, 0, 1, 3)
    block = np.concatenate([block[:, :, :RIM], block[:, :, -RIM:], block[:, :, RIM:-RIM]], 2)
    return block.reshape(2 * LONG, 2 * LONG)


def z_inverse():
    block = complex_block(angle(np.arange(DEPTH) + HALF, np.arange(KZ), KZ), 1.0) / KZ
    table = np.zeros((YPER, 2, LANES, 2, YPER, DEPTH))
    for y in range(YPER):
        table[y, :, :KZ, :, y, :] = block.transpose(2, 3, 0, 1)
    return table.reshape(YPER * 2 * LANES, 2 * YPER * DEPTH)


def x_inverse(patches):
    theta = angle(np.arange(LONG), np.arange(KX) + 0.5, LONG)
    block = np.stack([np.cos(theta), -np.sin(theta)], 1) * (2.0 / LONG)
    rows = patches * PATCH
    table = np.zeros((rows + PSFW, patches, 2, KX))
    for p in range(patches):
        table[p * PATCH : p * PATCH + LONG, p] = block
    table = np.concatenate([table[HALF : HALF + rows], table[:HALF], table[HALF + rows :]], 0)
    return table.reshape(rows + PSFW, patches * 2 * KX)


def dot(a, b):
    return jnp.dot(a, b, preferred_element_type=F32)


def full(shape):
    return pl.BlockSpec(shape, lambda *_: (0,) * len(shape))


def parity(axis):
    return lax.rem(lax.axis_index(axis), 2)


def pick(flag, even, odd):
    return jnp.where(flag == 0, even, odd)


def image_kernel(patch, image_ref, tx_ref, tz_ref, ty_ref, out_ref, swap, mid, ready=None):
    tile = 2 * LANES
    rows = 2 * KX

    def along_x(t, _):
        at = pl.ds(pl.multiple_of(t * tile, tile), tile)
        cells = image_ref[patch * PATCH : (patch + 1) * PATCH, at].astype(BF16)
        result = dot(tx_ref[...], cells)
        for h in range(2):
            swap[pl.ds(2 * t + h, rows, stride=YROWS), :] = result[:, h * LANES : (h + 1) * LANES]
        return 0

    steps = PATCH * DEPTH // tile
    if ready is None:
        lax.fori_loop(0, steps, along_x, 0, unroll=8)
    else:
        for t in range(steps):
            ready(t, steps)
            along_x(t, 0)

    half = KX * YROWS
    chunk = 8 * YROWS

    def along_z(t, _):
        start = pl.multiple_of(t * chunk, chunk)
        left = jnp.concatenate(
            [swap[pl.ds(start, chunk), :], swap[pl.ds(half + start, chunk), :]], 1
        ).astype(BF16)
        mid[pl.ds(start, chunk), :] = dot(left, tz_ref[...]).astype(BF16)
        return 0

    lax.fori_loop(0, half // chunk, along_z, 0, unroll=3)

    def along_y(t, _):
        pieces = []
        for h in range(2):
            rows_at = pl.ds(pl.multiple_of((2 * t + h) * YROWS, YROWS), YROWS)
            pieces.append(
                jnp.concatenate(
                    [mid[rows_at, b * LANES : (b + 1) * LANES] for b in range(2 * YPER)], 0
                )
            )
        result = dot(ty_ref[...], jnp.concatenate(pieces, 1)).astype(BF16)
        for h in range(2):
            out_ref[2 * t + h] = result[:, h * LANES : (h + 1) * LANES]
        return 0

    lax.fori_loop(0, KX // 2, along_y, 0, unroll=8)


PARTS = 4


def fetching_kernel(patch, image_hbm, *refs):
    tables_hbm, out_ref, swap, mid, cells = refs[:3], *refs[3:7]
    tables, sems = refs[7:10], refs[10]
    width = cells.shape[1] // PARTS
    parts = [
        pltpu.make_async_copy(
            image_hbm.at[pl.ds(patch * PATCH, PATCH), pl.ds(k * width, width)],
            cells.at[:, pl.ds(k * width, width)],
            sems.at[k],
        )
        for k in range(PARTS)
    ]
    fetched = [
        pltpu.make_async_copy(a, b, sems.at[PARTS + k])
        for k, (a, b) in enumerate(zip(tables_hbm, tables))
    ]
    for copy in [fetched[0], parts[0], *fetched[1:], *parts[1:]]:
        copy.start()

    def ready(t, steps):
        if t == 0:
            fetched[0].wait()
        if t % (steps // PARTS) == 0:
            parts[t // (steps // PARTS)].wait()
        if t == steps - 1:
            fetched[1].wait()
            fetched[2].wait()

    image_kernel(0, cells, *tables, out_ref, swap, mid, ready)


def image_forward(image, patch):
    tables = (
        constant(x_forward(PATCH)),
        constant(z_forward(DEPTH, YPER)),
        constant(y_forward(PATCH, YPER)),
    )
    scratch = [
        pltpu.VMEM((2 * KX * YROWS, LANES), F32),
        pltpu.VMEM((KX * YROWS, 2 * YPER * LANES), BF16),
    ]
    common = dict(
        out_shape=jax.ShapeDtypeStruct((KX, 2 * LONG, LANES), BF16),
        compiler_params=pltpu.CompilerParams(vmem_limit_bytes=16 << 20),
        cost_estimate=pl.CostEstimate(
            flops=4_000_000_000, bytes_accessed=4_000_000, transcendentals=0
        ),
    )
    if patch:
        return pl.pallas_call(
            functools.partial(image_kernel, patch),
            scratch_shapes=scratch,
            name="image_forward",
            **common,
        )(image, *tables)
    return pl.pallas_call(
        functools.partial(fetching_kernel, patch),
        in_specs=[pl.BlockSpec(memory_space=pltpu.HBM)] * 4,
        out_specs=pl.BlockSpec(memory_space=pltpu.VMEM),
        scratch_shapes=scratch
        + [pltpu.VMEM((PATCH, image.shape[1]), F32)]
        + [pltpu.VMEM(t.shape, BF16) for t in tables]
        + [pltpu.SemaphoreType.DMA((PARTS + len(tables),))],
        name="image_first",
        **common,
    )(*[pltpu.with_memory_space_constraint(x, pltpu.HBM) for x in (image, *tables)])


def blend_kernel(psfs_ref, even_ref, odd_ref, to_even_ref, to_odd_ref):
    count = psfs_ref.shape[0]
    gx, gy = parity("gx"), parity("gy")
    for out, column in ((to_even_ref, 1 - gy), (to_odd_ref, gy)):
        from_even = even_ref[0, column].astype(F32)
        from_odd = odd_ref[0, column].astype(F32)
        nodes = [pick(gx, from_odd, from_even)]
        nodes += [psfs_ref[i, column].astype(F32) for i in range(count)]
        nodes += [pick(gx, from_even, from_odd)]
        for p in range(count // 2):
            total = (nodes[2 * p] + nodes[2 * p + 3]) * BLEND[0]
            total += (nodes[2 * p + 1] + nodes[2 * p + 2]) * BLEND[1]
            out[p] = total.astype(BF16)


def blend_x(psfs, even, odd):
    shape = (psfs.shape[0] // 2,) + psfs.shape[2:]
    return pl.pallas_call(
        blend_kernel,
        out_shape=(jax.ShapeDtypeStruct(shape, BF16),) * 2,
        compiler_params=pltpu.CompilerParams(vmem_limit_bytes=16 << 20),
        name="blend_x",
    )(psfs, even, odd)


def z_swapped(rows_ref, tiz, grid_ref, p, pairs, group):
    def along_z(t, _):
        start = pl.multiple_of(t * group * pairs, group * pairs)
        result = dot(rows_ref[p, pl.ds(start, group * pairs), :], tiz[...])
        for k in range(group):
            for c in range(2):
                grid_ref[p, c, pl.ds(t * group + k, pairs, stride=KX), :] = result[
                    k * pairs : (k + 1) * pairs, c * LANES : (c + 1) * LANES
                ]
        return 0

    lax.fori_loop(0, KX // group, along_z, 0, unroll=True)


def x_inverted(grid_ref, tix, t):
    pieces = []
    for p in range(grid_ref.shape[0]):
        for c in range(2):
            parts = []
            for h in range(2):
                start = pl.multiple_of((2 * t + h) * KX, KX)
                parts.append(grid_ref[p, c, pl.ds(start, KX), :])
            pieces.append(jnp.concatenate(parts, 1).astype(BF16))
    return dot(tix[...], jnp.concatenate(pieces, 0))


def respond_kernel(patches, *refs):
    spectra = refs[:patches]
    columns = refs[patches : patches + 4]
    tpx, tpz, tpy, tiy, tiz, tix = refs[patches + 4 : patches + 10]
    inner_ref, to_even_ref, to_odd_ref = refs[patches + 10 : patches + 13]
    pswap, pmid, edge_rows, grid_x = refs[patches + 13 :]
    tile = 2 * LANES

    for p in range(patches):
        for t in range(PSFW * PSFW // tile):
            data = jnp.concatenate([c[p, :, t * tile : (t + 1) * tile] for c in columns], 0)
            result = dot(tpx[...], data)
            for h in range(2):
                pswap[p, pl.ds(2 * t + h, 2 * KX, stride=PROWS), :] = result[
                    :, h * LANES : (h + 1) * LANES
                ]
    half = KX * PROWS
    for p in range(patches):
        left = jnp.concatenate([pswap[p, :half, :], pswap[p, half:, :]], 1).astype(BF16)
        for b in range(PPER):
            result = dot(left, tpz[:, b * tile : (b + 1) * tile])
            result = result.reshape(KX, PROWS, tile)
            both = jnp.concatenate([result[:, :, :LANES], result[:, :, LANES:]], 1)
            pmid[p, :, 2 * b * PROWS : 2 * (b + 1) * PROWS, :] = both.astype(BF16)

    inner = OROWS - EDGE

    def along_y(t, _):
        for p in range(patches):
            psf = dot(tpy[...], jnp.concatenate([pmid[p, 2 * t], pmid[p, 2 * t + 1]], 1))
            field = jnp.concatenate([spectra[p][2 * t], spectra[p][2 * t + 1]], 1).astype(F32)
            are, aim = field[:LONG], field[LONG:]
            bre, bim = psf[:LONG], psf[LONG:]
            product = jnp.concatenate([are * bre - aim * bim, are * bim + aim * bre], 0)
            back = dot(tiy[...], product.astype(BF16)).astype(BF16)
            for h in range(2):
                edge_at = pl.ds(pl.multiple_of((2 * t + h) * EDGE, EDGE), EDGE)
                inner_at = pl.ds(pl.multiple_of((2 * t + h) * inner, inner), inner)
                for b in range(2 * YPER):
                    block = back[b * OROWS : (b + 1) * OROWS, h * LANES : (h + 1) * LANES]
                    at = slice(b * LANES, (b + 1) * LANES)
                    edge_rows[p, edge_at, at] = block[:EDGE]
                    inner_ref[p, inner_at, at] = block[EDGE:]
        return 0

    lax.fori_loop(0, KX // 2, along_y, 0, unroll=8)

    for p in range(patches):
        z_swapped(edge_rows, tiz, grid_x, p, EDGE, KX // 2)
    flag = parity("gy")
    rim = RIM // 2
    for out, first in ((to_even_ref, 1 - flag), (to_odd_ref, flag)):
        for t in range(rim):
            out[:, t * tile : (t + 1) * tile] = x_inverted(grid_x, tix, first * rim + t).astype(BF16)


def respond(spectra, columns):
    patches = len(spectra)
    weighted = np.concatenate([w * x_forward(PSFW) for w in BLEND], 1)
    z_table = constant(z_inverse())
    x_table = constant(x_inverse(patches))
    tables = (
        constant(weighted),
        constant(z_forward(PSFW, PPER)),
        constant(y_forward(PSFW, PPER)),
        constant(y_inverse()),
        z_table,
        x_table,
    )
    rows = patches * PATCH + PSFW
    rim = (rows, HALF * DEPTH)
    inner = OROWS - EDGE
    inner_rows, out_even, out_odd = pl.pallas_call(
        functools.partial(respond_kernel, patches),
        out_shape=(
            jax.ShapeDtypeStruct((patches, KX * inner, 2 * YPER * LANES), BF16),
            jax.ShapeDtypeStruct(rim, BF16),
            jax.ShapeDtypeStruct(rim, BF16),
        ),
        scratch_shapes=[
            pltpu.VMEM((patches, 2 * KX * PROWS, LANES), F32),
            pltpu.VMEM((patches, KX, 2 * PSFW, LANES), BF16),
            pltpu.VMEM((patches, KX * EDGE, 2 * YPER * LANES), BF16),
            pltpu.VMEM((patches, 2, EDGE * KX, LANES), F32),
        ],
        compiler_params=pltpu.CompilerParams(vmem_limit_bytes=24 << 20),
        name="respond",
    )(*spectra, *columns, *tables)

    def middle():
        return pl.pallas_call(
            middle_kernel,
            out_shape=jax.ShapeDtypeStruct((rows, PATCH * DEPTH), F32),
            scratch_shapes=[pltpu.VMEM((patches, 2, inner * KX, LANES), F32)],
            compiler_params=pltpu.CompilerParams(vmem_limit_bytes=24 << 20),
            cost_estimate=pl.CostEstimate(
                flops=3_000_000_000, bytes_accessed=6_000_000, transcendentals=0
            ),
            name="middle",
        )(inner_rows, z_table, x_table)

    return middle, out_even, out_odd


def middle_kernel(rows_ref, tiz, tix, out_ref, grid_x):
    tile = 2 * LANES
    inner = OROWS - EDGE
    for p in range(rows_ref.shape[0]):
        z_swapped(rows_ref, tiz, grid_x, p, inner, KX // 4)

    def along_x(t, _):
        out_ref[:, pl.ds(pl.multiple_of(t * tile, tile), tile)] = x_inverted(grid_x, tix, t)
        return 0

    lax.fori_loop(0, inner // 2, along_x, 0, unroll=4)


def rim_kernel(mid_ref, even_ref, odd_ref, to_even_ref, to_odd_ref):
    band = even_ref.shape[1]
    rows = mid_ref.shape[0] - PSFW
    gx, gy = parity("gx"), parity("gy")
    for out, side in ((to_even_ref, 1 - gx), (to_odd_ref, gx)):
        at = pl.ds(pl.multiple_of(rows + side * HALF, HALF), HALF)
        low = pick(gy, odd_ref[at, :], even_ref[at, :]).astype(F32)
        high = pick(gy, even_ref[at, :], odd_ref[at, :]).astype(F32)
        out[:, band:-band] = mid_ref[at, band:-band].astype(BF16)
        out[:, :band] = (mid_ref[at, :band] + low).astype(BF16)
        out[:, -band:] = (mid_ref[at, -band:] + high).astype(BF16)


def x_rims(mid, even, odd):
    shape = jax.ShapeDtypeStruct((HALF, mid.shape[1]), BF16)
    return pl.pallas_call(
        rim_kernel,
        out_shape=(shape,) * 2,
        compiler_params=pltpu.CompilerParams(vmem_limit_bytes=16 << 20),
        name="x_rims",
    )(mid, even, odd)


def fold_kernel(mid_ref, even_y_ref, odd_y_ref, even_x_ref, odd_x_ref, out_ref):
    rows, columns = out_ref.shape
    band = even_y_ref.shape[1]
    gx, gy = parity("gx"), parity("gy")
    out_ref[...] = mid_ref[:rows, :]
    for ref, side in ((even_y_ref, 1 - gy), (odd_y_ref, gy)):
        at = pl.ds(pl.multiple_of(side * (columns - band), band), band)
        out_ref[:, at] += ref[:rows, :].astype(F32)
    for ref, side in ((even_x_ref, 1 - gx), (odd_x_ref, gx)):
        at = pl.ds(pl.multiple_of(side * (rows - HALF), HALF), HALF)
        out_ref[at, :] += ref[...].astype(F32)


def fold(mid, *received):
    rows = mid.shape[0] - PSFW
    return pl.pallas_call(
        fold_kernel,
        out_shape=jax.ShapeDtypeStruct((rows, mid.shape[1]), F32),
        compiler_params=pltpu.CompilerParams(vmem_limit_bytes=16 << 20),
        name="fold",
    )(mid, *received)


def swap_even(value, axis):
    count = lax.axis_size(axis)
    return lax.ppermute(value, axis, [(i, i ^ 1) for i in range(count) if i ^ 1 < count])


def swap_odd(value, axis):
    ends = [i + 1 if i % 2 else i - 1 for i in range(lax.axis_size(axis))]
    pairs = [(i, j) for i, j in enumerate(ends) if 0 <= j < len(ends)]
    return lax.ppermute(value, axis, pairs)


def body(image, psfs):
    patches = image.shape[0] // PATCH
    last = psfs.shape[0] - 1
    gx = parity("gx")
    to_odd = lax.dynamic_slice_in_dim(psfs, gx * last, 1, 0)
    to_even = lax.dynamic_slice_in_dim(psfs, (1 - gx) * last, 1, 0)
    even = swap_even(to_even, "gx")
    odd = swap_odd(to_odd, "gx")
    spectra = [image_forward(image, 0)]
    spectra[0], even, odd = lax.optimization_barrier((spectra[0], even, odd))
    to_even, to_odd = blend_x(psfs, even, odd)
    image, to_even, to_odd = lax.optimization_barrier((image, to_even, to_odd))
    even = swap_even(to_even, "gy")
    odd = swap_odd(to_odd, "gy")
    spectra += [image_forward(image, p) for p in range(1, patches)]
    middle, out_even, out_odd = respond(spectra, (odd, to_odd, to_even, even))
    odd_y = swap_odd(out_odd, "gy")
    even_y = swap_even(out_even, "gy")
    mid = middle()
    out_even, out_odd = x_rims(mid, even_y, odd_y)
    even_x = swap_even(out_even, "gx")
    odd_x = swap_odd(out_odd, "gx")
    return fold(mid, even_y, odd_y, even_x, odd_x)


def solution(mesh):
    placed = (P("gx", "gy"), P("gx", "gy", None, None))
    return jax.shard_map(body, mesh=mesh, in_specs=placed, out_specs=P("gx", "gy"), check_vma=False)
```

```python
import functools
import math

import jax
import jax.numpy as jnp
import ml_dtypes
import numpy as np
from jax import lax
from jax.experimental import pallas as pl
from jax.experimental.pallas import tpu as pltpu
from jax.sharding import PartitionSpec as P

PATCH = 64
PSFW = 32
DEPTH = 64
BLEND = (0.125, 0.375, 0.375, 0.125)

HALF = PSFW // 2
LONG = PATCH + PSFW
KX = LONG // 2
KZ = DEPTH + HALF
LANES = 128
YPER = LANES // DEPTH
PPER = LANES // PSFW
YROWS = PATCH // YPER
PROWS = PSFW // PPER
OROWS = LONG // YPER
RIM = HALF // YPER
EDGE = 2 * RIM
YSTEP = YROWS + 2
XSTEP = KX + 2
F32 = jnp.float32
BF16 = jnp.bfloat16


def constant(values):
    return jnp.asarray(np.asarray(values, np.float32).astype(ml_dtypes.bfloat16))


def angle(k, n, length):
    return 2.0 * math.pi * np.outer(k, n) / length


def complex_block(theta, sign):
    cosine, sine = np.cos(theta), sign * np.sin(theta)
    return np.stack([np.stack([cosine, -sine], 1), np.stack([sine, cosine], 1)], 0)


def x_forward(count):
    theta = angle(np.arange(KX) + 0.5, np.arange(count), LONG)
    return np.concatenate([np.cos(theta), -np.sin(theta)], 0)


def z_forward(count, per):
    block = complex_block(angle(np.arange(KZ), np.arange(count), KZ), -1.0)
    table = np.zeros((2, per, count, per, 2, LANES))
    for y in range(per):
        table[:, y, :, y, :, :KZ] = block.transpose(2, 3, 0, 1)
    return table.reshape(2 * per * count, per * 2 * LANES)


def y_forward(count, per):
    block = complex_block(angle(np.arange(LONG), np.arange(count), LONG), -1.0)
    block = block.reshape(2, LONG, 2, count // per, per).transpose(0, 1, 4, 2, 3)
    return block.reshape(2 * LONG, 2 * count)


def y_inverse():
    block = complex_block(angle(np.arange(LONG), np.arange(LONG), LONG).T, 1.0) / LONG
    block = block.reshape(2, OROWS, YPER, 2 * LONG).transpose(2, 0, 1, 3)
    edge = np.concatenate([block[:, :, :RIM], block[:, :, -RIM:]], 2)
    inner = block[:, :, RIM:-RIM]
    return edge.reshape(-1, 2 * LONG), inner.reshape(-1, 2 * LONG)


def z_inverse():
    block = complex_block(angle(np.arange(DEPTH) + HALF, np.arange(KZ), KZ), 1.0) / KZ
    table = np.zeros((YPER, 2, LANES, 2, YPER, DEPTH))
    for y in range(YPER):
        table[y, :, :KZ, :, y, :] = block.transpose(2, 3, 0, 1)
    return table.reshape(YPER * 2 * LANES, 2 * YPER * DEPTH)


def x_inverse(patches):
    theta = angle(np.arange(LONG), np.arange(KX) + 0.5, LONG)
    block = np.stack([np.cos(theta), -np.sin(theta)], 1) * (2.0 / LONG)
    rows = patches * PATCH
    table = np.zeros((rows + PSFW, patches, 2, KX))
    for p in range(patches):
        table[p * PATCH : p * PATCH + LONG, p] = block
    table = np.concatenate([table[HALF : HALF + rows], table[:HALF], table[HALF + rows :]], 0)
    return table.reshape(rows + PSFW, patches * 2 * KX)


def dot(a, b):
    return jnp.dot(a, b, preferred_element_type=F32)


def full(shape):
    return pl.BlockSpec(shape, lambda *_: (0,) * len(shape))


def parity(axis):
    return lax.rem(lax.axis_index(axis), 2)


def pick(flag, even, odd):
    return jnp.where(flag == 0, even, odd)


def image_kernel(patch, image_ref, tx_ref, tz_ref, ty_ref, out_ref, swap, mid, ready=None):
    tile = 2 * LANES
    rows = 2 * KX

    def along_x(t, _):
        at = pl.ds(pl.multiple_of(t * tile, tile), tile)
        cells = image_ref[patch * PATCH : (patch + 1) * PATCH, at].astype(BF16)
        result = dot(tx_ref[...], cells)
        for h in range(2):
            swap[pl.ds(2 * t + h, rows, stride=YSTEP), :] = result[:, h * LANES : (h + 1) * LANES]
        return 0

    steps = PATCH * DEPTH // tile
    if ready is None:
        lax.fori_loop(0, steps, along_x, 0, unroll=8)
    else:
        for t in range(steps):
            ready(t, steps)
            along_x(t, 0)

    group = 8

    def along_z(t):
        left = [
            jnp.concatenate(
                [
                    swap[pl.ds((c * KX + t * group + k) * YSTEP, YROWS), :].astype(BF16)
                    for k in range(group)
                ],
                0,
            )
            for c in range(2)
        ]
        chunk = group * YROWS
        result = dot(jnp.concatenate(left, 1), tz_ref[...])
        mid[t * chunk : (t + 1) * chunk, :] = result.astype(BF16)

    for t in range(KX // group):
        along_z(t)

    def along_y(t, _):
        pieces = []
        for h in range(2):
            rows_at = pl.ds(pl.multiple_of((2 * t + h) * YROWS, YROWS), YROWS)
            pieces.append(
                jnp.concatenate(
                    [mid[rows_at, b * LANES : (b + 1) * LANES] for b in range(2 * YPER)], 0
                )
            )
        result = dot(ty_ref[...], jnp.concatenate(pieces, 1)).astype(BF16)
        for h in range(2):
            out_ref[2 * t + h] = result[:, h * LANES : (h + 1) * LANES]
        return 0

    lax.fori_loop(0, KX // 2, along_y, 0, unroll=True)


PARTS = 4


def fetching_kernel(patch, image_hbm, *refs):
    tables_hbm, out_ref, swap, mid, cells = refs[:3], *refs[3:7]
    tables, sems = refs[7:10], refs[10]
    width = cells.shape[1] // PARTS
    parts = [
        pltpu.make_async_copy(
            image_hbm.at[pl.ds(patch * PATCH, PATCH), pl.ds(k * width, width)],
            cells.at[:, pl.ds(k * width, width)],
            sems.at[k],
        )
        for k in range(PARTS)
    ]
    fetched = [
        pltpu.make_async_copy(a, b, sems.at[PARTS + k])
        for k, (a, b) in enumerate(zip(tables_hbm, tables))
    ]
    for copy in [fetched[0], parts[0], *fetched[1:], *parts[1:]]:
        copy.start()

    def ready(t, steps):
        if t == 0:
            fetched[0].wait()
        if t % (steps // PARTS) == 0:
            parts[t // (steps // PARTS)].wait()
        if t == steps - 1:
            fetched[1].wait()
            fetched[2].wait()

    image_kernel(0, cells, *tables, out_ref, swap, mid, ready)


def image_forward(image, patch):
    tables = (
        constant(x_forward(PATCH)),
        constant(z_forward(DEPTH, YPER)),
        constant(y_forward(PATCH, YPER)),
    )
    scratch = [
        pltpu.VMEM((2 * KX * YSTEP, LANES), F32),
        pltpu.VMEM((KX * YROWS, 2 * YPER * LANES), BF16),
    ]
    common = dict(
        out_shape=jax.ShapeDtypeStruct((KX, 2 * LONG, LANES), BF16),
        compiler_params=pltpu.CompilerParams(vmem_limit_bytes=16 << 20),
        cost_estimate=pl.CostEstimate(
            flops=4_000_000_000, bytes_accessed=4_000_000, transcendentals=0
        ),
    )
    if patch:
        return pl.pallas_call(
            functools.partial(image_kernel, patch),
            scratch_shapes=scratch,
            name="image_forward",
            **common,
        )(image, *tables)
    return pl.pallas_call(
        functools.partial(fetching_kernel, patch),
        in_specs=[pl.BlockSpec(memory_space=pltpu.HBM)] * 4,
        out_specs=pl.BlockSpec(memory_space=pltpu.VMEM),
        scratch_shapes=scratch
        + [pltpu.VMEM((PATCH, image.shape[1]), F32)]
        + [pltpu.VMEM(t.shape, BF16) for t in tables]
        + [pltpu.SemaphoreType.DMA((PARTS + len(tables),))],
        name="image_first",
        **common,
    )(*[pltpu.with_memory_space_constraint(x, pltpu.HBM) for x in (image, *tables)])


def blend_kernel(psfs_ref, even_ref, odd_ref, to_even_ref, to_odd_ref):
    count = psfs_ref.shape[0]
    gx, gy = parity("gx"), parity("gy")
    for out, column in ((to_even_ref, 1 - gy), (to_odd_ref, gy)):
        from_even = even_ref[0, column].astype(F32)
        from_odd = odd_ref[0, column].astype(F32)
        nodes = [pick(gx, from_odd, from_even)]
        nodes += [psfs_ref[i, column].astype(F32) for i in range(count)]
        nodes += [pick(gx, from_even, from_odd)]
        for p in range(count // 2):
            total = (nodes[2 * p] + nodes[2 * p + 3]) * BLEND[0]
            total += (nodes[2 * p + 1] + nodes[2 * p + 2]) * BLEND[1]
            out[p] = total.astype(BF16)


def blend_x(psfs, even, odd):
    shape = (psfs.shape[0] // 2,) + psfs.shape[2:]
    return pl.pallas_call(
        blend_kernel,
        out_shape=(jax.ShapeDtypeStruct(shape, BF16),) * 2,
        compiler_params=pltpu.CompilerParams(vmem_limit_bytes=16 << 20),
        name="blend_x",
    )(psfs, even, odd)


def y_inverted(tiy, product, rows_ref, p, t):
    back = dot(tiy[...], product).astype(BF16)
    pairs = back.shape[0] // (2 * YPER)
    for h in range(2):
        at = pl.ds(pl.multiple_of((2 * t + h) * pairs, pairs), pairs)
        for b in range(2 * YPER):
            rows_ref[p, at, b * LANES : (b + 1) * LANES] = back[
                b * pairs : (b + 1) * pairs, h * LANES : (h + 1) * LANES
            ]


def z_swapped(rows_ref, tiz, grid_ref, p, pairs, group):
    def along_z(t, _):
        start = pl.multiple_of(t * group * pairs, group * pairs)
        result = dot(rows_ref[p, pl.ds(start, group * pairs), :], tiz[...])
        for k in range(group):
            for c in range(2):
                grid_ref[p, c, pl.ds(t * group + k, pairs, stride=XSTEP), :] = result[
                    k * pairs : (k + 1) * pairs, c * LANES : (c + 1) * LANES
                ]
        return 0

    lax.fori_loop(0, KX // group, along_z, 0, unroll=True)


def x_inverted(grid_ref, tix, t):
    pieces = []
    for p in range(grid_ref.shape[0]):
        for c in range(2):
            parts = []
            for h in range(2):
                parts.append(grid_ref[p, c, pl.ds((2 * t + h) * XSTEP, KX), :])
            pieces.append(jnp.concatenate(parts, 1).astype(BF16))
    return dot(tix[...], jnp.concatenate(pieces, 0))


def respond_kernel(patches, *refs):
    spectra = refs[:patches]
    columns = refs[patches : patches + 4]
    tpx, tpz, tpy, tiy, tiz, tix = refs[patches + 4 : patches + 10]
    product_ref, to_even_ref, to_odd_ref = refs[patches + 10 : patches + 13]
    pswap, pmid, edge_rows, grid_x = refs[patches + 13 :]
    tile = 2 * LANES

    for p in range(patches):
        for t in range(PSFW * PSFW // tile):
            data = jnp.concatenate([c[p, :, t * tile : (t + 1) * tile] for c in columns], 0)
            result = dot(tpx[...], data)
            for h in range(2):
                pswap[p, pl.ds(2 * t + h, 2 * KX, stride=PROWS), :] = result[
                    :, h * LANES : (h + 1) * LANES
                ]
    half = KX * PROWS
    for p in range(patches):
        left = jnp.concatenate([pswap[p, :half, :], pswap[p, half:, :]], 1).astype(BF16)
        for b in range(PPER):
            result = dot(left, tpz[:, b * tile : (b + 1) * tile])
            result = result.reshape(KX, PROWS, tile)
            both = jnp.concatenate([result[:, :, :LANES], result[:, :, LANES:]], 1)
            pmid[p, :, 2 * b * PROWS : 2 * (b + 1) * PROWS, :] = both.astype(BF16)

    def along_y(t, _):
        for p in range(patches):
            psf = dot(tpy[...], jnp.concatenate([pmid[p, 2 * t], pmid[p, 2 * t + 1]], 1))
            field = jnp.concatenate([spectra[p][2 * t], spectra[p][2 * t + 1]], 1).astype(F32)
            are, aim = field[:LONG], field[LONG:]
            bre, bim = psf[:LONG], psf[LONG:]
            product = jnp.concatenate([are * bre - aim * bim, are * bim + aim * bre], 0)
            product_ref[p, t] = product.astype(BF16)
        return 0

    lax.fori_loop(0, KX // 2, along_y, 0, unroll=True)

    def back_along_y(t, _):
        for p in range(patches):
            y_inverted(tiy, product_ref[p, t], edge_rows, p, t)
        return 0

    lax.fori_loop(0, KX // 2, back_along_y, 0, unroll=True)
    for p in range(patches):
        z_swapped(edge_rows, tiz, grid_x, p, EDGE, KX // 2)
    flag = parity("gy")
    rim = RIM // 2
    for out, first in ((to_even_ref, 1 - flag), (to_odd_ref, flag)):
        for t in range(rim):
            out[:, t * tile : (t + 1) * tile] = x_inverted(grid_x, tix, first * rim + t).astype(BF16)


def respond(spectra, columns):
    patches = len(spectra)
    weighted = np.concatenate([w * x_forward(PSFW) for w in BLEND], 1)
    edge_table, inner_table = [constant(t) for t in y_inverse()]
    z_table = constant(z_inverse())
    x_table = constant(x_inverse(patches))
    tables = (
        constant(weighted),
        constant(z_forward(PSFW, PPER)),
        constant(y_forward(PSFW, PPER)),
        edge_table,
        z_table,
        x_table,
    )
    rows = patches * PATCH + PSFW
    rim = (rows, HALF * DEPTH)
    inner = OROWS - EDGE
    product, out_even, out_odd = pl.pallas_call(
        functools.partial(respond_kernel, patches),
        out_shape=(
            jax.ShapeDtypeStruct((patches, KX // 2, 2 * LONG, 2 * LANES), BF16),
            jax.ShapeDtypeStruct(rim, BF16),
            jax.ShapeDtypeStruct(rim, BF16),
        ),
        scratch_shapes=[
            pltpu.VMEM((patches, 2 * KX * PROWS, LANES), F32),
            pltpu.VMEM((patches, KX, 2 * PSFW, LANES), BF16),
            pltpu.VMEM((patches, KX * EDGE, 2 * YPER * LANES), BF16),
            pltpu.VMEM((patches, 2, EDGE * XSTEP, LANES), F32),
        ],
        compiler_params=pltpu.CompilerParams(vmem_limit_bytes=24 << 20),
        name="respond",
    )(*spectra, *columns, *tables)

    def middle():
        return pl.pallas_call(
            middle_kernel,
            out_shape=jax.ShapeDtypeStruct((rows, PATCH * DEPTH), F32),
            scratch_shapes=[
                pltpu.VMEM((patches, KX * inner, 2 * YPER * LANES), BF16),
                pltpu.VMEM((patches, 2, inner * XSTEP, LANES), F32),
            ],
            compiler_params=pltpu.CompilerParams(vmem_limit_bytes=24 << 20),
            cost_estimate=pl.CostEstimate(
                flops=3_000_000_000, bytes_accessed=6_000_000, transcendentals=0
            ),
            name="middle",
        )(product, inner_table, z_table, x_table)

    return middle, out_even, out_odd


def middle_kernel(product_ref, tiy, tiz, tix, out_ref, rows_ref, grid_x):
    tile = 2 * LANES
    patches = product_ref.shape[0]
    inner = OROWS - EDGE

    def along_y(t, _):
        for p in range(patches):
            y_inverted(tiy, product_ref[p, t], rows_ref, p, t)
        return 0

    lax.fori_loop(0, KX // 2, along_y, 0, unroll=True)
    for p in range(patches):
        z_swapped(rows_ref, tiz, grid_x, p, inner, 8)
    for t in range(inner // 2):
        out_ref[:, t * tile : (t + 1) * tile] = x_inverted(grid_x, tix, t)


def rim_kernel(mid_ref, even_ref, odd_ref, to_even_ref, to_odd_ref):
    band = even_ref.shape[1]
    rows = mid_ref.shape[0] - PSFW
    gx, gy = parity("gx"), parity("gy")
    for out, side in ((to_even_ref, 1 - gx), (to_odd_ref, gx)):
        at = pl.ds(pl.multiple_of(rows + side * HALF, HALF), HALF)
        low = pick(gy, odd_ref[at, :], even_ref[at, :]).astype(F32)
        high = pick(gy, even_ref[at, :], odd_ref[at, :]).astype(F32)
        out[:, band:-band] = mid_ref[at, band:-band].astype(BF16)
        out[:, :band] = (mid_ref[at, :band] + low).astype(BF16)
        out[:, -band:] = (mid_ref[at, -band:] + high).astype(BF16)


def x_rims(mid, even, odd):
    shape = jax.ShapeDtypeStruct((HALF, mid.shape[1]), BF16)
    return pl.pallas_call(
        rim_kernel,
        out_shape=(shape,) * 2,
        compiler_params=pltpu.CompilerParams(vmem_limit_bytes=16 << 20),
        name="x_rims",
    )(mid, even, odd)


def fold_kernel(mid_ref, even_ref, odd_ref, out_ref, rims_ref):
    rows, columns = out_ref.shape
    band = even_ref.shape[1]
    gy = parity("gy")
    out_ref[...] = mid_ref[:rows, :]
    for ref, side in ((even_ref, 1 - gy), (odd_ref, gy)):
        at = pl.ds(pl.multiple_of(side * (columns - band), band), band)
        out_ref[:, at] += ref[:rows, :].astype(F32)
    rims_ref[:HALF, :] = out_ref[:HALF, :]
    rims_ref[HALF:, :] = out_ref[rows - HALF :, :]


def fold(mid, even, odd):
    rows = mid.shape[0] - PSFW
    return pl.pallas_call(
        fold_kernel,
        out_shape=(
            jax.ShapeDtypeStruct((rows, mid.shape[1]), F32),
            jax.ShapeDtypeStruct((2 * HALF, mid.shape[1]), F32),
        ),
        compiler_params=pltpu.CompilerParams(vmem_limit_bytes=16 << 20),
        cost_estimate=pl.CostEstimate(
            flops=10_000_000, bytes_accessed=8_000_000, transcendentals=0
        ),
        name="fold",
    )(mid, even, odd)


def close_kernel(out_in, rims_ref, even_ref, odd_ref, out_ref, total, sems):
    del out_in
    gx = parity("gx")
    copies = []
    for k, (ref, side) in enumerate(((even_ref, 1 - gx), (odd_ref, gx))):
        at = pl.ds(pl.multiple_of(side * HALF, HALF), HALF)
        total[k] = rims_ref[at, :] + ref[...].astype(F32)
        first = pl.multiple_of(side * (out_ref.shape[0] - HALF), HALF)
        copies.append(
            pltpu.make_async_copy(total.at[k], out_ref.at[pl.ds(first, HALF), :], sems.at[k])
        )
        copies[-1].start()
    for copy in copies:
        copy.wait()


def close(out, rims, even, odd):
    vmem = pl.BlockSpec(memory_space=pltpu.VMEM)
    return pl.pallas_call(
        close_kernel,
        in_specs=[pl.BlockSpec(memory_space=pl.ANY), vmem, vmem, vmem],
        out_specs=pl.BlockSpec(memory_space=pl.ANY),
        out_shape=jax.ShapeDtypeStruct(out.shape, F32),
        scratch_shapes=[
            pltpu.VMEM((2, HALF, out.shape[1]), F32),
            pltpu.SemaphoreType.DMA((2,)),
        ],
        input_output_aliases={0: 0},
        compiler_params=pltpu.CompilerParams(vmem_limit_bytes=16 << 20),
        name="close",
    )(out, rims, even, odd)


def swap_even(value, axis):
    count = lax.axis_size(axis)
    return lax.ppermute(value, axis, [(i, i ^ 1) for i in range(count) if i ^ 1 < count])


def swap_odd(value, axis):
    ends = [i + 1 if i % 2 else i - 1 for i in range(lax.axis_size(axis))]
    pairs = [(i, j) for i, j in enumerate(ends) if 0 <= j < len(ends)]
    return lax.ppermute(value, axis, pairs)


def body(image, psfs):
    patches = image.shape[0] // PATCH
    last = psfs.shape[0] - 1
    gx = parity("gx")
    to_odd = lax.dynamic_slice_in_dim(psfs, gx * last, 1, 0)
    to_even = lax.dynamic_slice_in_dim(psfs, (1 - gx) * last, 1, 0)
    even = swap_even(to_even, "gx")
    odd = swap_odd(to_odd, "gx")
    spectra = [image_forward(image, 0)]
    spectra[0], even, odd = lax.optimization_barrier((spectra[0], even, odd))
    to_even, to_odd = blend_x(psfs, even, odd)
    image, to_even, to_odd = lax.optimization_barrier((image, to_even, to_odd))
    even = swap_even(to_even, "gy")
    odd = swap_odd(to_odd, "gy")
    spectra += [image_forward(image, p) for p in range(1, patches)]
    middle, out_even, out_odd = respond(spectra, (odd, to_odd, to_even, even))
    odd_y = swap_odd(out_odd, "gy")
    even_y = swap_even(out_even, "gy")
    mid = middle()
    out_even, out_odd = x_rims(mid, even_y, odd_y)
    even_x = swap_even(out_even, "gx")
    odd_x = swap_odd(out_odd, "gx")
    out, rims = fold(mid, even_y, odd_y)
    return close(out, rims, even_x, odd_x)


def solution(mesh):
    placed = (P("gx", "gy"), P("gx", "gy", None, None))
    return jax.shard_map(body, mesh=mesh, in_specs=placed, out_specs=P("gx", "gy"), check_vma=False)
```

```python
import functools
import math

import jax
import jax.numpy as jnp
import ml_dtypes
import numpy as np
from jax import lax
from jax.experimental import pallas as pl
from jax.experimental.pallas import tpu as pltpu
from jax.sharding import PartitionSpec as P

PATCH = 64
PSFW = 32
DEPTH = 64
BLEND = (0.125, 0.375, 0.375, 0.125)

HALF = PSFW // 2
LONG = PATCH + PSFW
KX = LONG // 2
KZ = DEPTH + HALF
LANES = 128
YPER = LANES // DEPTH
PPER = LANES // PSFW
YROWS = PATCH // YPER
PROWS = PSFW // PPER
OROWS = LONG // YPER
RIM = HALF // YPER
EDGE = 2 * RIM
YSTEP = YROWS + 2
XSTEP = KX + 2
F32 = jnp.float32
BF16 = jnp.bfloat16


def constant(values):
    return jnp.asarray(np.asarray(values, np.float32).astype(ml_dtypes.bfloat16))


def angle(k, n, length):
    return 2.0 * math.pi * np.outer(k, n) / length


def complex_block(theta, sign):
    cosine, sine = np.cos(theta), sign * np.sin(theta)
    return np.stack([np.stack([cosine, -sine], 1), np.stack([sine, cosine], 1)], 0)


def x_forward(count):
    theta = angle(np.arange(KX) + 0.5, np.arange(count), LONG)
    return np.concatenate([np.cos(theta), -np.sin(theta)], 0)


def z_forward(count, per):
    block = complex_block(angle(np.arange(KZ), np.arange(count), KZ), -1.0)
    table = np.zeros((2, per, count, per, 2, LANES))
    for y in range(per):
        table[:, y, :, y, :, :KZ] = block.transpose(2, 3, 0, 1)
    return table.reshape(2 * per * count, per * 2 * LANES)


def y_forward(count, per):
    block = complex_block(angle(np.arange(LONG), np.arange(count), LONG), -1.0)
    block = block.reshape(2, LONG, 2, count // per, per).transpose(0, 1, 4, 2, 3)
    return block.reshape(2 * LONG, 2 * count)


def y_inverse():
    block = complex_block(angle(np.arange(LONG), np.arange(LONG), LONG).T, 1.0) / LONG
    block = block.reshape(2, OROWS, YPER, 2 * LONG).transpose(2, 0, 1, 3)
    edge = np.concatenate([block[:, :, :RIM], block[:, :, -RIM:]], 2)
    inner = block[:, :, RIM:-RIM]
    return edge.reshape(-1, 2 * LONG), inner.reshape(-1, 2 * LONG)


def z_inverse():
    block = complex_block(angle(np.arange(DEPTH) + HALF, np.arange(KZ), KZ), 1.0) / KZ
    table = np.zeros((YPER, 2, LANES, 2, YPER, DEPTH))
    for y in range(YPER):
        table[y, :, :KZ, :, y, :] = block.transpose(2, 3, 0, 1)
    return table.reshape(YPER * 2 * LANES, 2 * YPER * DEPTH)


def x_inverse(patches):
    theta = angle(np.arange(LONG), np.arange(KX) + 0.5, LONG)
    block = np.stack([np.cos(theta), -np.sin(theta)], 1) * (2.0 / LONG)
    rows = patches * PATCH
    table = np.zeros((rows + PSFW, patches, 2, KX))
    for p in range(patches):
        table[p * PATCH : p * PATCH + LONG, p] = block
    table = np.concatenate([table[HALF : HALF + rows], table[:HALF], table[HALF + rows :]], 0)
    return table.reshape(rows + PSFW, patches * 2 * KX)


def dot(a, b):
    return jnp.dot(a, b, preferred_element_type=F32)


def full(shape):
    return pl.BlockSpec(shape, lambda *_: (0,) * len(shape))


def parity(axis):
    return lax.rem(lax.axis_index(axis), 2)


def pick(flag, even, odd):
    return jnp.where(flag == 0, even, odd)


def image_kernel(patch, image_ref, tx_ref, tz_ref, ty_ref, out_ref, swap, mid, ready=None):
    tile = 2 * LANES
    rows = 2 * KX

    def along_x(t, _):
        at = pl.ds(pl.multiple_of(t * tile, tile), tile)
        cells = image_ref[patch * PATCH : (patch + 1) * PATCH, at].astype(BF16)
        result = dot(tx_ref[...], cells)
        for h in range(2):
            swap[pl.ds(2 * t + h, rows, stride=YSTEP), :] = result[:, h * LANES : (h + 1) * LANES]
        return 0

    steps = PATCH * DEPTH // tile
    if ready is None:
        lax.fori_loop(0, steps, along_x, 0, unroll=8)
    else:
        for t in range(steps):
            ready(t, steps)
            along_x(t, 0)

    group = 8

    def along_z(t):
        left = [
            jnp.concatenate(
                [
                    swap[pl.ds((c * KX + t * group + k) * YSTEP, YROWS), :].astype(BF16)
                    for k in range(group)
                ],
                0,
            )
            for c in range(2)
        ]
        chunk = group * YROWS
        result = dot(jnp.concatenate(left, 1), tz_ref[...])
        mid[t * chunk : (t + 1) * chunk, :] = result.astype(BF16)

    for t in range(KX // group):
        along_z(t)

    def along_y(t, _):
        pieces = []
        for h in range(2):
            rows_at = pl.ds(pl.multiple_of((2 * t + h) * YROWS, YROWS), YROWS)
            pieces.append(
                jnp.concatenate(
                    [mid[rows_at, b * LANES : (b + 1) * LANES] for b in range(2 * YPER)], 0
                )
            )
        result = dot(ty_ref[...], jnp.concatenate(pieces, 1)).astype(BF16)
        for h in range(2):
            out_ref[2 * t + h] = result[:, h * LANES : (h + 1) * LANES]
        return 0

    lax.fori_loop(0, KX // 2, along_y, 0, unroll=True)


PARTS = 4


def fetching_kernel(patch, image_hbm, *refs):
    tables_hbm, out_ref, swap, mid, cells = refs[:3], *refs[3:7]
    tables, sems = refs[7:10], refs[10]
    width = cells.shape[1] // PARTS
    parts = [
        pltpu.make_async_copy(
            image_hbm.at[pl.ds(patch * PATCH, PATCH), pl.ds(k * width, width)],
            cells.at[:, pl.ds(k * width, width)],
            sems.at[k],
        )
        for k in range(PARTS)
    ]
    fetched = [
        pltpu.make_async_copy(a, b, sems.at[PARTS + k])
        for k, (a, b) in enumerate(zip(tables_hbm, tables))
    ]
    for copy in [fetched[0], parts[0], *fetched[1:], *parts[1:]]:
        copy.start()

    def ready(t, steps):
        if t == 0:
            fetched[0].wait()
        if t % (steps // PARTS) == 0:
            parts[t // (steps // PARTS)].wait()
        if t == steps - 1:
            fetched[1].wait()
            fetched[2].wait()

    image_kernel(0, cells, *tables, out_ref, swap, mid, ready)


def image_forward(image, patch):
    tables = (
        constant(x_forward(PATCH)),
        constant(z_forward(DEPTH, YPER)),
        constant(y_forward(PATCH, YPER)),
    )
    scratch = [
        pltpu.VMEM((2 * KX * YSTEP, LANES), F32),
        pltpu.VMEM((KX * YROWS, 2 * YPER * LANES), BF16),
    ]
    common = dict(
        out_shape=jax.ShapeDtypeStruct((KX, 2 * LONG, LANES), BF16),
        compiler_params=pltpu.CompilerParams(vmem_limit_bytes=16 << 20),
        cost_estimate=pl.CostEstimate(
            flops=4_000_000_000, bytes_accessed=4_000_000, transcendentals=0
        ),
    )
    if patch:
        return pl.pallas_call(
            functools.partial(image_kernel, patch),
            scratch_shapes=scratch,
            name="image_forward",
            **common,
        )(image, *tables)
    return pl.pallas_call(
        functools.partial(fetching_kernel, patch),
        in_specs=[pl.BlockSpec(memory_space=pltpu.HBM)] * 4,
        out_specs=pl.BlockSpec(memory_space=pltpu.VMEM),
        scratch_shapes=scratch
        + [pltpu.VMEM((PATCH, image.shape[1]), F32)]
        + [pltpu.VMEM(t.shape, BF16) for t in tables]
        + [pltpu.SemaphoreType.DMA((PARTS + len(tables),))],
        name="image_first",
        **common,
    )(*[pltpu.with_memory_space_constraint(x, pltpu.HBM) for x in (image, *tables)])


def blend_kernel(psfs_ref, odd_ref, even_ref, to_even_ref, to_odd_ref):
    count = psfs_ref.shape[0]
    gx, gy = parity("gx"), parity("gy")
    for out, column in ((to_even_ref, 1 - gy), (to_odd_ref, gy)):
        from_even = even_ref[0, column].astype(F32)
        from_odd = odd_ref[0, column].astype(F32)
        nodes = [pick(gx, from_odd, from_even)]
        nodes += [psfs_ref[i, column].astype(F32) for i in range(count)]
        nodes += [pick(gx, from_even, from_odd)]
        for p in range(count // 2):
            total = (nodes[2 * p] + nodes[2 * p + 3]) * BLEND[0]
            total += (nodes[2 * p + 1] + nodes[2 * p + 2]) * BLEND[1]
            out[p] = total.astype(BF16)


def blend_x(psfs, odd, even):
    shape = (psfs.shape[0] // 2,) + psfs.shape[2:]
    return pl.pallas_call(
        blend_kernel,
        out_shape=(jax.ShapeDtypeStruct(shape, BF16),) * 2,
        compiler_params=pltpu.CompilerParams(vmem_limit_bytes=16 << 20),
        name="blend_x",
    )(psfs, odd, even)


def y_inverted(tiy, product, rows_ref, p, t):
    back = dot(tiy[...], product).astype(BF16)
    pairs = back.shape[0] // (2 * YPER)
    for h in range(2):
        at = pl.ds(pl.multiple_of((2 * t + h) * pairs, pairs), pairs)
        for b in range(2 * YPER):
            rows_ref[p, at, b * LANES : (b + 1) * LANES] = back[
                b * pairs : (b + 1) * pairs, h * LANES : (h + 1) * LANES
            ]


def z_swapped(rows_ref, tiz, grid_ref, p, pairs, group):
    def along_z(t, _):
        start = pl.multiple_of(t * group * pairs, group * pairs)
        result = dot(rows_ref[p, pl.ds(start, group * pairs), :], tiz[...])
        for k in range(group):
            for c in range(2):
                grid_ref[p, c, pl.ds(t * group + k, pairs, stride=XSTEP), :] = result[
                    k * pairs : (k + 1) * pairs, c * LANES : (c + 1) * LANES
                ]
        return 0

    lax.fori_loop(0, KX // group, along_z, 0, unroll=True)


def x_inverted(grid_ref, tix, t):
    pieces = []
    for p in range(grid_ref.shape[0]):
        for c in range(2):
            parts = []
            for h in range(2):
                parts.append(grid_ref[p, c, pl.ds((2 * t + h) * XSTEP, KX), :])
            pieces.append(jnp.concatenate(parts, 1).astype(BF16))
    return dot(tix[...], jnp.concatenate(pieces, 0))


def respond_kernel(patches, *refs):
    spectra = refs[:patches]
    columns = refs[patches : patches + 4]
    tpx, tpz, tpy, tiy, tiz, tix = refs[patches + 4 : patches + 10]
    product_ref, to_even_ref, to_odd_ref = refs[patches + 10 : patches + 13]
    pswap, pmid, edge_rows, grid_x = refs[patches + 13 :]
    tile = 2 * LANES

    for p in range(patches):
        for t in range(PSFW * PSFW // tile):
            data = jnp.concatenate([c[p, :, t * tile : (t + 1) * tile] for c in columns], 0)
            result = dot(tpx[...], data)
            for h in range(2):
                pswap[p, pl.ds(2 * t + h, 2 * KX, stride=PROWS), :] = result[
                    :, h * LANES : (h + 1) * LANES
                ]
    half = KX * PROWS
    for p in range(patches):
        left = jnp.concatenate([pswap[p, :half, :], pswap[p, half:, :]], 1).astype(BF16)
        for b in range(PPER):
            result = dot(left, tpz[:, b * tile : (b + 1) * tile])
            result = result.reshape(KX, PROWS, tile)
            both = jnp.concatenate([result[:, :, :LANES], result[:, :, LANES:]], 1)
            pmid[p, :, 2 * b * PROWS : 2 * (b + 1) * PROWS, :] = both.astype(BF16)

    def along_y(t, _):
        for p in range(patches):
            psf = dot(tpy[...], jnp.concatenate([pmid[p, 2 * t], pmid[p, 2 * t + 1]], 1))
            field = jnp.concatenate([spectra[p][2 * t], spectra[p][2 * t + 1]], 1).astype(F32)
            are, aim = field[:LONG], field[LONG:]
            bre, bim = psf[:LONG], psf[LONG:]
            product = jnp.concatenate([are * bre - aim * bim, are * bim + aim * bre], 0)
            product_ref[p, t] = product.astype(BF16)
        return 0

    lax.fori_loop(0, KX // 2, along_y, 0, unroll=True)

    def back_along_y(t, _):
        for p in range(patches):
            y_inverted(tiy, product_ref[p, t], edge_rows, p, t)
        return 0

    lax.fori_loop(0, KX // 2, back_along_y, 0, unroll=True)
    for p in range(patches):
        z_swapped(edge_rows, tiz, grid_x, p, EDGE, KX // 2)
    flag = parity("gy")
    rim = RIM // 2
    for out, first in ((to_even_ref, 1 - flag), (to_odd_ref, flag)):
        for t in range(rim):
            out[:, t * tile : (t + 1) * tile] = x_inverted(grid_x, tix, first * rim + t).astype(BF16)


def respond(spectra, columns):
    patches = len(spectra)
    weighted = np.concatenate([w * x_forward(PSFW) for w in BLEND], 1)
    edge_table, inner_table = [constant(t) for t in y_inverse()]
    z_table = constant(z_inverse())
    x_table = constant(x_inverse(patches))
    tables = (
        constant(weighted),
        constant(z_forward(PSFW, PPER)),
        constant(y_forward(PSFW, PPER)),
        edge_table,
        z_table,
        x_table,
    )
    rows = patches * PATCH + PSFW
    rim = (rows, HALF * DEPTH)
    inner = OROWS - EDGE
    product, out_even, out_odd = pl.pallas_call(
        functools.partial(respond_kernel, patches),
        out_shape=(
            jax.ShapeDtypeStruct((patches, KX // 2, 2 * LONG, 2 * LANES), BF16),
            jax.ShapeDtypeStruct(rim, BF16),
            jax.ShapeDtypeStruct(rim, BF16),
        ),
        scratch_shapes=[
            pltpu.VMEM((patches, 2 * KX * PROWS, LANES), F32),
            pltpu.VMEM((patches, KX, 2 * PSFW, LANES), BF16),
            pltpu.VMEM((patches, KX * EDGE, 2 * YPER * LANES), BF16),
            pltpu.VMEM((patches, 2, EDGE * XSTEP, LANES), F32),
        ],
        compiler_params=pltpu.CompilerParams(vmem_limit_bytes=24 << 20),
        name="respond",
    )(*spectra, *columns, *tables)

    def middle():
        return pl.pallas_call(
            middle_kernel,
            out_shape=jax.ShapeDtypeStruct((rows, PATCH * DEPTH), F32),
            scratch_shapes=[
                pltpu.VMEM((patches, KX * inner, 2 * YPER * LANES), BF16),
                pltpu.VMEM((patches, 2, inner * XSTEP, LANES), F32),
            ],
            compiler_params=pltpu.CompilerParams(vmem_limit_bytes=24 << 20),
            cost_estimate=pl.CostEstimate(
                flops=3_000_000_000, bytes_accessed=6_000_000, transcendentals=0
            ),
            name="middle",
        )(product, inner_table, z_table, x_table)

    return middle, out_even, out_odd


def middle_kernel(product_ref, tiy, tiz, tix, out_ref, rows_ref, grid_x):
    tile = 2 * LANES
    patches = product_ref.shape[0]
    inner = OROWS - EDGE

    def along_y(t, _):
        for p in range(patches):
            y_inverted(tiy, product_ref[p, t], rows_ref, p, t)
        return 0

    lax.fori_loop(0, KX // 2, along_y, 0, unroll=True)
    for p in range(patches):
        z_swapped(rows_ref, tiz, grid_x, p, inner, 8)
    for t in range(inner // 2):
        out_ref[:, t * tile : (t + 1) * tile] = x_inverted(grid_x, tix, t)


def rim_kernel(mid_ref, even_ref, odd_ref, to_even_ref, to_odd_ref):
    band = even_ref.shape[1]
    rows = mid_ref.shape[0] - PSFW
    gx, gy = parity("gx"), parity("gy")
    for out, side in ((to_even_ref, 1 - gx), (to_odd_ref, gx)):
        at = pl.ds(pl.multiple_of(rows + side * HALF, HALF), HALF)
        low = pick(gy, odd_ref[at, :], even_ref[at, :]).astype(F32)
        high = pick(gy, even_ref[at, :], odd_ref[at, :]).astype(F32)
        out[:, band:-band] = mid_ref[at, band:-band].astype(BF16)
        out[:, :band] = (mid_ref[at, :band] + low).astype(BF16)
        out[:, -band:] = (mid_ref[at, -band:] + high).astype(BF16)


def x_rims(mid, even, odd):
    shape = jax.ShapeDtypeStruct((HALF, mid.shape[1]), BF16)
    return pl.pallas_call(
        rim_kernel,
        out_shape=(shape,) * 2,
        compiler_params=pltpu.CompilerParams(vmem_limit_bytes=16 << 20),
        name="x_rims",
    )(mid, even, odd)


def fold_kernel(mid_ref, even_ref, odd_ref, out_ref, rims_ref):
    rows, columns = out_ref.shape
    band = even_ref.shape[1]
    gy = parity("gy")
    out_ref[...] = mid_ref[:rows, :]
    for ref, side in ((even_ref, 1 - gy), (odd_ref, gy)):
        at = pl.ds(pl.multiple_of(side * (columns - band), band), band)
        out_ref[:, at] += ref[:rows, :].astype(F32)
    rims_ref[:HALF, :] = out_ref[:HALF, :]
    rims_ref[HALF:, :] = out_ref[rows - HALF :, :]


def fold(mid, even, odd):
    rows = mid.shape[0] - PSFW
    return pl.pallas_call(
        fold_kernel,
        out_shape=(
            jax.ShapeDtypeStruct((rows, mid.shape[1]), F32),
            jax.ShapeDtypeStruct((2 * HALF, mid.shape[1]), F32),
        ),
        compiler_params=pltpu.CompilerParams(vmem_limit_bytes=16 << 20),
        cost_estimate=pl.CostEstimate(
            flops=10_000_000, bytes_accessed=8_000_000, transcendentals=0
        ),
        name="fold",
    )(mid, even, odd)


def close_kernel(out_in, rims_ref, even_ref, odd_ref, out_ref, total, sems):
    del out_in
    gx = parity("gx")
    copies = []
    for k, (ref, side) in enumerate(((even_ref, 1 - gx), (odd_ref, gx))):
        at = pl.ds(pl.multiple_of(side * HALF, HALF), HALF)
        total[k] = rims_ref[at, :] + ref[...].astype(F32)
        first = pl.multiple_of(side * (out_ref.shape[0] - HALF), HALF)
        copies.append(
            pltpu.make_async_copy(total.at[k], out_ref.at[pl.ds(first, HALF), :], sems.at[k])
        )
        copies[-1].start()
    for copy in copies:
        copy.wait()


def close(out, rims, even, odd):
    vmem = pl.BlockSpec(memory_space=pltpu.VMEM)
    return pl.pallas_call(
        close_kernel,
        in_specs=[pl.BlockSpec(memory_space=pl.ANY), vmem, vmem, vmem],
        out_specs=pl.BlockSpec(memory_space=pl.ANY),
        out_shape=jax.ShapeDtypeStruct(out.shape, F32),
        scratch_shapes=[
            pltpu.VMEM((2, HALF, out.shape[1]), F32),
            pltpu.SemaphoreType.DMA((2,)),
        ],
        input_output_aliases={0: 0},
        compiler_params=pltpu.CompilerParams(vmem_limit_bytes=16 << 20),
        name="close",
    )(out, rims, even, odd)


def swap_even(value, axis):
    count = lax.axis_size(axis)
    return lax.ppermute(value, axis, [(i, i ^ 1) for i in range(count) if i ^ 1 < count])


def swap_odd(value, axis):
    ends = [i + 1 if i % 2 else i - 1 for i in range(lax.axis_size(axis))]
    pairs = [(i, j) for i, j in enumerate(ends) if 0 <= j < len(ends)]
    return lax.ppermute(value, axis, pairs)


def body(image, psfs):
    patches = image.shape[0] // PATCH
    last = psfs.shape[0] - 1
    gx = parity("gx")
    to_odd = lax.dynamic_slice_in_dim(psfs, gx * last, 1, 0)
    to_even = lax.dynamic_slice_in_dim(psfs, (1 - gx) * last, 1, 0)
    even = swap_even(to_even, "gx")
    odd = swap_odd(to_odd, "gx")
    spectra = [image_forward(image, 0)]
    spectra[0], odd, even = lax.optimization_barrier((spectra[0], odd, even))
    to_even, to_odd = blend_x(psfs, odd, even)
    image, to_even, to_odd = lax.optimization_barrier((image, to_even, to_odd))
    even = swap_even(to_even, "gy")
    odd = swap_odd(to_odd, "gy")
    spectra += [image_forward(image, p) for p in range(1, patches)]
    middle, out_even, out_odd = respond(spectra, (even, to_even, to_odd, odd))
    odd_y = swap_odd(out_odd, "gy")
    even_y = swap_even(out_even, "gy")
    mid = middle()
    out_even, out_odd = x_rims(mid, even_y, odd_y)
    even_x = swap_even(out_even, "gx")
    odd_x = swap_odd(out_odd, "gx")
    out, rims = fold(mid, even_y, odd_y)
    return close(out, rims, even_x, odd_x)


def solution(mesh):
    placed = (P("gx", "gy"), P("gx", "gy", None, None))
    return jax.shard_map(body, mesh=mesh, in_specs=placed, out_specs=P("gx", "gy"), check_vma=False)
```

```python
import functools
import math

import jax
import jax.numpy as jnp
import ml_dtypes
import numpy as np
from jax import lax
from jax.experimental import pallas as pl
from jax.experimental.pallas import tpu as pltpu
from jax.sharding import PartitionSpec as P

PATCH = 64
PSFW = 32
DEPTH = 64
BLEND = (0.125, 0.375, 0.375, 0.125)

HALF = PSFW // 2
LONG = PATCH + PSFW
KX = LONG // 2
KZ = DEPTH + HALF
LANES = 128
YPER = LANES // DEPTH
PPER = LANES // PSFW
YROWS = PATCH // YPER
PROWS = PSFW // PPER
OROWS = LONG // YPER
RIM = HALF // YPER
EDGE = 2 * RIM
YSTEP = YROWS + 2
XSTEP = KX + 2
F32 = jnp.float32
BF16 = jnp.bfloat16


def constant(values):
    return jnp.asarray(np.asarray(values, np.float32).astype(ml_dtypes.bfloat16))


def angle(k, n, length):
    return 2.0 * math.pi * np.outer(k, n) / length


def complex_block(theta, sign):
    cosine, sine = np.cos(theta), sign * np.sin(theta)
    return np.stack([np.stack([cosine, -sine], 1), np.stack([sine, cosine], 1)], 0)


def x_forward(count):
    theta = angle(np.arange(KX) + 0.5, np.arange(count), LONG)
    return np.concatenate([np.cos(theta), -np.sin(theta)], 0)


def z_forward(count, per):
    block = complex_block(angle(np.arange(KZ), np.arange(count), KZ), -1.0)
    table = np.zeros((2, per, count, per, 2, LANES))
    for y in range(per):
        table[:, y, :, y, :, :KZ] = block.transpose(2, 3, 0, 1)
    return table.reshape(2 * per * count, per * 2 * LANES)


def y_forward(count, per):
    block = complex_block(angle(np.arange(LONG), np.arange(count), LONG), -1.0)
    block = block.reshape(2, LONG, 2, count // per, per).transpose(0, 1, 4, 2, 3)
    return block.reshape(2 * LONG, 2 * count)


def y_inverse():
    block = complex_block(angle(np.arange(LONG), np.arange(LONG), LONG).T, 1.0) / LONG
    block = block.reshape(2, OROWS, YPER, 2 * LONG).transpose(2, 0, 1, 3)
    edge = np.concatenate([block[:, :, :RIM], block[:, :, -RIM:]], 2)
    inner = block[:, :, RIM:-RIM]
    return edge.reshape(-1, 2 * LONG), inner.reshape(-1, 2 * LONG)


def z_inverse():
    block = complex_block(angle(np.arange(DEPTH) + HALF, np.arange(KZ), KZ), 1.0) / KZ
    table = np.zeros((YPER, 2, LANES, 2, YPER, DEPTH))
    for y in range(YPER):
        table[y, :, :KZ, :, y, :] = block.transpose(2, 3, 0, 1)
    return table.reshape(YPER * 2 * LANES, 2 * YPER * DEPTH)


def x_inverse(patches):
    theta = angle(np.arange(LONG), np.arange(KX) + 0.5, LONG)
    block = np.stack([np.cos(theta), -np.sin(theta)], 1) * (2.0 / LONG)
    rows = patches * PATCH
    table = np.zeros((rows + PSFW, patches, 2, KX))
    for p in range(patches):
        table[p * PATCH : p * PATCH + LONG, p] = block
    table = np.concatenate([table[HALF : HALF + rows], table[:HALF], table[HALF + rows :]], 0)
    return table.reshape(rows + PSFW, patches * 2 * KX)


def dot(a, b):
    return jnp.dot(a, b, preferred_element_type=F32)


def full(shape):
    return pl.BlockSpec(shape, lambda *_: (0,) * len(shape))


def parity(axis):
    return lax.rem(lax.axis_index(axis), 2)


def pick(flag, even, odd):
    return jnp.where(flag == 0, even, odd)


def image_kernel(patch, image_ref, tx_ref, tz_ref, ty_ref, out_ref, swap, mid, ready=None):
    tile = 2 * LANES
    rows = 2 * KX

    def along_x(t, _):
        at = pl.ds(pl.multiple_of(t * tile, tile), tile)
        cells = image_ref[patch * PATCH : (patch + 1) * PATCH, at].astype(BF16)
        result = dot(tx_ref[...], cells)
        for h in range(2):
            swap[pl.ds(2 * t + h, rows, stride=YSTEP), :] = result[:, h * LANES : (h + 1) * LANES]
        return 0

    steps = PATCH * DEPTH // tile
    if ready is None:
        lax.fori_loop(0, steps, along_x, 0, unroll=8)
    else:
        for t in range(steps):
            ready(t, steps)
            along_x(t, 0)

    group = 8

    def along_z(t):
        left = [
            jnp.concatenate(
                [
                    swap[pl.ds((c * KX + t * group + k) * YSTEP, YROWS), :].astype(BF16)
                    for k in range(group)
                ],
                0,
            )
            for c in range(2)
        ]
        chunk = group * YROWS
        result = dot(jnp.concatenate(left, 1), tz_ref[...])
        mid[t * chunk : (t + 1) * chunk, :] = result.astype(BF16)

    for t in range(KX // group):
        along_z(t)

    def along_y(t, _):
        pieces = []
        for h in range(2):
            rows_at = pl.ds(pl.multiple_of((2 * t + h) * YROWS, YROWS), YROWS)
            pieces.append(
                jnp.concatenate(
                    [mid[rows_at, b * LANES : (b + 1) * LANES] for b in range(2 * YPER)], 0
                )
            )
        result = dot(ty_ref[...], jnp.concatenate(pieces, 1)).astype(BF16)
        for h in range(2):
            out_ref[2 * t + h] = result[:, h * LANES : (h + 1) * LANES]
        return 0

    lax.fori_loop(0, KX // 2, along_y, 0, unroll=True)


PARTS = 4


def fetching_kernel(patch, image_hbm, *refs):
    tables_hbm, out_ref, swap, mid, cells = refs[:3], *refs[3:7]
    tables, sems = refs[7:10], refs[10]
    width = cells.shape[1] // PARTS
    parts = [
        pltpu.make_async_copy(
            image_hbm.at[pl.ds(patch * PATCH, PATCH), pl.ds(k * width, width)],
            cells.at[:, pl.ds(k * width, width)],
            sems.at[k],
        )
        for k in range(PARTS)
    ]
    fetched = [
        pltpu.make_async_copy(a, b, sems.at[PARTS + k])
        for k, (a, b) in enumerate(zip(tables_hbm, tables))
    ]
    for copy in [fetched[0], parts[0], *fetched[1:], *parts[1:]]:
        copy.start()

    def ready(t, steps):
        if t == 0:
            fetched[0].wait()
        if t % (steps // PARTS) == 0:
            parts[t // (steps // PARTS)].wait()
        if t == steps - 1:
            fetched[1].wait()
            fetched[2].wait()

    image_kernel(0, cells, *tables, out_ref, swap, mid, ready)


def image_forward(image, patch):
    tables = (
        constant(x_forward(PATCH)),
        constant(z_forward(DEPTH, YPER)),
        constant(y_forward(PATCH, YPER)),
    )
    scratch = [
        pltpu.VMEM((2 * KX * YSTEP, LANES), F32),
        pltpu.VMEM((KX * YROWS, 2 * YPER * LANES), BF16),
    ]
    common = dict(
        out_shape=jax.ShapeDtypeStruct((KX, 2 * LONG, LANES), BF16),
        compiler_params=pltpu.CompilerParams(vmem_limit_bytes=16 << 20),
        cost_estimate=pl.CostEstimate(
            flops=4_000_000_000, bytes_accessed=4_000_000, transcendentals=0
        ),
    )
    if patch:
        return pl.pallas_call(
            functools.partial(image_kernel, patch),
            scratch_shapes=scratch,
            name="image_forward",
            **common,
        )(image, *tables)
    return pl.pallas_call(
        functools.partial(fetching_kernel, patch),
        in_specs=[pl.BlockSpec(memory_space=pltpu.HBM)] * 4,
        out_specs=pl.BlockSpec(memory_space=pltpu.VMEM),
        scratch_shapes=scratch
        + [pltpu.VMEM((PATCH, image.shape[1]), F32)]
        + [pltpu.VMEM(t.shape, BF16) for t in tables]
        + [pltpu.SemaphoreType.DMA((PARTS + len(tables),))],
        name="image_first",
        **common,
    )(*[pltpu.with_memory_space_constraint(x, pltpu.HBM) for x in (image, *tables)])


def blend_kernel(psfs_ref, odd_ref, even_ref, to_even_ref, to_odd_ref):
    count = psfs_ref.shape[0]
    gx, gy = parity("gx"), parity("gy")
    for out, column in ((to_even_ref, 1 - gy), (to_odd_ref, gy)):
        from_even = even_ref[0, column].astype(F32)
        from_odd = odd_ref[0, column].astype(F32)
        nodes = [pick(gx, from_odd, from_even)]
        nodes += [psfs_ref[i, column].astype(F32) for i in range(count)]
        nodes += [pick(gx, from_even, from_odd)]
        for p in range(count // 2):
            total = (nodes[2 * p] + nodes[2 * p + 3]) * BLEND[0]
            total += (nodes[2 * p + 1] + nodes[2 * p + 2]) * BLEND[1]
            out[p] = total.astype(BF16)


def blend_x(psfs, odd, even):
    shape = (psfs.shape[0] // 2,) + psfs.shape[2:]
    return pl.pallas_call(
        blend_kernel,
        out_shape=(jax.ShapeDtypeStruct(shape, BF16),) * 2,
        compiler_params=pltpu.CompilerParams(vmem_limit_bytes=16 << 20),
        name="blend_x",
    )(psfs, odd, even)


def y_inverted(tiy, product, rows_ref, p, t):
    back = dot(tiy[...], product).astype(BF16)
    pairs = back.shape[0] // (2 * YPER)
    for h in range(2):
        at = pl.ds(pl.multiple_of((2 * t + h) * pairs, pairs), pairs)
        for b in range(2 * YPER):
            rows_ref[p, at, b * LANES : (b + 1) * LANES] = back[
                b * pairs : (b + 1) * pairs, h * LANES : (h + 1) * LANES
            ]


def z_swapped(rows_ref, tiz, grid_ref, p, pairs, group):
    def along_z(t, _):
        start = pl.multiple_of(t * group * pairs, group * pairs)
        result = dot(rows_ref[p, pl.ds(start, group * pairs), :], tiz[...])
        for k in range(group):
            for c in range(2):
                grid_ref[p, c, pl.ds(t * group + k, pairs, stride=XSTEP), :] = result[
                    k * pairs : (k + 1) * pairs, c * LANES : (c + 1) * LANES
                ]
        return 0

    lax.fori_loop(0, KX // group, along_z, 0, unroll=True)


def x_inverted(grid_ref, tix, t):
    pieces = []
    for p in range(grid_ref.shape[0]):
        for c in range(2):
            parts = []
            for h in range(2):
                parts.append(grid_ref[p, c, pl.ds((2 * t + h) * XSTEP, KX), :])
            pieces.append(jnp.concatenate(parts, 1).astype(BF16))
    return dot(tix[...], jnp.concatenate(pieces, 0))


def respond_kernel(patches, *refs):
    spectra = refs[:patches]
    columns = refs[patches : patches + 4]
    tpx, tpz, tpy, tiy, tiz, tix = refs[patches + 4 : patches + 10]
    product_ref, to_even_ref, to_odd_ref = refs[patches + 10 : patches + 13]
    pswap, pmid, edge_rows, grid_x = refs[patches + 13 :]
    tile = 2 * LANES

    for p in range(patches):
        for t in range(PSFW * PSFW // tile):
            data = jnp.concatenate([c[p, :, t * tile : (t + 1) * tile] for c in columns], 0)
            result = dot(tpx[...], data)
            for h in range(2):
                pswap[p, pl.ds(2 * t + h, 2 * KX, stride=PROWS), :] = result[
                    :, h * LANES : (h + 1) * LANES
                ]
    half = KX * PROWS
    for p in range(patches):
        left = jnp.concatenate([pswap[p, :half, :], pswap[p, half:, :]], 1).astype(BF16)
        for b in range(PPER):
            result = dot(left, tpz[:, b * tile : (b + 1) * tile])
            result = result.reshape(KX, PROWS, tile)
            both = jnp.concatenate([result[:, :, :LANES], result[:, :, LANES:]], 1)
            pmid[p, :, 2 * b * PROWS : 2 * (b + 1) * PROWS, :] = both.astype(BF16)

    def along_y(t, _):
        for p in range(patches):
            psf = dot(tpy[...], jnp.concatenate([pmid[p, 2 * t], pmid[p, 2 * t + 1]], 1))
            psf = psf.astype(BF16)
            field = jnp.concatenate([spectra[p][2 * t], spectra[p][2 * t + 1]], 1)
            are, aim = field[:LONG], field[LONG:]
            bre, bim = psf[:LONG], psf[LONG:]
            product = jnp.concatenate([are * bre - aim * bim, are * bim + aim * bre], 0)
            product_ref[p, t] = product
        return 0

    lax.fori_loop(0, KX // 2, along_y, 0, unroll=True)

    def back_along_y(t, _):
        for p in range(patches):
            y_inverted(tiy, product_ref[p, t], edge_rows, p, t)
        return 0

    lax.fori_loop(0, KX // 2, back_along_y, 0, unroll=True)
    for p in range(patches):
        z_swapped(edge_rows, tiz, grid_x, p, EDGE, KX // 2)
    flag = parity("gy")
    rim = RIM // 2
    for out, first in ((to_even_ref, 1 - flag), (to_odd_ref, flag)):
        for t in range(rim):
            out[:, t * tile : (t + 1) * tile] = x_inverted(grid_x, tix, first * rim + t).astype(BF16)


def respond(spectra, columns):
    patches = len(spectra)
    weighted = np.concatenate([w * x_forward(PSFW) for w in BLEND], 1)
    edge_table, inner_table = [constant(t) for t in y_inverse()]
    z_table = constant(z_inverse())
    x_table = constant(x_inverse(patches))
    tables = (
        constant(weighted),
        constant(z_forward(PSFW, PPER)),
        constant(y_forward(PSFW, PPER)),
        edge_table,
        z_table,
        x_table,
    )
    rows = patches * PATCH + PSFW
    rim = (rows, HALF * DEPTH)
    inner = OROWS - EDGE
    product, out_even, out_odd = pl.pallas_call(
        functools.partial(respond_kernel, patches),
        out_shape=(
            jax.ShapeDtypeStruct((patches, KX // 2, 2 * LONG, 2 * LANES), BF16),
            jax.ShapeDtypeStruct(rim, BF16),
            jax.ShapeDtypeStruct(rim, BF16),
        ),
        scratch_shapes=[
            pltpu.VMEM((patches, 2 * KX * PROWS, LANES), F32),
            pltpu.VMEM((patches, KX, 2 * PSFW, LANES), BF16),
            pltpu.VMEM((patches, KX * EDGE, 2 * YPER * LANES), BF16),
            pltpu.VMEM((patches, 2, EDGE * XSTEP, LANES), F32),
        ],
        compiler_params=pltpu.CompilerParams(vmem_limit_bytes=24 << 20),
        name="respond",
    )(*spectra, *columns, *tables)

    def middle():
        return pl.pallas_call(
            middle_kernel,
            out_shape=jax.ShapeDtypeStruct((rows, PATCH * DEPTH), F32),
            scratch_shapes=[
                pltpu.VMEM((patches, KX * inner, 2 * YPER * LANES), BF16),
                pltpu.VMEM((patches, 2, inner * XSTEP, LANES), F32),
            ],
            compiler_params=pltpu.CompilerParams(vmem_limit_bytes=24 << 20),
            cost_estimate=pl.CostEstimate(
                flops=3_000_000_000, bytes_accessed=6_000_000, transcendentals=0
            ),
            name="middle",
        )(product, inner_table, z_table, x_table)

    return middle, out_even, out_odd


def middle_kernel(product_ref, tiy, tiz, tix, out_ref, rows_ref, grid_x):
    tile = 2 * LANES
    patches = product_ref.shape[0]
    inner = OROWS - EDGE

    def along_y(t, _):
        for p in range(patches):
            y_inverted(tiy, product_ref[p, t], rows_ref, p, t)
        return 0

    lax.fori_loop(0, KX // 2, along_y, 0, unroll=True)
    for p in range(patches):
        z_swapped(rows_ref, tiz, grid_x, p, inner, 8)
    for t in range(inner // 2):
        out_ref[:, t * tile : (t + 1) * tile] = x_inverted(grid_x, tix, t)


def rim_kernel(mid_ref, even_ref, odd_ref, to_even_ref, to_odd_ref):
    band = even_ref.shape[1]
    rows = mid_ref.shape[0] - PSFW
    gx, gy = parity("gx"), parity("gy")
    for out, side in ((to_even_ref, 1 - gx), (to_odd_ref, gx)):
        at = pl.ds(pl.multiple_of(rows + side * HALF, HALF), HALF)
        low = pick(gy, odd_ref[at, :], even_ref[at, :]).astype(F32)
        high = pick(gy, even_ref[at, :], odd_ref[at, :]).astype(F32)
        out[:, band:-band] = mid_ref[at, band:-band].astype(BF16)
        out[:, :band] = (mid_ref[at, :band] + low).astype(BF16)
        out[:, -band:] = (mid_ref[at, -band:] + high).astype(BF16)


def x_rims(mid, even, odd):
    shape = jax.ShapeDtypeStruct((HALF, mid.shape[1]), BF16)
    return pl.pallas_call(
        rim_kernel,
        out_shape=(shape,) * 2,
        compiler_params=pltpu.CompilerParams(vmem_limit_bytes=16 << 20),
        name="x_rims",
    )(mid, even, odd)


def fold_kernel(mid_ref, even_ref, odd_ref, out_ref, rims_ref):
    rows, columns = out_ref.shape
    band = even_ref.shape[1]
    gy = parity("gy")
    out_ref[...] = mid_ref[:rows, :]
    for ref, side in ((even_ref, 1 - gy), (odd_ref, gy)):
        at = pl.ds(pl.multiple_of(side * (columns - band), band), band)
        out_ref[:, at] += ref[:rows, :].astype(F32)
    rims_ref[:HALF, :] = out_ref[:HALF, :]
    rims_ref[HALF:, :] = out_ref[rows - HALF :, :]


def fold(mid, even, odd):
    rows = mid.shape[0] - PSFW
    return pl.pallas_call(
        fold_kernel,
        out_shape=(
            jax.ShapeDtypeStruct((rows, mid.shape[1]), F32),
            jax.ShapeDtypeStruct((2 * HALF, mid.shape[1]), F32),
        ),
        compiler_params=pltpu.CompilerParams(vmem_limit_bytes=16 << 20),
        cost_estimate=pl.CostEstimate(
            flops=10_000_000, bytes_accessed=8_000_000, transcendentals=0
        ),
        name="fold",
    )(mid, even, odd)


def close_kernel(out_in, rims_ref, even_ref, odd_ref, out_ref, total, sems):
    del out_in
    gx = parity("gx")
    copies = []
    for k, (ref, side) in enumerate(((even_ref, 1 - gx), (odd_ref, gx))):
        at = pl.ds(pl.multiple_of(side * HALF, HALF), HALF)
        total[k] = rims_ref[at, :] + ref[...].astype(F32)
        first = pl.multiple_of(side * (out_ref.shape[0] - HALF), HALF)
        copies.append(
            pltpu.make_async_copy(total.at[k], out_ref.at[pl.ds(first, HALF), :], sems.at[k])
        )
        copies[-1].start()
    for copy in copies:
        copy.wait()


def close(out, rims, even, odd):
    vmem = pl.BlockSpec(memory_space=pltpu.VMEM)
    return pl.pallas_call(
        close_kernel,
        in_specs=[pl.BlockSpec(memory_space=pl.ANY), vmem, vmem, vmem],
        out_specs=pl.BlockSpec(memory_space=pl.ANY),
        out_shape=jax.ShapeDtypeStruct(out.shape, F32),
        scratch_shapes=[
            pltpu.VMEM((2, HALF, out.shape[1]), F32),
            pltpu.SemaphoreType.DMA((2,)),
        ],
        input_output_aliases={0: 0},
        compiler_params=pltpu.CompilerParams(vmem_limit_bytes=16 << 20),
        name="close",
    )(out, rims, even, odd)


def swap_even(value, axis):
    count = lax.axis_size(axis)
    return lax.ppermute(value, axis, [(i, i ^ 1) for i in range(count) if i ^ 1 < count])


def swap_odd(value, axis):
    ends = [i + 1 if i % 2 else i - 1 for i in range(lax.axis_size(axis))]
    pairs = [(i, j) for i, j in enumerate(ends) if 0 <= j < len(ends)]
    return lax.ppermute(value, axis, pairs)


def body(image, psfs):
    patches = image.shape[0] // PATCH
    last = psfs.shape[0] - 1
    gx = parity("gx")
    to_odd = lax.dynamic_slice_in_dim(psfs, gx * last, 1, 0)
    to_even = lax.dynamic_slice_in_dim(psfs, (1 - gx) * last, 1, 0)
    even = swap_even(to_even, "gx")
    odd = swap_odd(to_odd, "gx")
    spectra = [image_forward(image, 0)]
    spectra[0], odd, even = lax.optimization_barrier((spectra[0], odd, even))
    to_even, to_odd = blend_x(psfs, odd, even)
    image, to_even, to_odd = lax.optimization_barrier((image, to_even, to_odd))
    even = swap_even(to_even, "gy")
    odd = swap_odd(to_odd, "gy")
    spectra += [image_forward(image, p) for p in range(1, patches)]
    middle, out_even, out_odd = respond(spectra, (even, to_even, to_odd, odd))
    odd_y = swap_odd(out_odd, "gy")
    even_y = swap_even(out_even, "gy")
    mid = middle()
    out_even, out_odd = x_rims(mid, even_y, odd_y)
    even_x = swap_even(out_even, "gx")
    odd_x = swap_odd(out_odd, "gx")
    out, rims = fold(mid, even_y, odd_y)
    return close(out, rims, even_x, odd_x)


def solution(mesh):
    placed = (P("gx", "gy"), P("gx", "gy", None, None))
    return jax.shard_map(body, mesh=mesh, in_specs=placed, out_specs=P("gx", "gy"), check_vma=False)
```

```python
import functools
import math

import jax
import jax.numpy as jnp
import ml_dtypes
import numpy as np
from jax import lax
from jax.experimental import pallas as pl
from jax.experimental.pallas import tpu as pltpu
from jax.sharding import PartitionSpec as P

PATCH = 64
PSFW = 32
DEPTH = 64
BLEND = (0.125, 0.375, 0.375, 0.125)

HALF = PSFW // 2
LONG = PATCH + PSFW
KX = LONG // 2
KZ = DEPTH + HALF
LANES = 128
YPER = LANES // DEPTH
PPER = LANES // PSFW
YROWS = PATCH // YPER
PROWS = PSFW // PPER
OROWS = LONG // YPER
RIM = HALF // YPER
EDGE = 2 * RIM
YSTEP = YROWS + 2
XSTEP = KX + 2
F32 = jnp.float32
BF16 = jnp.bfloat16


def constant(values):
    return jnp.asarray(np.asarray(values, np.float32).astype(ml_dtypes.bfloat16))


def angle(k, n, length):
    return 2.0 * math.pi * np.outer(k, n) / length


def complex_block(theta, sign):
    cosine, sine = np.cos(theta), sign * np.sin(theta)
    return np.stack([np.stack([cosine, -sine], 1), np.stack([sine, cosine], 1)], 0)


def x_forward(count):
    theta = angle(np.arange(KX) + 0.5, np.arange(count), LONG)
    return np.concatenate([np.cos(theta), -np.sin(theta)], 0)


def z_forward(count, per):
    block = complex_block(angle(np.arange(KZ), np.arange(count), KZ), -1.0)
    table = np.zeros((2, per, count, per, 2, LANES))
    for y in range(per):
        table[:, y, :, y, :, :KZ] = block.transpose(2, 3, 0, 1)
    return table.reshape(2 * per * count, per * 2 * LANES)


def y_forward(count, per):
    block = complex_block(angle(np.arange(LONG), np.arange(count), LONG), -1.0)
    block = block.reshape(2, LONG, 2, count // per, per).transpose(0, 1, 4, 2, 3)
    return block.reshape(2 * LONG, 2 * count)


def y_inverse():
    block = complex_block(angle(np.arange(LONG), np.arange(LONG), LONG).T, 1.0) / LONG
    block = block.reshape(2, OROWS, YPER, 2 * LONG).transpose(2, 0, 1, 3)
    edge = np.concatenate([block[:, :, :RIM], block[:, :, -RIM:]], 2)
    inner = block[:, :, RIM:-RIM]
    return edge.reshape(-1, 2 * LONG), inner.reshape(-1, 2 * LONG)


def z_inverse():
    block = complex_block(angle(np.arange(DEPTH) + HALF, np.arange(KZ), KZ), 1.0) / KZ
    table = np.zeros((YPER, 2, LANES, 2, YPER, DEPTH))
    for y in range(YPER):
        table[y, :, :KZ, :, y, :] = block.transpose(2, 3, 0, 1)
    return table.reshape(YPER * 2 * LANES, 2 * YPER * DEPTH)


def x_inverse(patches):
    theta = angle(np.arange(LONG), np.arange(KX) + 0.5, LONG)
    block = np.stack([np.cos(theta), -np.sin(theta)], 1) * (2.0 / LONG)
    rows = patches * PATCH
    table = np.zeros((rows + PSFW, patches, 2, KX))
    for p in range(patches):
        table[p * PATCH : p * PATCH + LONG, p] = block
    table = np.concatenate([table[HALF : HALF + rows], table[:HALF], table[HALF + rows :]], 0)
    return table.reshape(rows + PSFW, patches * 2 * KX)


def dot(a, b):
    return jnp.dot(a, b, preferred_element_type=F32)


def full(shape):
    return pl.BlockSpec(shape, lambda *_: (0,) * len(shape))


def parity(axis):
    return lax.rem(lax.axis_index(axis), 2)


def pick(flag, even, odd):
    return jnp.where(flag == 0, even, odd)


def image_kernel(patch, image_ref, tx_ref, tz_ref, ty_ref, out_ref, swap, mid, ready=None):
    tile = 2 * LANES
    rows = 2 * KX

    def along_x(t, _):
        at = pl.ds(pl.multiple_of(t * tile, tile), tile)
        cells = image_ref[patch * PATCH : (patch + 1) * PATCH, at].astype(BF16)
        result = dot(tx_ref[...], cells)
        for h in range(2):
            swap[pl.ds(2 * t + h, rows, stride=YSTEP), :] = result[:, h * LANES : (h + 1) * LANES]
        return 0

    steps = PATCH * DEPTH // tile
    if ready is None:
        lax.fori_loop(0, steps, along_x, 0, unroll=8)
    else:
        for t in range(steps):
            ready(t, steps)
            along_x(t, 0)

    group = 8

    def along_z(t):
        left = [
            jnp.concatenate(
                [
                    swap[pl.ds((c * KX + t * group + k) * YSTEP, YROWS), :].astype(BF16)
                    for k in range(group)
                ],
                0,
            )
            for c in range(2)
        ]
        chunk = group * YROWS
        result = dot(jnp.concatenate(left, 1), tz_ref[...])
        mid[t * chunk : (t + 1) * chunk, :] = result.astype(BF16)

    for t in range(KX // group):
        along_z(t)

    def along_y(t, _):
        pieces = []
        for h in range(2):
            rows_at = pl.ds(pl.multiple_of((2 * t + h) * YROWS, YROWS), YROWS)
            pieces.append(
                jnp.concatenate(
                    [mid[rows_at, b * LANES : (b + 1) * LANES] for b in range(2 * YPER)], 0
                )
            )
        result = dot(ty_ref[...], jnp.concatenate(pieces, 1)).astype(BF16)
        for h in range(2):
            out_ref[2 * t + h] = result[:, h * LANES : (h + 1) * LANES]
        return 0

    lax.fori_loop(0, KX // 2, along_y, 0, unroll=True)


PARTS = 4


def fetching_kernel(patch, image_hbm, *refs):
    tables_hbm, out_ref, swap, mid, cells = refs[:3], *refs[3:7]
    tables, sems = refs[7:10], refs[10]
    width = cells.shape[1] // PARTS
    parts = [
        pltpu.make_async_copy(
            image_hbm.at[pl.ds(patch * PATCH, PATCH), pl.ds(k * width, width)],
            cells.at[:, pl.ds(k * width, width)],
            sems.at[k],
        )
        for k in range(PARTS)
    ]
    fetched = [
        pltpu.make_async_copy(a, b, sems.at[PARTS + k])
        for k, (a, b) in enumerate(zip(tables_hbm, tables))
    ]
    for copy in [fetched[0], parts[0], *fetched[1:], *parts[1:]]:
        copy.start()

    def ready(t, steps):
        if t == 0:
            fetched[0].wait()
        if t % (steps // PARTS) == 0:
            parts[t // (steps // PARTS)].wait()
        if t == steps - 1:
            fetched[1].wait()
            fetched[2].wait()

    image_kernel(0, cells, *tables, out_ref, swap, mid, ready)


def image_forward(image, patch):
    tables = (
        constant(x_forward(PATCH)),
        constant(z_forward(DEPTH, YPER)),
        constant(y_forward(PATCH, YPER)),
    )
    scratch = [
        pltpu.VMEM((2 * KX * YSTEP, LANES), F32),
        pltpu.VMEM((KX * YROWS, 2 * YPER * LANES), BF16),
    ]
    common = dict(
        out_shape=jax.ShapeDtypeStruct((KX, 2 * LONG, LANES), BF16),
        compiler_params=pltpu.CompilerParams(vmem_limit_bytes=16 << 20),
        cost_estimate=pl.CostEstimate(
            flops=4_000_000_000, bytes_accessed=4_000_000, transcendentals=0
        ),
    )
    if patch:
        return pl.pallas_call(
            functools.partial(image_kernel, patch),
            scratch_shapes=scratch,
            name="image_forward",
            **common,
        )(image, *tables)
    return pl.pallas_call(
        functools.partial(fetching_kernel, patch),
        in_specs=[pl.BlockSpec(memory_space=pltpu.HBM)] * 4,
        out_specs=pl.BlockSpec(memory_space=pltpu.VMEM),
        scratch_shapes=scratch
        + [pltpu.VMEM((PATCH, image.shape[1]), F32)]
        + [pltpu.VMEM(t.shape, BF16) for t in tables]
        + [pltpu.SemaphoreType.DMA((PARTS + len(tables),))],
        name="image_first",
        **common,
    )(*[pltpu.with_memory_space_constraint(x, pltpu.HBM) for x in (image, *tables)])


def blend_kernel(psfs_ref, odd_ref, even_ref, to_even_ref, to_odd_ref):
    count = psfs_ref.shape[0]
    gx, gy = parity("gx"), parity("gy")
    for out, column in ((to_even_ref, 1 - gy), (to_odd_ref, gy)):
        from_even = even_ref[0, column].astype(F32)
        from_odd = odd_ref[0, column].astype(F32)
        nodes = [pick(gx, from_odd, from_even)]
        nodes += [psfs_ref[i, column].astype(F32) for i in range(count)]
        nodes += [pick(gx, from_even, from_odd)]
        for p in range(count // 2):
            total = (nodes[2 * p] + nodes[2 * p + 3]) * BLEND[0]
            total += (nodes[2 * p + 1] + nodes[2 * p + 2]) * BLEND[1]
            out[p] = total.astype(BF16)


def blend_x(psfs, odd, even):
    shape = (psfs.shape[0] // 2,) + psfs.shape[2:]
    return pl.pallas_call(
        blend_kernel,
        out_shape=(jax.ShapeDtypeStruct(shape, BF16),) * 2,
        compiler_params=pltpu.CompilerParams(vmem_limit_bytes=16 << 20),
        name="blend_x",
    )(psfs, odd, even)


def y_inverted(tiy, product, rows_ref, p, t):
    back = dot(tiy[...], product).astype(BF16)
    pairs = back.shape[0] // (2 * YPER)
    for h in range(2):
        at = pl.ds(pl.multiple_of((2 * t + h) * pairs, pairs), pairs)
        for b in range(2 * YPER):
            rows_ref[p, at, b * LANES : (b + 1) * LANES] = back[
                b * pairs : (b + 1) * pairs, h * LANES : (h + 1) * LANES
            ]


def z_swapped(rows_ref, tiz, grid_ref, p, pairs, group):
    def along_z(t, _):
        start = pl.multiple_of(t * group * pairs, group * pairs)
        result = dot(rows_ref[p, pl.ds(start, group * pairs), :], tiz[...])
        for k in range(group):
            for c in range(2):
                grid_ref[p, c, pl.ds(t * group + k, pairs, stride=XSTEP), :] = result[
                    k * pairs : (k + 1) * pairs, c * LANES : (c + 1) * LANES
                ]
        return 0

    lax.fori_loop(0, KX // group, along_z, 0, unroll=True)


def x_inverted(grid_ref, tix, t):
    pieces = []
    for p in range(grid_ref.shape[0]):
        for c in range(2):
            parts = []
            for h in range(2):
                parts.append(grid_ref[p, c, pl.ds((2 * t + h) * XSTEP, KX), :])
            pieces.append(jnp.concatenate(parts, 1).astype(BF16))
    return dot(tix[...], jnp.concatenate(pieces, 0))


def respond_kernel(patches, *refs):
    spectra = refs[:patches]
    columns = refs[patches : patches + 4]
    tpx, tpz, tpy, tiy, tiz, tix = refs[patches + 4 : patches + 10]
    product_ref, to_even_ref, to_odd_ref = refs[patches + 10 : patches + 13]
    pswap, pmid, edge_rows, grid_x = refs[patches + 13 :]
    tile = 2 * LANES

    for p in range(patches):
        for t in range(PSFW * PSFW // tile):
            data = jnp.concatenate([c[p, :, t * tile : (t + 1) * tile] for c in columns], 0)
            result = dot(tpx[...], data)
            for h in range(2):
                pswap[p, pl.ds(2 * t + h, 2 * KX, stride=PROWS), :] = result[
                    :, h * LANES : (h + 1) * LANES
                ]
    half = KX * PROWS
    for p in range(patches):
        left = jnp.concatenate([pswap[p, :half, :], pswap[p, half:, :]], 1).astype(BF16)
        for b in range(PPER):
            result = dot(left, tpz[:, b * tile : (b + 1) * tile])
            result = result.reshape(KX, PROWS, tile)
            both = jnp.concatenate([result[:, :, :LANES], result[:, :, LANES:]], 1)
            pmid[p, :, 2 * b * PROWS : 2 * (b + 1) * PROWS, :] = both.astype(BF16)

    def along_y(t, _):
        for p in range(patches):
            psf = dot(tpy[...], jnp.concatenate([pmid[p, 2 * t], pmid[p, 2 * t + 1]], 1))
            psf = psf.astype(BF16)
            field = jnp.concatenate([spectra[p][2 * t], spectra[p][2 * t + 1]], 1)
            are, aim = field[:LONG], field[LONG:]
            bre, bim = psf[:LONG], psf[LONG:]
            product = jnp.concatenate([are * bre - aim * bim, are * bim + aim * bre], 0)
            product_ref[p, t] = product
        return 0

    lax.fori_loop(0, KX // 2, along_y, 0, unroll=True)

    def back_along_y(t, _):
        for p in range(patches):
            y_inverted(tiy, product_ref[p, t], edge_rows, p, t)
        return 0

    lax.fori_loop(0, KX // 2, back_along_y, 0, unroll=True)
    for p in range(patches):
        z_swapped(edge_rows, tiz, grid_x, p, EDGE, KX // 2)
    flag = parity("gy")
    rim = RIM // 2
    for out, first in ((to_even_ref, 1 - flag), (to_odd_ref, flag)):
        for t in range(rim):
            out[:, t * tile : (t + 1) * tile] = x_inverted(grid_x, tix, first * rim + t).astype(BF16)


def respond(spectra, columns):
    patches = len(spectra)
    weighted = np.concatenate([w * x_forward(PSFW) for w in BLEND], 1)
    edge_table, inner_table = [constant(t) for t in y_inverse()]
    z_table = constant(z_inverse())
    x_table = constant(x_inverse(patches))
    tables = (
        constant(weighted),
        constant(z_forward(PSFW, PPER)),
        constant(y_forward(PSFW, PPER)),
        edge_table,
        z_table,
        x_table,
    )
    rows = patches * PATCH + PSFW
    rim = (rows, HALF * DEPTH)
    inner = OROWS - EDGE
    product, out_even, out_odd = pl.pallas_call(
        functools.partial(respond_kernel, patches),
        out_shape=(
            jax.ShapeDtypeStruct((patches, KX // 2, 2 * LONG, 2 * LANES), BF16),
            jax.ShapeDtypeStruct(rim, BF16),
            jax.ShapeDtypeStruct(rim, BF16),
        ),
        scratch_shapes=[
            pltpu.VMEM((patches, 2 * KX * PROWS, LANES), F32),
            pltpu.VMEM((patches, KX, 2 * PSFW, LANES), BF16),
            pltpu.VMEM((patches, KX * EDGE, 2 * YPER * LANES), BF16),
            pltpu.VMEM((patches, 2, EDGE * XSTEP, LANES), F32),
        ],
        compiler_params=pltpu.CompilerParams(vmem_limit_bytes=24 << 20),
        name="respond",
    )(*spectra, *columns, *tables)

    def middle():
        return pl.pallas_call(
            middle_kernel,
            out_shape=jax.ShapeDtypeStruct((rows, PATCH * DEPTH), F32),
            scratch_shapes=[
                pltpu.VMEM((patches, KX * inner, 2 * YPER * LANES), BF16),
                pltpu.VMEM((patches, 2, inner * XSTEP, LANES), F32),
            ],
            compiler_params=pltpu.CompilerParams(vmem_limit_bytes=24 << 20),
            cost_estimate=pl.CostEstimate(
                flops=3_000_000_000, bytes_accessed=6_000_000, transcendentals=0
            ),
            name="middle",
        )(product, inner_table, z_table, x_table)

    return middle, out_even, out_odd


def middle_kernel(product_ref, tiy, tiz, tix, out_ref, rows_ref, grid_x):
    tile = 2 * LANES
    patches = product_ref.shape[0]
    inner = OROWS - EDGE

    def along_y(t, _):
        for p in range(patches):
            y_inverted(tiy, product_ref[p, t], rows_ref, p, t)
        return 0

    lax.fori_loop(0, KX // 2, along_y, 0, unroll=True)
    for p in range(patches):
        z_swapped(rows_ref, tiz, grid_x, p, inner, 8)
    for t in range(inner // 2):
        out_ref[:, t * tile : (t + 1) * tile] = x_inverted(grid_x, tix, t)


def rim_kernel(mid_ref, even_ref, to_odd_ref, to_even_ref):
    band = even_ref.shape[1]
    rows, columns = mid_ref.shape[0] - PSFW, mid_ref.shape[1]
    gx, gy = parity("gx"), parity("gy")
    corner = pl.ds(pl.multiple_of((1 - gy) * (columns - band), band), band)
    for out, side in ((to_odd_ref, gx), (to_even_ref, 1 - gx)):
        at = pl.ds(pl.multiple_of(rows + side * HALF, HALF), HALF)
        out[...] = mid_ref[at, :].astype(BF16)
        out[:, corner] = (mid_ref[at, corner] + even_ref[at, :].astype(F32)).astype(BF16)


def x_rims(mid, even):
    shape = jax.ShapeDtypeStruct((HALF, mid.shape[1]), BF16)
    return pl.pallas_call(
        rim_kernel,
        out_shape=(shape,) * 2,
        compiler_params=pltpu.CompilerParams(vmem_limit_bytes=16 << 20),
        name="x_rims",
    )(mid, even)


def corner_kernel(odd_ref, to_odd_ref, to_even_ref):
    rows = odd_ref.shape[0] - PSFW
    gx = parity("gx")
    for out, side in ((to_odd_ref, gx), (to_even_ref, 1 - gx)):
        out[...] = odd_ref[pl.ds(pl.multiple_of(rows + side * HALF, HALF), HALF), :]


def x_corners(odd):
    shape = jax.ShapeDtypeStruct((HALF, odd.shape[1]), BF16)
    return pl.pallas_call(
        corner_kernel,
        out_shape=(shape,) * 2,
        compiler_params=pltpu.CompilerParams(vmem_limit_bytes=16 << 20),
        name="x_corners",
    )(odd)


def fold_kernel(mid_ref, even_ref, odd_ref, out_ref, rims_ref):
    rows, columns = out_ref.shape
    band = even_ref.shape[1]
    gy = parity("gy")
    out_ref[...] = mid_ref[:rows, :]
    for ref, side in ((even_ref, 1 - gy), (odd_ref, gy)):
        at = pl.ds(pl.multiple_of(side * (columns - band), band), band)
        out_ref[:, at] += ref[:rows, :].astype(F32)
    rims_ref[:HALF, :] = out_ref[:HALF, :]
    rims_ref[HALF:, :] = out_ref[rows - HALF :, :]


def fold(mid, even, odd):
    rows = mid.shape[0] - PSFW
    return pl.pallas_call(
        fold_kernel,
        out_shape=(
            jax.ShapeDtypeStruct((rows, mid.shape[1]), F32),
            jax.ShapeDtypeStruct((2 * HALF, mid.shape[1]), F32),
        ),
        compiler_params=pltpu.CompilerParams(vmem_limit_bytes=16 << 20),
        cost_estimate=pl.CostEstimate(
            flops=10_000_000, bytes_accessed=8_000_000, transcendentals=0
        ),
        name="fold",
    )(mid, even, odd)


def close_kernel(
    out_in, rims_ref, even_ref, odd_ref, even_corner, odd_corner, out_ref, total, sems
):
    del out_in
    gx, gy = parity("gx"), parity("gy")
    band = even_corner.shape[1]
    far = pl.ds(pl.multiple_of(gy * (out_ref.shape[1] - band), band), band)
    copies = []
    sides = ((even_ref, even_corner, 1 - gx), (odd_ref, odd_corner, gx))
    for k, (ref, corner, side) in enumerate(sides):
        at = pl.ds(pl.multiple_of(side * HALF, HALF), HALF)
        total[k] = rims_ref[at, :] + ref[...].astype(F32)
        total[k, :, far] += corner[...].astype(F32)
        first = pl.multiple_of(side * (out_ref.shape[0] - HALF), HALF)
        copies.append(
            pltpu.make_async_copy(total.at[k], out_ref.at[pl.ds(first, HALF), :], sems.at[k])
        )
        copies[-1].start()
    for copy in copies:
        copy.wait()


def close(out, rims, *received):
    vmem = pl.BlockSpec(memory_space=pltpu.VMEM)
    return pl.pallas_call(
        close_kernel,
        in_specs=[pl.BlockSpec(memory_space=pl.ANY)] + [vmem] * 5,
        out_specs=pl.BlockSpec(memory_space=pl.ANY),
        out_shape=jax.ShapeDtypeStruct(out.shape, F32),
        scratch_shapes=[
            pltpu.VMEM((2, HALF, out.shape[1]), F32),
            pltpu.SemaphoreType.DMA((2,)),
        ],
        input_output_aliases={0: 0},
        compiler_params=pltpu.CompilerParams(vmem_limit_bytes=16 << 20),
        name="close",
    )(out, rims, *received)


def swap_even(value, axis):
    count = lax.axis_size(axis)
    return lax.ppermute(value, axis, [(i, i ^ 1) for i in range(count) if i ^ 1 < count])


def swap_odd(value, axis):
    ends = [i + 1 if i % 2 else i - 1 for i in range(lax.axis_size(axis))]
    pairs = [(i, j) for i, j in enumerate(ends) if 0 <= j < len(ends)]
    return lax.ppermute(value, axis, pairs)


def body(image, psfs):
    patches = image.shape[0] // PATCH
    last = psfs.shape[0] - 1
    gx = parity("gx")
    to_odd = lax.dynamic_slice_in_dim(psfs, gx * last, 1, 0)
    to_even = lax.dynamic_slice_in_dim(psfs, (1 - gx) * last, 1, 0)
    even = swap_even(to_even, "gx")
    odd = swap_odd(to_odd, "gx")
    spectra = [image_forward(image, 0)]
    spectra[0], odd, even = lax.optimization_barrier((spectra[0], odd, even))
    to_even, to_odd = blend_x(psfs, odd, even)
    image, to_even, to_odd = lax.optimization_barrier((image, to_even, to_odd))
    even = swap_even(to_even, "gy")
    odd = swap_odd(to_odd, "gy")
    spectra += [image_forward(image, p) for p in range(1, patches)]
    middle, out_even, out_odd = respond(spectra, (even, to_even, to_odd, odd))
    odd_y = swap_odd(out_odd, "gy")
    even_y = swap_even(out_even, "gy")
    mid = middle()
    out_odd, out_even = x_rims(mid, even_y)
    even_x = swap_even(out_even, "gx")
    odd_x = swap_odd(out_odd, "gx")
    out_odd, out_even = x_corners(odd_y)
    even_corner = swap_even(out_even, "gx")
    odd_corner = swap_odd(out_odd, "gx")
    out, rims = fold(mid, even_y, odd_y)
    return close(out, rims, even_x, odd_x, even_corner, odd_corner)


def solution(mesh):
    placed = (P("gx", "gy"), P("gx", "gy", None, None))
    return jax.shard_map(body, mesh=mesh, in_specs=placed, out_specs=P("gx", "gy"), check_vma=False)
```

```python
import functools
import math

import jax
import jax.numpy as jnp
import ml_dtypes
import numpy as np
from jax import lax
from jax.experimental import pallas as pl
from jax.experimental.pallas import tpu as pltpu
from jax.sharding import PartitionSpec as P

PATCH = 64
PSFW = 32
DEPTH = 64
BLEND = (0.125, 0.375, 0.375, 0.125)

HALF = PSFW // 2
LONG = PATCH + PSFW
KX = LONG // 2
KZ = DEPTH + HALF
LANES = 128
YPER = LANES // DEPTH
PPER = LANES // PSFW
YROWS = PATCH // YPER
PROWS = PSFW // PPER
OROWS = LONG // YPER
RIM = HALF // YPER
EDGE = 2 * RIM
YSTEP = YROWS + 2
XSTEP = KX + 2
F32 = jnp.float32
BF16 = jnp.bfloat16


def constant(values):
    return jnp.asarray(np.asarray(values, np.float32).astype(ml_dtypes.bfloat16))


def angle(k, n, length):
    return 2.0 * math.pi * np.outer(k, n) / length


def complex_block(theta, sign):
    cosine, sine = np.cos(theta), sign * np.sin(theta)
    return np.stack([np.stack([cosine, -sine], 1), np.stack([sine, cosine], 1)], 0)


def x_forward(count):
    theta = angle(np.arange(KX) + 0.5, np.arange(count), LONG)
    return np.concatenate([np.cos(theta), -np.sin(theta)], 0)


def z_forward(count, per):
    block = complex_block(angle(np.arange(KZ), np.arange(count), KZ), -1.0)
    table = np.zeros((2, per, count, per, 2, LANES))
    for y in range(per):
        table[:, y, :, y, :, :KZ] = block.transpose(2, 3, 0, 1)
    return table.reshape(2 * per * count, per * 2 * LANES)


def y_forward(count, per):
    block = complex_block(angle(np.arange(LONG), np.arange(count), LONG), -1.0)
    block = block.reshape(2, LONG, 2, count // per, per).transpose(0, 1, 4, 2, 3)
    return block.reshape(2 * LONG, 2 * count)


def y_inverse():
    block = complex_block(angle(np.arange(LONG), np.arange(LONG), LONG).T, 1.0) / LONG
    block = block.reshape(2, OROWS, YPER, 2 * LONG).transpose(2, 0, 1, 3)
    edge = np.concatenate([block[:, :, :RIM], block[:, :, -RIM:]], 2)
    inner = block[:, :, RIM:-RIM]
    return edge.reshape(-1, 2 * LONG), inner.reshape(-1, 2 * LONG)


def z_inverse():
    block = complex_block(angle(np.arange(DEPTH) + HALF, np.arange(KZ), KZ), 1.0) / KZ
    table = np.zeros((YPER, 2, LANES, 2, YPER, DEPTH))
    for y in range(YPER):
        table[y, :, :KZ, :, y, :] = block.transpose(2, 3, 0, 1)
    return table.reshape(YPER * 2 * LANES, 2 * YPER * DEPTH)


def x_inverse(patches):
    theta = angle(np.arange(LONG), np.arange(KX) + 0.5, LONG)
    block = np.stack([np.cos(theta), -np.sin(theta)], 1) * (2.0 / LONG)
    rows = patches * PATCH
    table = np.zeros((rows + PSFW, patches, 2, KX))
    for p in range(patches):
        table[p * PATCH : p * PATCH + LONG, p] = block
    table = np.concatenate([table[HALF : HALF + rows], table[:HALF], table[HALF + rows :]], 0)
    return table.reshape(rows + PSFW, patches * 2 * KX)


def dot(a, b):
    return jnp.dot(a, b, preferred_element_type=F32)


def full(shape):
    return pl.BlockSpec(shape, lambda *_: (0,) * len(shape))


def parity(axis):
    return lax.rem(lax.axis_index(axis), 2)


def pick(flag, even, odd):
    return jnp.where(flag == 0, even, odd)


def image_kernel(patch, image_ref, tx_ref, tz_ref, ty_ref, out_ref, swap, mid, ready=None):
    tile = 2 * LANES
    rows = 2 * KX

    def along_x(t, _):
        at = pl.ds(pl.multiple_of(t * tile, tile), tile)
        cells = image_ref[patch * PATCH : (patch + 1) * PATCH, at].astype(BF16)
        result = dot(tx_ref[...], cells)
        for h in range(2):
            swap[pl.ds(2 * t + h, rows, stride=YSTEP), :] = result[:, h * LANES : (h + 1) * LANES]
        return 0

    steps = PATCH * DEPTH // tile
    if ready is None:
        lax.fori_loop(0, steps, along_x, 0, unroll=8)
    else:
        for t in range(steps):
            ready(t, steps)
            along_x(t, 0)

    group = 8

    def along_z(t):
        left = [
            jnp.concatenate(
                [
                    swap[pl.ds((c * KX + t * group + k) * YSTEP, YROWS), :].astype(BF16)
                    for k in range(group)
                ],
                0,
            )
            for c in range(2)
        ]
        chunk = group * YROWS
        result = dot(jnp.concatenate(left, 1), tz_ref[...])
        mid[t * chunk : (t + 1) * chunk, :] = result.astype(BF16)

    for t in range(KX // group):
        along_z(t)

    def along_y(t, _):
        pieces = []
        for h in range(2):
            rows_at = pl.ds(pl.multiple_of((2 * t + h) * YROWS, YROWS), YROWS)
            pieces.append(
                jnp.concatenate(
                    [mid[rows_at, b * LANES : (b + 1) * LANES] for b in range(2 * YPER)], 0
                )
            )
        result = dot(ty_ref[...], jnp.concatenate(pieces, 1)).astype(BF16)
        for h in range(2):
            out_ref[2 * t + h] = result[:, h * LANES : (h + 1) * LANES]
        return 0

    lax.fori_loop(0, KX // 2, along_y, 0, unroll=True)


PARTS = 4


def fetching_kernel(patch, image_hbm, *refs):
    tables_hbm, out_ref, swap, mid, cells = refs[:3], *refs[3:7]
    tables, sems = refs[7:10], refs[10]
    width = cells.shape[1] // PARTS
    parts = [
        pltpu.make_async_copy(
            image_hbm.at[pl.ds(patch * PATCH, PATCH), pl.ds(k * width, width)],
            cells.at[:, pl.ds(k * width, width)],
            sems.at[k],
        )
        for k in range(PARTS)
    ]
    fetched = [
        pltpu.make_async_copy(a, b, sems.at[PARTS + k])
        for k, (a, b) in enumerate(zip(tables_hbm, tables))
    ]
    for copy in [fetched[0], parts[0], *fetched[1:], *parts[1:]]:
        copy.start()

    def ready(t, steps):
        if t == 0:
            fetched[0].wait()
        if t % (steps // PARTS) == 0:
            parts[t // (steps // PARTS)].wait()
        if t == steps - 1:
            fetched[1].wait()
            fetched[2].wait()

    image_kernel(0, cells, *tables, out_ref, swap, mid, ready)


def image_forward(image, patch):
    tables = (
        constant(x_forward(PATCH)),
        constant(z_forward(DEPTH, YPER)),
        constant(y_forward(PATCH, YPER)),
    )
    scratch = [
        pltpu.VMEM((2 * KX * YSTEP, LANES), F32),
        pltpu.VMEM((KX * YROWS, 2 * YPER * LANES), BF16),
    ]
    common = dict(
        out_shape=jax.ShapeDtypeStruct((KX, 2 * LONG, LANES), BF16),
        compiler_params=pltpu.CompilerParams(vmem_limit_bytes=16 << 20),
        cost_estimate=pl.CostEstimate(
            flops=4_000_000_000, bytes_accessed=4_000_000, transcendentals=0
        ),
    )
    if patch:
        return pl.pallas_call(
            functools.partial(image_kernel, patch),
            scratch_shapes=scratch,
            name="image_forward",
            **common,
        )(image, *tables)
    return pl.pallas_call(
        functools.partial(fetching_kernel, patch),
        in_specs=[pl.BlockSpec(memory_space=pltpu.HBM)] * 4,
        out_specs=pl.BlockSpec(memory_space=pltpu.VMEM),
        scratch_shapes=scratch
        + [pltpu.VMEM((PATCH, image.shape[1]), F32)]
        + [pltpu.VMEM(t.shape, BF16) for t in tables]
        + [pltpu.SemaphoreType.DMA((PARTS + len(tables),))],
        name="image_first",
        **common,
    )(*[pltpu.with_memory_space_constraint(x, pltpu.HBM) for x in (image, *tables)])


def blend_kernel(psfs_ref, odd_ref, even_ref, to_even_ref, to_odd_ref):
    count = psfs_ref.shape[0]
    gx, gy = parity("gx"), parity("gy")
    for out, column in ((to_even_ref, 1 - gy), (to_odd_ref, gy)):
        from_even = even_ref[0, column].astype(F32)
        from_odd = odd_ref[0, column].astype(F32)
        nodes = [pick(gx, from_odd, from_even)]
        nodes += [psfs_ref[i, column].astype(F32) for i in range(count)]
        nodes += [pick(gx, from_even, from_odd)]
        for p in range(count // 2):
            total = (nodes[2 * p] + nodes[2 * p + 3]) * BLEND[0]
            total += (nodes[2 * p + 1] + nodes[2 * p + 2]) * BLEND[1]
            out[p] = total.astype(BF16)


def blend_x(psfs, odd, even):
    shape = (psfs.shape[0] // 2,) + psfs.shape[2:]
    return pl.pallas_call(
        blend_kernel,
        out_shape=(jax.ShapeDtypeStruct(shape, BF16),) * 2,
        compiler_params=pltpu.CompilerParams(vmem_limit_bytes=16 << 20),
        name="blend_x",
    )(psfs, odd, even)


def y_inverted(tiy, product, rows_ref, p, t):
    back = dot(tiy[...], product).astype(BF16)
    pairs = back.shape[0] // (2 * YPER)
    for h in range(2):
        at = pl.ds(pl.multiple_of((2 * t + h) * pairs, pairs), pairs)
        for b in range(2 * YPER):
            rows_ref[p, at, b * LANES : (b + 1) * LANES] = back[
                b * pairs : (b + 1) * pairs, h * LANES : (h + 1) * LANES
            ]


def z_swapped(rows_ref, tiz, grid_ref, p, pairs, group):
    def along_z(t, _):
        start = pl.multiple_of(t * group * pairs, group * pairs)
        result = dot(rows_ref[p, pl.ds(start, group * pairs), :], tiz[...])
        for k in range(group):
            for c in range(2):
                grid_ref[p, c, pl.ds(t * group + k, pairs, stride=XSTEP), :] = result[
                    k * pairs : (k + 1) * pairs, c * LANES : (c + 1) * LANES
                ]
        return 0

    lax.fori_loop(0, KX // group, along_z, 0, unroll=True)


def x_inverted(grid_ref, tix, t):
    pieces = []
    for p in range(grid_ref.shape[0]):
        for c in range(2):
            parts = []
            for h in range(2):
                parts.append(grid_ref[p, c, pl.ds((2 * t + h) * XSTEP, KX), :])
            pieces.append(jnp.concatenate(parts, 1).astype(BF16))
    return dot(tix[...], jnp.concatenate(pieces, 0))


def respond_kernel(patches, *refs):
    spectra = refs[:patches]
    columns = refs[patches : patches + 4]
    tpx, tpz, tpy, tiy, tiz, tix = refs[patches + 4 : patches + 10]
    product_ref, to_even_ref, to_odd_ref = refs[patches + 10 : patches + 13]
    pswap, pmid, edge_rows, grid_x = refs[patches + 13 :]
    tile = 2 * LANES

    for p in range(patches):
        for t in range(PSFW * PSFW // tile):
            data = jnp.concatenate([c[p, :, t * tile : (t + 1) * tile] for c in columns], 0)
            result = dot(tpx[...], data)
            for h in range(2):
                pswap[p, pl.ds(2 * t + h, 2 * KX, stride=PROWS), :] = result[
                    :, h * LANES : (h + 1) * LANES
                ]
    half = KX * PROWS
    for p in range(patches):
        left = jnp.concatenate([pswap[p, :half, :], pswap[p, half:, :]], 1).astype(BF16)
        for b in range(PPER):
            result = dot(left, tpz[:, b * tile : (b + 1) * tile])
            result = result.reshape(KX, PROWS, tile)
            both = jnp.concatenate([result[:, :, :LANES], result[:, :, LANES:]], 1)
            pmid[p, :, 2 * b * PROWS : 2 * (b + 1) * PROWS, :] = both.astype(BF16)

    def along_y(t, _):
        for p in range(patches):
            psf = dot(tpy[...], jnp.concatenate([pmid[p, 2 * t], pmid[p, 2 * t + 1]], 1))
            psf = psf.astype(BF16)
            field = jnp.concatenate([spectra[p][2 * t], spectra[p][2 * t + 1]], 1)
            are, aim = field[:LONG], field[LONG:]
            bre, bim = psf[:LONG], psf[LONG:]
            product = jnp.concatenate([are * bre - aim * bim, are * bim + aim * bre], 0)
            product_ref[p, t] = product
        return 0

    lax.fori_loop(0, KX // 2, along_y, 0, unroll=True)

    def back_along_y(t, _):
        for p in range(patches):
            y_inverted(tiy, product_ref[p, t], edge_rows, p, t)
        return 0

    lax.fori_loop(0, KX // 2, back_along_y, 0, unroll=True)
    for p in range(patches):
        z_swapped(edge_rows, tiz, grid_x, p, EDGE, KX // 2)
    flag = parity("gy")
    rim = RIM // 2
    for out, first in ((to_even_ref, 1 - flag), (to_odd_ref, flag)):
        for t in range(rim):
            out[:, t * tile : (t + 1) * tile] = x_inverted(grid_x, tix, first * rim + t).astype(BF16)


def respond(spectra, columns):
    patches = len(spectra)
    weighted = np.concatenate([w * x_forward(PSFW) for w in BLEND], 1)
    edge_table, inner_table = [constant(t) for t in y_inverse()]
    z_table = constant(z_inverse())
    x_table = constant(x_inverse(patches))
    tables = (
        constant(weighted),
        constant(z_forward(PSFW, PPER)),
        constant(y_forward(PSFW, PPER)),
        edge_table,
        z_table,
        x_table,
    )
    rows = patches * PATCH + PSFW
    rim = (rows, HALF * DEPTH)
    inner = OROWS - EDGE
    product, out_even, out_odd = pl.pallas_call(
        functools.partial(respond_kernel, patches),
        out_shape=(
            jax.ShapeDtypeStruct((patches, KX // 2, 2 * LONG, 2 * LANES), BF16),
            jax.ShapeDtypeStruct(rim, BF16),
            jax.ShapeDtypeStruct(rim, BF16),
        ),
        scratch_shapes=[
            pltpu.VMEM((patches, 2 * KX * PROWS, LANES), F32),
            pltpu.VMEM((patches, KX, 2 * PSFW, LANES), BF16),
            pltpu.VMEM((patches, KX * EDGE, 2 * YPER * LANES), BF16),
            pltpu.VMEM((patches, 2, EDGE * XSTEP, LANES), F32),
        ],
        compiler_params=pltpu.CompilerParams(vmem_limit_bytes=24 << 20),
        name="respond",
    )(*spectra, *columns, *tables)

    def middle():
        return pl.pallas_call(
            middle_kernel,
            out_shape=jax.ShapeDtypeStruct((rows, PATCH * DEPTH), F32),
            scratch_shapes=[
                pltpu.VMEM((patches, KX * inner, 2 * YPER * LANES), BF16),
                pltpu.VMEM((patches, 2, inner * XSTEP, LANES), F32),
            ],
            compiler_params=pltpu.CompilerParams(vmem_limit_bytes=24 << 20),
            cost_estimate=pl.CostEstimate(
                flops=3_000_000_000, bytes_accessed=6_000_000, transcendentals=0
            ),
            name="middle",
        )(product, inner_table, z_table, x_table)

    return middle, out_even, out_odd


def middle_kernel(product_ref, tiy, tiz, tix, out_ref, rows_ref, grid_x):
    tile = 2 * LANES
    patches = product_ref.shape[0]
    inner = OROWS - EDGE

    def along_y(t, _):
        for p in range(patches):
            y_inverted(tiy, product_ref[p, t], rows_ref, p, t)
        return 0

    lax.fori_loop(0, KX // 2, along_y, 0, unroll=True)
    for p in range(patches):
        z_swapped(rows_ref, tiz, grid_x, p, inner, 8)
    for t in range(inner // 2):
        out_ref[:, t * tile : (t + 1) * tile] = x_inverted(grid_x, tix, t)


def rim_kernel(mid_ref, even_ref, to_odd_ref, to_even_ref):
    band = even_ref.shape[1]
    rows, columns = mid_ref.shape[0] - PSFW, mid_ref.shape[1]
    gx, gy = parity("gx"), parity("gy")
    corner = pl.ds(pl.multiple_of((1 - gy) * (columns - band), band), band)
    for out, side in ((to_odd_ref, gx), (to_even_ref, 1 - gx)):
        at = pl.ds(pl.multiple_of(rows + side * HALF, HALF), HALF)
        out[...] = mid_ref[at, :].astype(BF16)
        out[:, corner] = (mid_ref[at, corner] + even_ref[at, :].astype(F32)).astype(BF16)


def x_rims(mid, even):
    shape = jax.ShapeDtypeStruct((HALF, mid.shape[1]), BF16)
    return pl.pallas_call(
        rim_kernel,
        out_shape=(shape,) * 2,
        compiler_params=pltpu.CompilerParams(vmem_limit_bytes=16 << 20),
        name="x_rims",
    )(mid, even)


def corner_kernel(odd_ref, to_odd_ref, to_even_ref):
    rows = odd_ref.shape[0] - PSFW
    gx = parity("gx")
    for out, side in ((to_odd_ref, gx), (to_even_ref, 1 - gx)):
        out[...] = odd_ref[pl.ds(pl.multiple_of(rows + side * HALF, HALF), HALF), :]


def x_corners(odd):
    shape = jax.ShapeDtypeStruct((HALF, odd.shape[1]), BF16)
    return pl.pallas_call(
        corner_kernel,
        out_shape=(shape,) * 2,
        compiler_params=pltpu.CompilerParams(vmem_limit_bytes=16 << 20),
        name="x_corners",
    )(odd)


def fold_kernel(mid_ref, even_ref, odd_ref, out_ref, rims_ref):
    rows, columns = out_ref.shape
    band = even_ref.shape[1]
    gy = parity("gy")
    out_ref[...] = mid_ref[:rows, :]
    for ref, side in ((even_ref, 1 - gy), (odd_ref, gy)):
        at = pl.ds(pl.multiple_of(side * (columns - band), band), band)
        out_ref[:, at] += ref[:rows, :].astype(F32)
    rims_ref[:HALF, :] = out_ref[:HALF, :]
    rims_ref[HALF:, :] = out_ref[rows - HALF :, :]


def fold(mid, even, odd):
    rows = mid.shape[0] - PSFW
    return pl.pallas_call(
        fold_kernel,
        out_shape=(
            jax.ShapeDtypeStruct((rows, mid.shape[1]), F32),
            jax.ShapeDtypeStruct((2 * HALF, mid.shape[1]), F32),
        ),
        compiler_params=pltpu.CompilerParams(vmem_limit_bytes=16 << 20),
        cost_estimate=pl.CostEstimate(
            flops=10_000_000, bytes_accessed=8_000_000, transcendentals=0
        ),
        name="fold",
    )(mid, even, odd)


def edges_kernel(out_in, rims_ref, even_ref, odd_ref, out_ref, corners_ref, total, sems):
    del out_in
    gx, gy = parity("gx"), parity("gy")
    rows, columns = out_ref.shape
    band = corners_ref.shape[2]
    far = pl.ds(pl.multiple_of(gy * (columns - band), band), band)
    copies = []
    for k, (ref, side) in enumerate(((even_ref, 1 - gx), (odd_ref, gx))):
        at = pl.ds(pl.multiple_of(side * HALF, HALF), HALF)
        total[k] = rims_ref[at, :] + ref[...].astype(F32)
        first = pl.multiple_of(side * (rows - HALF), HALF)
        copies.append(
            pltpu.make_async_copy(total.at[k], out_ref.at[pl.ds(first, HALF), :], sems.at[k])
        )
        copies[-1].start()
        corners_ref[k] = total[k, :, far]
    for copy in copies:
        copy.wait()


def close_kernel(out_in, corners_ref, even_ref, odd_ref, out_ref, total, sems):
    del out_in
    gx, gy = parity("gx"), parity("gy")
    rows, columns = out_ref.shape
    band = even_ref.shape[1]
    far = pl.ds(pl.multiple_of(gy * (columns - band), band), band)
    copies = []
    for k, (ref, side) in enumerate(((even_ref, 1 - gx), (odd_ref, gx))):
        total[k] = corners_ref[k] + ref[...].astype(F32)
        at = pl.ds(pl.multiple_of(side * (rows - HALF), HALF), HALF)
        copies.append(pltpu.make_async_copy(total.at[k], out_ref.at[at, far], sems.at[k]))
        copies[-1].start()
    for copy in copies:
        copy.wait()


def close(kernel, name, width, out, kept, even, odd):
    vmem, anywhere = pl.BlockSpec(memory_space=pltpu.VMEM), pl.BlockSpec(memory_space=pl.ANY)
    corners = jax.ShapeDtypeStruct((2, HALF, HALF * DEPTH), F32)
    first = kernel is edges_kernel
    shape = jax.ShapeDtypeStruct(out.shape, F32)
    return pl.pallas_call(
        kernel,
        in_specs=[anywhere, vmem, vmem, vmem],
        out_specs=(anywhere, vmem) if first else anywhere,
        out_shape=(shape, corners) if first else shape,
        scratch_shapes=[
            pltpu.VMEM((2, HALF, width), F32),
            pltpu.SemaphoreType.DMA((2,)),
        ],
        input_output_aliases={0: 0},
        compiler_params=pltpu.CompilerParams(vmem_limit_bytes=16 << 20),
        name=name,
    )(out, kept, even, odd)


def swap_even(value, axis):
    count = lax.axis_size(axis)
    return lax.ppermute(value, axis, [(i, i ^ 1) for i in range(count) if i ^ 1 < count])


def swap_odd(value, axis):
    ends = [i + 1 if i % 2 else i - 1 for i in range(lax.axis_size(axis))]
    pairs = [(i, j) for i, j in enumerate(ends) if 0 <= j < len(ends)]
    return lax.ppermute(value, axis, pairs)


def body(image, psfs):
    patches = image.shape[0] // PATCH
    last = psfs.shape[0] - 1
    gx = parity("gx")
    to_odd = lax.dynamic_slice_in_dim(psfs, gx * last, 1, 0)
    to_even = lax.dynamic_slice_in_dim(psfs, (1 - gx) * last, 1, 0)
    even = swap_even(to_even, "gx")
    odd = swap_odd(to_odd, "gx")
    spectra = [image_forward(image, 0)]
    spectra[0], odd, even = lax.optimization_barrier((spectra[0], odd, even))
    to_even, to_odd = blend_x(psfs, odd, even)
    image, to_even, to_odd = lax.optimization_barrier((image, to_even, to_odd))
    even = swap_even(to_even, "gy")
    odd = swap_odd(to_odd, "gy")
    spectra += [image_forward(image, p) for p in range(1, patches)]
    middle, out_even, out_odd = respond(spectra, (even, to_even, to_odd, odd))
    odd_y = swap_odd(out_odd, "gy")
    even_y = swap_even(out_even, "gy")
    mid = middle()
    out_odd, out_even = x_rims(mid, even_y)
    even_x = swap_even(out_even, "gx")
    odd_x = swap_odd(out_odd, "gx")
    out_odd, out_even = x_corners(odd_y)
    even_corner = swap_even(out_even, "gx")
    odd_corner = swap_odd(out_odd, "gx")
    out, rims = fold(mid, even_y, odd_y)
    out, corners = close(edges_kernel, "edges", out.shape[1], out, rims, even_x, odd_x)
    return close(close_kernel, "corners", HALF * DEPTH, out, corners, even_corner, odd_corner)


def solution(mesh):
    placed = (P("gx", "gy"), P("gx", "gy", None, None))
    return jax.shard_map(body, mesh=mesh, in_specs=placed, out_specs=P("gx", "gy"), check_vma=False)
```

```python
import functools
import math

import jax
import jax.numpy as jnp
import ml_dtypes
import numpy as np
from jax import lax
from jax.experimental import pallas as pl
from jax.experimental.pallas import tpu as pltpu
from jax.sharding import PartitionSpec as P

PATCH = 64
PSFW = 32
DEPTH = 64
BLEND = (0.125, 0.375, 0.375, 0.125)

HALF = PSFW // 2
LONG = PATCH + PSFW
KX = LONG // 2
KZ = DEPTH + HALF
LANES = 128
YPER = LANES // DEPTH
PPER = LANES // PSFW
YROWS = PATCH // YPER
PROWS = PSFW // PPER
OROWS = LONG // YPER
RIM = HALF // YPER
EDGE = 2 * RIM
YSTEP = YROWS + 2
XSTEP = KX + 2
F32 = jnp.float32
BF16 = jnp.bfloat16


def constant(values):
    return jnp.asarray(np.asarray(values, np.float32).astype(ml_dtypes.bfloat16))


def angle(k, n, length):
    return 2.0 * math.pi * np.outer(k, n) / length


def complex_block(theta, sign):
    cosine, sine = np.cos(theta), sign * np.sin(theta)
    return np.stack([np.stack([cosine, -sine], 1), np.stack([sine, cosine], 1)], 0)


def x_forward(count):
    theta = angle(np.arange(KX) + 0.5, np.arange(count), LONG)
    return np.concatenate([np.cos(theta), -np.sin(theta)], 0)


def z_forward(count, per):
    block = complex_block(angle(np.arange(KZ), np.arange(count), KZ), -1.0)
    table = np.zeros((2, per, count, per, 2, LANES))
    for y in range(per):
        table[:, y, :, y, :, :KZ] = block.transpose(2, 3, 0, 1)
    return table.reshape(2 * per * count, per * 2 * LANES)


def y_forward(count, per):
    block = complex_block(angle(np.arange(LONG), np.arange(count), LONG), -1.0)
    block = block.reshape(2, LONG, 2, count // per, per).transpose(0, 1, 4, 2, 3)
    return block.reshape(2 * LONG, 2 * count)


def y_inverse():
    block = complex_block(angle(np.arange(LONG), np.arange(LONG), LONG).T, 1.0) / LONG
    block = block.reshape(2, OROWS, YPER, 2 * LONG).transpose(2, 0, 1, 3)
    edge = np.concatenate([block[:, :, :RIM], block[:, :, -RIM:]], 2)
    inner = block[:, :, RIM:-RIM]
    return edge.reshape(-1, 2 * LONG), inner.reshape(-1, 2 * LONG)


def z_inverse():
    block = complex_block(angle(np.arange(DEPTH) + HALF, np.arange(KZ), KZ), 1.0) / KZ
    table = np.zeros((YPER, 2, LANES, 2, YPER, DEPTH))
    for y in range(YPER):
        table[y, :, :KZ, :, y, :] = block.transpose(2, 3, 0, 1)
    return table.reshape(YPER * 2 * LANES, 2 * YPER * DEPTH)


def x_inverse(patches):
    theta = angle(np.arange(LONG), np.arange(KX) + 0.5, LONG)
    block = np.stack([np.cos(theta), -np.sin(theta)], 1) * (2.0 / LONG)
    rows = patches * PATCH
    table = np.zeros((rows + PSFW, patches, 2, KX))
    for p in range(patches):
        table[p * PATCH : p * PATCH + LONG, p] = block
    table = np.concatenate([table[HALF : HALF + rows], table[:HALF], table[HALF + rows :]], 0)
    return table.reshape(rows + PSFW, patches * 2 * KX)


def dot(a, b):
    return jnp.dot(a, b, preferred_element_type=F32)


def full(shape):
    return pl.BlockSpec(shape, lambda *_: (0,) * len(shape))


def parity(axis):
    return lax.rem(lax.axis_index(axis), 2)


def pick(flag, even, odd):
    return jnp.where(flag == 0, even, odd)


def image_kernel(patch, image_ref, tx_ref, tz_ref, ty_ref, out_ref, swap, mid, ready=None):
    tile = 2 * LANES
    rows = 2 * KX

    def along_x(t, _):
        at = pl.ds(pl.multiple_of(t * tile, tile), tile)
        cells = image_ref[patch * PATCH : (patch + 1) * PATCH, at].astype(BF16)
        result = dot(tx_ref[...], cells)
        for h in range(2):
            swap[pl.ds(2 * t + h, rows, stride=YSTEP), :] = result[:, h * LANES : (h + 1) * LANES]
        return 0

    steps = PATCH * DEPTH // tile
    if ready is None:
        lax.fori_loop(0, steps, along_x, 0, unroll=8)
    else:
        for t in range(steps):
            ready(t, steps)
            along_x(t, 0)

    group = 8

    def along_z(t):
        left = [
            jnp.concatenate(
                [
                    swap[pl.ds((c * KX + t * group + k) * YSTEP, YROWS), :].astype(BF16)
                    for k in range(group)
                ],
                0,
            )
            for c in range(2)
        ]
        chunk = group * YROWS
        result = dot(jnp.concatenate(left, 1), tz_ref[...])
        mid[t * chunk : (t + 1) * chunk, :] = result.astype(BF16)

    for t in range(KX // group):
        along_z(t)

    def along_y(t, _):
        pieces = []
        for h in range(2):
            rows_at = pl.ds(pl.multiple_of((2 * t + h) * YROWS, YROWS), YROWS)
            pieces.append(
                jnp.concatenate(
                    [mid[rows_at, b * LANES : (b + 1) * LANES] for b in range(2 * YPER)], 0
                )
            )
        result = dot(ty_ref[...], jnp.concatenate(pieces, 1)).astype(BF16)
        for h in range(2):
            out_ref[2 * t + h] = result[:, h * LANES : (h + 1) * LANES]
        return 0

    lax.fori_loop(0, KX // 2, along_y, 0, unroll=True)


PARTS = 4


def fetching_kernel(patch, image_hbm, *refs):
    tables_hbm, out_ref, swap, mid, cells = refs[:3], *refs[3:7]
    tables, sems = refs[7:10], refs[10]
    width = cells.shape[1] // PARTS
    parts = [
        pltpu.make_async_copy(
            image_hbm.at[pl.ds(patch * PATCH, PATCH), pl.ds(k * width, width)],
            cells.at[:, pl.ds(k * width, width)],
            sems.at[k],
        )
        for k in range(PARTS)
    ]
    fetched = [
        pltpu.make_async_copy(a, b, sems.at[PARTS + k])
        for k, (a, b) in enumerate(zip(tables_hbm, tables))
    ]
    for copy in [fetched[0], parts[0], *fetched[1:], *parts[1:]]:
        copy.start()

    def ready(t, steps):
        if t == 0:
            fetched[0].wait()
        if t % (steps // PARTS) == 0:
            parts[t // (steps // PARTS)].wait()
        if t == steps - 1:
            fetched[1].wait()
            fetched[2].wait()

    image_kernel(0, cells, *tables, out_ref, swap, mid, ready)


def image_forward(image, patch):
    tables = (
        constant(x_forward(PATCH)),
        constant(z_forward(DEPTH, YPER)),
        constant(y_forward(PATCH, YPER)),
    )
    scratch = [
        pltpu.VMEM((2 * KX * YSTEP, LANES), F32),
        pltpu.VMEM((KX * YROWS, 2 * YPER * LANES), BF16),
    ]
    common = dict(
        out_shape=jax.ShapeDtypeStruct((KX, 2 * LONG, LANES), BF16),
        compiler_params=pltpu.CompilerParams(vmem_limit_bytes=16 << 20),
        cost_estimate=pl.CostEstimate(
            flops=4_000_000_000, bytes_accessed=4_000_000, transcendentals=0
        ),
    )
    if patch:
        return pl.pallas_call(
            functools.partial(image_kernel, patch),
            scratch_shapes=scratch,
            name="image_forward",
            **common,
        )(image, *tables)
    return pl.pallas_call(
        functools.partial(fetching_kernel, patch),
        in_specs=[pl.BlockSpec(memory_space=pltpu.HBM)] * 4,
        out_specs=pl.BlockSpec(memory_space=pltpu.VMEM),
        scratch_shapes=scratch
        + [pltpu.VMEM((PATCH, image.shape[1]), F32)]
        + [pltpu.VMEM(t.shape, BF16) for t in tables]
        + [pltpu.SemaphoreType.DMA((PARTS + len(tables),))],
        name="image_first",
        **common,
    )(*[pltpu.with_memory_space_constraint(x, pltpu.HBM) for x in (image, *tables)])


def blend_kernel(psfs_ref, odd_ref, even_ref, to_even_ref, to_odd_ref):
    count = psfs_ref.shape[0]
    gx, gy = parity("gx"), parity("gy")
    for out, column in ((to_even_ref, 1 - gy), (to_odd_ref, gy)):
        from_even = even_ref[0, column].astype(F32)
        from_odd = odd_ref[0, column].astype(F32)
        nodes = [pick(gx, from_odd, from_even)]
        nodes += [psfs_ref[i, column].astype(F32) for i in range(count)]
        nodes += [pick(gx, from_even, from_odd)]
        for p in range(count // 2):
            total = (nodes[2 * p] + nodes[2 * p + 3]) * BLEND[0]
            total += (nodes[2 * p + 1] + nodes[2 * p + 2]) * BLEND[1]
            out[p] = total.astype(BF16)


def blend_x(psfs, odd, even):
    shape = (psfs.shape[0] // 2,) + psfs.shape[2:]
    return pl.pallas_call(
        blend_kernel,
        out_shape=(jax.ShapeDtypeStruct(shape, BF16),) * 2,
        compiler_params=pltpu.CompilerParams(vmem_limit_bytes=16 << 20),
        name="blend_x",
    )(psfs, odd, even)


def y_inverted(tiy, product, rows_ref, p, t):
    back = dot(tiy[...], product).astype(BF16)
    pairs = back.shape[0] // (2 * YPER)
    for h in range(2):
        at = pl.ds(pl.multiple_of((2 * t + h) * pairs, pairs), pairs)
        for b in range(2 * YPER):
            rows_ref[p, at, b * LANES : (b + 1) * LANES] = back[
                b * pairs : (b + 1) * pairs, h * LANES : (h + 1) * LANES
            ]


def z_swapped(rows_ref, tiz, grid_ref, p, pairs, group):
    def along_z(t, _):
        start = pl.multiple_of(t * group * pairs, group * pairs)
        result = dot(rows_ref[p, pl.ds(start, group * pairs), :], tiz[...])
        for k in range(group):
            for c in range(2):
                grid_ref[p, c, pl.ds(t * group + k, pairs, stride=XSTEP), :] = result[
                    k * pairs : (k + 1) * pairs, c * LANES : (c + 1) * LANES
                ]
        return 0

    lax.fori_loop(0, KX // group, along_z, 0, unroll=True)


def x_inverted(grid_ref, tix, t):
    pieces = []
    for p in range(grid_ref.shape[0]):
        for c in range(2):
            parts = []
            for h in range(2):
                parts.append(grid_ref[p, c, pl.ds((2 * t + h) * XSTEP, KX), :])
            pieces.append(jnp.concatenate(parts, 1).astype(BF16))
    return dot(tix[...], jnp.concatenate(pieces, 0))


def respond_kernel(patches, *refs):
    spectra = refs[:patches]
    columns = refs[patches : patches + 4]
    tpx, tpz, tpy, tiy, tiz, tix = refs[patches + 4 : patches + 10]
    product_ref, to_even_ref, to_odd_ref = refs[patches + 10 : patches + 13]
    pswap, pmid, edge_rows, grid_x = refs[patches + 13 :]
    tile = 2 * LANES

    for p in range(patches):
        for t in range(PSFW * PSFW // tile):
            data = jnp.concatenate([c[p, :, t * tile : (t + 1) * tile] for c in columns], 0)
            result = dot(tpx[...], data)
            for h in range(2):
                pswap[p, pl.ds(2 * t + h, 2 * KX, stride=PROWS), :] = result[
                    :, h * LANES : (h + 1) * LANES
                ]
    half = KX * PROWS
    for p in range(patches):
        left = jnp.concatenate([pswap[p, :half, :], pswap[p, half:, :]], 1).astype(BF16)
        for b in range(PPER):
            result = dot(left, tpz[:, b * tile : (b + 1) * tile])
            result = result.reshape(KX, PROWS, tile)
            both = jnp.concatenate([result[:, :, :LANES], result[:, :, LANES:]], 1)
            pmid[p, :, 2 * b * PROWS : 2 * (b + 1) * PROWS, :] = both.astype(BF16)

    def along_y(t, _):
        for p in range(patches):
            psf = dot(tpy[...], jnp.concatenate([pmid[p, 2 * t], pmid[p, 2 * t + 1]], 1))
            psf = psf.astype(BF16)
            field = jnp.concatenate([spectra[p][2 * t], spectra[p][2 * t + 1]], 1)
            are, aim = field[:LONG], field[LONG:]
            bre, bim = psf[:LONG], psf[LONG:]
            product = jnp.concatenate([are * bre - aim * bim, are * bim + aim * bre], 0)
            product_ref[p, t] = product
        return 0

    lax.fori_loop(0, KX // 2, along_y, 0, unroll=True)

    def back_along_y(t, _):
        for p in range(patches):
            y_inverted(tiy, product_ref[p, t], edge_rows, p, t)
        return 0

    lax.fori_loop(0, KX // 2, back_along_y, 0, unroll=True)
    for p in range(patches):
        z_swapped(edge_rows, tiz, grid_x, p, EDGE, KX // 2)
    flag = parity("gy")
    rim = RIM // 2
    for out, first in ((to_even_ref, 1 - flag), (to_odd_ref, flag)):
        for t in range(rim):
            out[:, t * tile : (t + 1) * tile] = x_inverted(grid_x, tix, first * rim + t).astype(BF16)


def respond(spectra, columns):
    patches = len(spectra)
    weighted = np.concatenate([w * x_forward(PSFW) for w in BLEND], 1)
    edge_table, inner_table = [constant(t) for t in y_inverse()]
    z_table = constant(z_inverse())
    x_table = constant(x_inverse(patches))
    tables = (
        constant(weighted),
        constant(z_forward(PSFW, PPER)),
        constant(y_forward(PSFW, PPER)),
        edge_table,
        z_table,
        x_table,
    )
    rows = patches * PATCH + PSFW
    rim = (rows, HALF * DEPTH)
    inner = OROWS - EDGE
    product, out_even, out_odd = pl.pallas_call(
        functools.partial(respond_kernel, patches),
        out_shape=(
            jax.ShapeDtypeStruct((patches, KX // 2, 2 * LONG, 2 * LANES), BF16),
            jax.ShapeDtypeStruct(rim, BF16),
            jax.ShapeDtypeStruct(rim, BF16),
        ),
        scratch_shapes=[
            pltpu.VMEM((patches, 2 * KX * PROWS, LANES), F32),
            pltpu.VMEM((patches, KX, 2 * PSFW, LANES), BF16),
            pltpu.VMEM((patches, KX * EDGE, 2 * YPER * LANES), BF16),
            pltpu.VMEM((patches, 2, EDGE * XSTEP, LANES), F32),
        ],
        compiler_params=pltpu.CompilerParams(vmem_limit_bytes=24 << 20),
        name="respond",
    )(*spectra, *columns, *tables)

    def middle(even):
        return pl.pallas_call(
            middle_kernel,
            out_shape=(
                jax.ShapeDtypeStruct((rows, PATCH * DEPTH), F32),
                jax.ShapeDtypeStruct((HALF, PATCH * DEPTH), BF16),
                jax.ShapeDtypeStruct((HALF, PATCH * DEPTH), BF16),
            ),
            scratch_shapes=[
                pltpu.VMEM((patches, KX * inner, 2 * YPER * LANES), BF16),
                pltpu.VMEM((patches, 2, inner * XSTEP, LANES), F32),
            ],
            compiler_params=pltpu.CompilerParams(vmem_limit_bytes=24 << 20),
            cost_estimate=pl.CostEstimate(
                flops=3_000_000_000, bytes_accessed=6_000_000, transcendentals=0
            ),
            name="middle",
        )(product, even, inner_table, z_table, x_table)

    return middle, out_even, out_odd


def middle_kernel(
    product_ref, even_ref, tiy, tiz, tix, out_ref, to_odd_ref, to_even_ref, rows_ref, grid_x
):
    tile = 2 * LANES
    patches = product_ref.shape[0]
    inner = OROWS - EDGE

    def along_y(t, _):
        for p in range(patches):
            y_inverted(tiy, product_ref[p, t], rows_ref, p, t)
        return 0

    lax.fori_loop(0, KX // 2, along_y, 0, unroll=True)
    for p in range(patches):
        z_swapped(rows_ref, tiz, grid_x, p, inner, 8)
    for t in range(inner // 2):
        out_ref[:, t * tile : (t + 1) * tile] = x_inverted(grid_x, tix, t)
    x_rims(out_ref, even_ref, to_odd_ref, to_even_ref)


def x_rims(mid_ref, even_ref, to_odd_ref, to_even_ref):
    band = even_ref.shape[1]
    rows, columns = mid_ref.shape[0] - PSFW, mid_ref.shape[1]
    gx, gy = parity("gx"), parity("gy")
    corner = pl.ds(pl.multiple_of((1 - gy) * (columns - band), band), band)
    for out, side in ((to_odd_ref, gx), (to_even_ref, 1 - gx)):
        at = pl.ds(pl.multiple_of(rows + side * HALF, HALF), HALF)
        out[...] = mid_ref[at, :].astype(BF16)
        out[:, corner] = (mid_ref[at, corner] + even_ref[at, :].astype(F32)).astype(BF16)


def corner_kernel(odd_ref, to_odd_ref, to_even_ref):
    rows = odd_ref.shape[0] - PSFW
    gx = parity("gx")
    for out, side in ((to_odd_ref, gx), (to_even_ref, 1 - gx)):
        out[...] = odd_ref[pl.ds(pl.multiple_of(rows + side * HALF, HALF), HALF), :]


def x_corners(odd):
    shape = jax.ShapeDtypeStruct((HALF, odd.shape[1]), BF16)
    return pl.pallas_call(
        corner_kernel,
        out_shape=(shape,) * 2,
        compiler_params=pltpu.CompilerParams(vmem_limit_bytes=16 << 20),
        name="x_corners",
    )(odd)


def fold_kernel(mid_ref, even_ref, odd_ref, out_ref, rims_ref):
    rows, columns = out_ref.shape
    band = even_ref.shape[1]
    gy = parity("gy")
    out_ref[...] = mid_ref[:rows, :]
    for ref, side in ((even_ref, 1 - gy), (odd_ref, gy)):
        at = pl.ds(pl.multiple_of(side * (columns - band), band), band)
        out_ref[:, at] += ref[:rows, :].astype(F32)
    rims_ref[:HALF, :] = out_ref[:HALF, :]
    rims_ref[HALF:, :] = out_ref[rows - HALF :, :]


def fold(mid, even, odd):
    rows = mid.shape[0] - PSFW
    return pl.pallas_call(
        fold_kernel,
        out_shape=(
            jax.ShapeDtypeStruct((rows, mid.shape[1]), F32),
            jax.ShapeDtypeStruct((2 * HALF, mid.shape[1]), F32),
        ),
        compiler_params=pltpu.CompilerParams(vmem_limit_bytes=16 << 20),
        cost_estimate=pl.CostEstimate(
            flops=10_000_000, bytes_accessed=8_000_000, transcendentals=0
        ),
        name="fold",
    )(mid, even, odd)


def edges_kernel(out_in, rims_ref, even_ref, odd_ref, out_ref, corners_ref, total, sems):
    del out_in
    gx, gy = parity("gx"), parity("gy")
    rows, columns = out_ref.shape
    band = corners_ref.shape[2]
    far = pl.ds(pl.multiple_of(gy * (columns - band), band), band)
    copies = []
    for k, (ref, side) in enumerate(((even_ref, 1 - gx), (odd_ref, gx))):
        at = pl.ds(pl.multiple_of(side * HALF, HALF), HALF)
        total[k] = rims_ref[at, :] + ref[...].astype(F32)
        first = pl.multiple_of(side * (rows - HALF), HALF)
        copies.append(
            pltpu.make_async_copy(total.at[k], out_ref.at[pl.ds(first, HALF), :], sems.at[k])
        )
        copies[-1].start()
        corners_ref[k] = total[k, :, far]
    for copy in copies:
        copy.wait()


def close_kernel(out_in, corners_ref, even_ref, odd_ref, out_ref, total, sems):
    del out_in
    gx, gy = parity("gx"), parity("gy")
    rows, columns = out_ref.shape
    band = even_ref.shape[1]
    far = pl.ds(pl.multiple_of(gy * (columns - band), band), band)
    copies = []
    for k, (ref, side) in enumerate(((even_ref, 1 - gx), (odd_ref, gx))):
        total[k] = corners_ref[k] + ref[...].astype(F32)
        at = pl.ds(pl.multiple_of(side * (rows - HALF), HALF), HALF)
        copies.append(pltpu.make_async_copy(total.at[k], out_ref.at[at, far], sems.at[k]))
        copies[-1].start()
    for copy in copies:
        copy.wait()


def close(kernel, name, width, out, kept, even, odd):
    vmem, anywhere = pl.BlockSpec(memory_space=pltpu.VMEM), pl.BlockSpec(memory_space=pl.ANY)
    corners = jax.ShapeDtypeStruct((2, HALF, HALF * DEPTH), F32)
    first = kernel is edges_kernel
    shape = jax.ShapeDtypeStruct(out.shape, F32)
    return pl.pallas_call(
        kernel,
        in_specs=[anywhere, vmem, vmem, vmem],
        out_specs=(anywhere, vmem) if first else anywhere,
        out_shape=(shape, corners) if first else shape,
        scratch_shapes=[
            pltpu.VMEM((2, HALF, width), F32),
            pltpu.SemaphoreType.DMA((2,)),
        ],
        input_output_aliases={0: 0},
        compiler_params=pltpu.CompilerParams(vmem_limit_bytes=16 << 20),
        name=name,
    )(out, kept, even, odd)


def swap_even(value, axis):
    count = lax.axis_size(axis)
    return lax.ppermute(value, axis, [(i, i ^ 1) for i in range(count) if i ^ 1 < count])


def swap_odd(value, axis):
    ends = [i + 1 if i % 2 else i - 1 for i in range(lax.axis_size(axis))]
    pairs = [(i, j) for i, j in enumerate(ends) if 0 <= j < len(ends)]
    return lax.ppermute(value, axis, pairs)


def body(image, psfs):
    patches = image.shape[0] // PATCH
    last = psfs.shape[0] - 1
    gx = parity("gx")
    to_odd = lax.dynamic_slice_in_dim(psfs, gx * last, 1, 0)
    to_even = lax.dynamic_slice_in_dim(psfs, (1 - gx) * last, 1, 0)
    even = swap_even(to_even, "gx")
    odd = swap_odd(to_odd, "gx")
    spectra = [image_forward(image, 0)]
    spectra[0], odd, even = lax.optimization_barrier((spectra[0], odd, even))
    to_even, to_odd = blend_x(psfs, odd, even)
    image, to_even, to_odd = lax.optimization_barrier((image, to_even, to_odd))
    even = swap_even(to_even, "gy")
    odd = swap_odd(to_odd, "gy")
    spectra += [image_forward(image, p) for p in range(1, patches)]
    middle, out_even, out_odd = respond(spectra, (even, to_even, to_odd, odd))
    odd_y = swap_odd(out_odd, "gy")
    even_y = swap_even(out_even, "gy")
    mid, out_odd, out_even = middle(even_y)
    even_x = swap_even(out_even, "gx")
    odd_x = swap_odd(out_odd, "gx")
    out_odd, out_even = x_corners(odd_y)
    even_corner = swap_even(out_even, "gx")
    odd_corner = swap_odd(out_odd, "gx")
    out, rims = fold(mid, even_y, odd_y)
    out, corners = close(edges_kernel, "edges", out.shape[1], out, rims, even_x, odd_x)
    return close(close_kernel, "corners", HALF * DEPTH, out, corners, even_corner, odd_corner)


def solution(mesh):
    placed = (P("gx", "gy"), P("gx", "gy", None, None))
    return jax.shard_map(body, mesh=mesh, in_specs=placed, out_specs=P("gx", "gy"), check_vma=False)
```

```python
import functools
import math

import jax
import jax.numpy as jnp
import ml_dtypes
import numpy as np
from jax import lax
from jax.experimental import pallas as pl
from jax.experimental.pallas import tpu as pltpu
from jax.sharding import PartitionSpec as P

PATCH = 64
PSFW = 32
DEPTH = 64
BLEND = (0.125, 0.375, 0.375, 0.125)

HALF = PSFW // 2
LONG = PATCH + PSFW
KX = LONG // 2
KZ = DEPTH + HALF
LANES = 128
YPER = LANES // DEPTH
PPER = LANES // PSFW
YROWS = PATCH // YPER
PROWS = PSFW // PPER
OROWS = LONG // YPER
RIM = HALF // YPER
EDGE = 2 * RIM
YSTEP = YROWS + 2
XSTEP = KX + 2
F32 = jnp.float32
BF16 = jnp.bfloat16


def constant(values):
    return jnp.asarray(np.asarray(values, np.float32).astype(ml_dtypes.bfloat16))


def angle(k, n, length):
    return 2.0 * math.pi * np.outer(k, n) / length


def complex_block(theta, sign):
    cosine, sine = np.cos(theta), sign * np.sin(theta)
    return np.stack([np.stack([cosine, -sine], 1), np.stack([sine, cosine], 1)], 0)


def x_forward(count):
    theta = angle(np.arange(KX) + 0.5, np.arange(count), LONG)
    return np.concatenate([np.cos(theta), -np.sin(theta)], 0)


def z_forward(count, per):
    block = complex_block(angle(np.arange(KZ), np.arange(count), KZ), -1.0)
    table = np.zeros((2, per, count, per, 2, LANES))
    for y in range(per):
        table[:, y, :, y, :, :KZ] = block.transpose(2, 3, 0, 1)
    return table.reshape(2 * per * count, per * 2 * LANES)


def y_forward(count, per):
    block = complex_block(angle(np.arange(LONG), np.arange(count), LONG), -1.0)
    block = block.reshape(2, LONG, 2, count // per, per).transpose(0, 1, 4, 2, 3)
    return block.reshape(2 * LONG, 2 * count)


def y_inverse():
    block = complex_block(angle(np.arange(LONG), np.arange(LONG), LONG).T, 1.0) / LONG
    block = block.reshape(2, OROWS, YPER, 2 * LONG).transpose(2, 0, 1, 3)
    edge = np.concatenate([block[:, :, :RIM], block[:, :, -RIM:]], 2)
    inner = block[:, :, RIM:-RIM]
    return edge.reshape(-1, 2 * LONG), inner.reshape(-1, 2 * LONG)


def z_inverse():
    block = complex_block(angle(np.arange(DEPTH) + HALF, np.arange(KZ), KZ), 1.0) / KZ
    table = np.zeros((YPER, 2, LANES, 2, YPER, DEPTH))
    for y in range(YPER):
        table[y, :, :KZ, :, y, :] = block.transpose(2, 3, 0, 1)
    return table.reshape(YPER * 2 * LANES, 2 * YPER * DEPTH)


def x_inverse(patches):
    theta = angle(np.arange(LONG), np.arange(KX) + 0.5, LONG)
    block = np.stack([np.cos(theta), -np.sin(theta)], 1) * (2.0 / LONG)
    rows = patches * PATCH
    table = np.zeros((rows + PSFW, patches, 2, KX))
    for p in range(patches):
        table[p * PATCH : p * PATCH + LONG, p] = block
    table = np.concatenate([table[HALF : HALF + rows], table[:HALF], table[HALF + rows :]], 0)
    return table.reshape(rows + PSFW, patches * 2 * KX)


def dot(a, b):
    return jnp.dot(a, b, preferred_element_type=F32)


def full(shape):
    return pl.BlockSpec(shape, lambda *_: (0,) * len(shape))


def parity(axis):
    return lax.rem(lax.axis_index(axis), 2)


def pick(flag, even, odd):
    return jnp.where(flag == 0, even, odd)


def image_kernel(patch, image_ref, tx_ref, tz_ref, ty_ref, out_ref, swap, mid, ready=None):
    tile = 2 * LANES
    rows = 2 * KX

    def along_x(t, _):
        at = pl.ds(pl.multiple_of(t * tile, tile), tile)
        cells = image_ref[patch * PATCH : (patch + 1) * PATCH, at].astype(BF16)
        result = dot(tx_ref[...], cells)
        for h in range(2):
            swap[pl.ds(2 * t + h, rows, stride=YSTEP), :] = result[:, h * LANES : (h + 1) * LANES]
        return 0

    steps = PATCH * DEPTH // tile
    if ready is None:
        lax.fori_loop(0, steps, along_x, 0, unroll=8)
    else:
        for t in range(steps):
            ready(t, steps)
            along_x(t, 0)

    group = 8

    def along_z(t):
        left = [
            jnp.concatenate(
                [
                    swap[pl.ds((c * KX + t * group + k) * YSTEP, YROWS), :].astype(BF16)
                    for k in range(group)
                ],
                0,
            )
            for c in range(2)
        ]
        chunk = group * YROWS
        result = dot(jnp.concatenate(left, 1), tz_ref[...])
        mid[t * chunk : (t + 1) * chunk, :] = result.astype(BF16)

    for t in range(KX // group):
        along_z(t)

    def along_y(t, _):
        pieces = []
        for h in range(2):
            rows_at = pl.ds(pl.multiple_of((2 * t + h) * YROWS, YROWS), YROWS)
            pieces.append(
                jnp.concatenate(
                    [mid[rows_at, b * LANES : (b + 1) * LANES] for b in range(2 * YPER)], 0
                )
            )
        result = dot(ty_ref[...], jnp.concatenate(pieces, 1)).astype(BF16)
        for h in range(2):
            out_ref[2 * t + h] = result[:, h * LANES : (h + 1) * LANES]
        return 0

    lax.fori_loop(0, KX // 2, along_y, 0, unroll=True)


PARTS = 4


def fetching_kernel(patch, image_hbm, *refs):
    tables_hbm, out_ref, swap, mid, cells = refs[:3], *refs[3:7]
    tables, sems = refs[7:10], refs[10]
    width = cells.shape[1] // PARTS
    parts = [
        pltpu.make_async_copy(
            image_hbm.at[pl.ds(patch * PATCH, PATCH), pl.ds(k * width, width)],
            cells.at[:, pl.ds(k * width, width)],
            sems.at[k],
        )
        for k in range(PARTS)
    ]
    fetched = [
        pltpu.make_async_copy(a, b, sems.at[PARTS + k])
        for k, (a, b) in enumerate(zip(tables_hbm, tables))
    ]
    for copy in [fetched[0], parts[0], *fetched[1:], *parts[1:]]:
        copy.start()

    def ready(t, steps):
        if t == 0:
            fetched[0].wait()
        if t % (steps // PARTS) == 0:
            parts[t // (steps // PARTS)].wait()
        if t == steps - 1:
            fetched[1].wait()
            fetched[2].wait()

    image_kernel(0, cells, *tables, out_ref, swap, mid, ready)


def image_forward(image, patch):
    tables = (
        constant(x_forward(PATCH)),
        constant(z_forward(DEPTH, YPER)),
        constant(y_forward(PATCH, YPER)),
    )
    scratch = [
        pltpu.VMEM((2 * KX * YSTEP, LANES), F32),
        pltpu.VMEM((KX * YROWS, 2 * YPER * LANES), BF16),
    ]
    common = dict(
        out_shape=jax.ShapeDtypeStruct((KX, 2 * LONG, LANES), BF16),
        compiler_params=pltpu.CompilerParams(vmem_limit_bytes=16 << 20),
        cost_estimate=pl.CostEstimate(
            flops=4_000_000_000, bytes_accessed=4_000_000, transcendentals=0
        ),
    )
    if patch:
        return pl.pallas_call(
            functools.partial(image_kernel, patch),
            scratch_shapes=scratch,
            name="image_forward",
            **common,
        )(image, *tables)
    return pl.pallas_call(
        functools.partial(fetching_kernel, patch),
        in_specs=[pl.BlockSpec(memory_space=pltpu.HBM)] * 4,
        out_specs=pl.BlockSpec(memory_space=pltpu.VMEM),
        scratch_shapes=scratch
        + [pltpu.VMEM((PATCH, image.shape[1]), F32)]
        + [pltpu.VMEM(t.shape, BF16) for t in tables]
        + [pltpu.SemaphoreType.DMA((PARTS + len(tables),))],
        name="image_first",
        **common,
    )(*[pltpu.with_memory_space_constraint(x, pltpu.HBM) for x in (image, *tables)])


def blend_kernel(psfs_ref, odd_ref, even_ref, to_even_ref, to_odd_ref):
    count = psfs_ref.shape[0]
    gx, gy = parity("gx"), parity("gy")
    for out, column in ((to_even_ref, 1 - gy), (to_odd_ref, gy)):
        from_even = even_ref[0, column].astype(F32)
        from_odd = odd_ref[0, column].astype(F32)
        nodes = [pick(gx, from_odd, from_even)]
        nodes += [psfs_ref[i, column].astype(F32) for i in range(count)]
        nodes += [pick(gx, from_even, from_odd)]
        for p in range(count // 2):
            total = (nodes[2 * p] + nodes[2 * p + 3]) * BLEND[0]
            total += (nodes[2 * p + 1] + nodes[2 * p + 2]) * BLEND[1]
            out[p] = total.astype(BF16)


def blend_x(psfs, odd, even):
    shape = (psfs.shape[0] // 2,) + psfs.shape[2:]
    return pl.pallas_call(
        blend_kernel,
        out_shape=(jax.ShapeDtypeStruct(shape, BF16),) * 2,
        compiler_params=pltpu.CompilerParams(vmem_limit_bytes=16 << 20),
        name="blend_x",
    )(psfs, odd, even)


def y_inverted(tiy, product, rows_ref, p, t):
    back = dot(tiy[...], product).astype(BF16)
    pairs = back.shape[0] // (2 * YPER)
    for h in range(2):
        at = pl.ds(pl.multiple_of((2 * t + h) * pairs, pairs), pairs)
        for b in range(2 * YPER):
            rows_ref[p, at, b * LANES : (b + 1) * LANES] = back[
                b * pairs : (b + 1) * pairs, h * LANES : (h + 1) * LANES
            ]


def z_swapped(rows_ref, tiz, grid_ref, p, pairs, group):
    def along_z(t, _):
        start = pl.multiple_of(t * group * pairs, group * pairs)
        result = dot(rows_ref[p, pl.ds(start, group * pairs), :], tiz[...])
        for k in range(group):
            for c in range(2):
                grid_ref[p, c, pl.ds(t * group + k, pairs, stride=XSTEP), :] = result[
                    k * pairs : (k + 1) * pairs, c * LANES : (c + 1) * LANES
                ]
        return 0

    lax.fori_loop(0, KX // group, along_z, 0, unroll=True)


def x_inverted(grid_ref, tix, t):
    pieces = []
    for p in range(grid_ref.shape[0]):
        for c in range(2):
            parts = []
            for h in range(2):
                parts.append(grid_ref[p, c, pl.ds((2 * t + h) * XSTEP, KX), :])
            pieces.append(jnp.concatenate(parts, 1).astype(BF16))
    return dot(tix[...], jnp.concatenate(pieces, 0))


def respond_kernel(patches, *refs):
    spectra = refs[:patches]
    columns = refs[patches : patches + 4]
    tpx, tpz, tpy, tiy, tiz, tix = refs[patches + 4 : patches + 10]
    product_ref, to_even_ref, to_odd_ref = refs[patches + 10 : patches + 13]
    pswap, pmid, edge_rows, grid_x = refs[patches + 13 :]
    tile = 2 * LANES

    for p in range(patches):
        for t in range(PSFW * PSFW // tile):
            data = jnp.concatenate([c[p, :, t * tile : (t + 1) * tile] for c in columns], 0)
            result = dot(tpx[...], data)
            for h in range(2):
                pswap[p, pl.ds(2 * t + h, 2 * KX, stride=PROWS), :] = result[
                    :, h * LANES : (h + 1) * LANES
                ]
    half = KX * PROWS
    for p in range(patches):
        left = jnp.concatenate([pswap[p, :half, :], pswap[p, half:, :]], 1).astype(BF16)
        for b in range(PPER):
            result = dot(left, tpz[:, b * tile : (b + 1) * tile])
            result = result.reshape(KX, PROWS, tile)
            both = jnp.concatenate([result[:, :, :LANES], result[:, :, LANES:]], 1)
            pmid[p, :, 2 * b * PROWS : 2 * (b + 1) * PROWS, :] = both.astype(BF16)

    def along_y(t, _):
        for p in range(patches):
            psf = dot(tpy[...], jnp.concatenate([pmid[p, 2 * t], pmid[p, 2 * t + 1]], 1))
            psf = psf.astype(BF16)
            field = jnp.concatenate([spectra[p][2 * t], spectra[p][2 * t + 1]], 1)
            are, aim = field[:LONG], field[LONG:]
            bre, bim = psf[:LONG], psf[LONG:]
            product = jnp.concatenate([are * bre - aim * bim, are * bim + aim * bre], 0)
            product_ref[p, t] = product
        return 0

    lax.fori_loop(0, KX // 2, along_y, 0, unroll=True)

    def back_along_y(t, _):
        for p in range(patches):
            y_inverted(tiy, product_ref[p, t], edge_rows, p, t)
        return 0

    lax.fori_loop(0, KX // 2, back_along_y, 0, unroll=True)
    for p in range(patches):
        z_swapped(edge_rows, tiz, grid_x, p, EDGE, KX // 2)
    flag = parity("gy")
    rim = RIM // 2
    for out, first in ((to_even_ref, 1 - flag), (to_odd_ref, flag)):
        for t in range(rim):
            out[:, t * tile : (t + 1) * tile] = x_inverted(grid_x, tix, first * rim + t).astype(BF16)


def respond(spectra, columns):
    patches = len(spectra)
    weighted = np.concatenate([w * x_forward(PSFW) for w in BLEND], 1)
    edge_table, inner_table = [constant(t) for t in y_inverse()]
    z_table = constant(z_inverse())
    x_table = constant(x_inverse(patches))
    tables = (
        constant(weighted),
        constant(z_forward(PSFW, PPER)),
        constant(y_forward(PSFW, PPER)),
        edge_table,
        z_table,
        x_table,
    )
    rows = patches * PATCH + PSFW
    rim = (rows, HALF * DEPTH)
    inner = OROWS - EDGE
    product, out_even, out_odd = pl.pallas_call(
        functools.partial(respond_kernel, patches),
        out_shape=(
            jax.ShapeDtypeStruct((patches, KX // 2, 2 * LONG, 2 * LANES), BF16),
            jax.ShapeDtypeStruct(rim, BF16),
            jax.ShapeDtypeStruct(rim, BF16),
        ),
        scratch_shapes=[
            pltpu.VMEM((patches, 2 * KX * PROWS, LANES), F32),
            pltpu.VMEM((patches, KX, 2 * PSFW, LANES), BF16),
            pltpu.VMEM((patches, KX * EDGE, 2 * YPER * LANES), BF16),
            pltpu.VMEM((patches, 2, EDGE * XSTEP, LANES), F32),
        ],
        compiler_params=pltpu.CompilerParams(vmem_limit_bytes=24 << 20),
        name="respond",
    )(*spectra, *columns, *tables)

    def bands():
        return pl.pallas_call(
            bands_kernel,
            out_shape=(
                jax.ShapeDtypeStruct((patches, 2, inner * XSTEP, LANES), F32),
                jax.ShapeDtypeStruct((PSFW, PATCH * DEPTH), F32),
            ),
            scratch_shapes=[pltpu.VMEM((patches, KX * inner, 2 * YPER * LANES), BF16)],
            compiler_params=pltpu.CompilerParams(vmem_limit_bytes=20 << 20),
            cost_estimate=pl.CostEstimate(
                flops=2_000_000_000, bytes_accessed=6_000_000, transcendentals=0
            ),
            name="bands",
        )(product, inner_table, z_table, x_table[rows - PSFW :])

    return bands, x_table[: rows - PSFW], out_even, out_odd


def bands_kernel(product_ref, tiy, tiz, tix, grid_x, out_ref, rows_ref):
    tile = 2 * LANES
    patches = product_ref.shape[0]
    inner = OROWS - EDGE

    def along_y(t, _):
        for p in range(patches):
            y_inverted(tiy, product_ref[p, t], rows_ref, p, t)
        return 0

    lax.fori_loop(0, KX // 2, along_y, 0, unroll=True)
    for p in range(patches):
        z_swapped(rows_ref, tiz, grid_x, p, inner, 8)
    for t in range(inner // 2):
        out_ref[:, t * tile : (t + 1) * tile] = x_inverted(grid_x, tix, t)


def rim_kernel(band_ref, even_ref, to_odd_ref, to_even_ref):
    width = even_ref.shape[1]
    rows, columns = even_ref.shape[0] - PSFW, band_ref.shape[1]
    gx, gy = parity("gx"), parity("gy")
    corner = pl.ds(pl.multiple_of((1 - gy) * (columns - width), width), width)
    for out, side in ((to_odd_ref, gx), (to_even_ref, 1 - gx)):
        at = pl.ds(pl.multiple_of(side * HALF, HALF), HALF)
        even_at = pl.ds(pl.multiple_of(rows + side * HALF, HALF), HALF)
        out[...] = band_ref[at, :].astype(BF16)
        out[:, corner] = (band_ref[at, corner] + even_ref[even_at, :].astype(F32)).astype(BF16)


def x_rims(band, even):
    shape = jax.ShapeDtypeStruct((HALF, band.shape[1]), BF16)
    return pl.pallas_call(
        rim_kernel,
        out_shape=(shape,) * 2,
        compiler_params=pltpu.CompilerParams(vmem_limit_bytes=16 << 20),
        name="x_rims",
    )(band, even)


def corner_kernel(odd_ref, to_odd_ref, to_even_ref):
    rows = odd_ref.shape[0] - PSFW
    gx = parity("gx")
    for out, side in ((to_odd_ref, gx), (to_even_ref, 1 - gx)):
        out[...] = odd_ref[pl.ds(pl.multiple_of(rows + side * HALF, HALF), HALF), :]


def x_corners(odd):
    shape = jax.ShapeDtypeStruct((HALF, odd.shape[1]), BF16)
    return pl.pallas_call(
        corner_kernel,
        out_shape=(shape,) * 2,
        compiler_params=pltpu.CompilerParams(vmem_limit_bytes=16 << 20),
        name="x_corners",
    )(odd)


def fold_kernel(grid_x, tix, even_ref, odd_ref, out_ref, rims_ref):
    rows, columns = out_ref.shape
    tile = 2 * LANES
    band = even_ref.shape[1]
    gy = parity("gy")
    for t in range(columns // tile):
        out_ref[:, t * tile : (t + 1) * tile] = x_inverted(grid_x, tix, t)
    for ref, side in ((even_ref, 1 - gy), (odd_ref, gy)):
        at = pl.ds(pl.multiple_of(side * (columns - band), band), band)
        out_ref[:, at] += ref[:rows, :].astype(F32)
    rims_ref[:HALF, :] = out_ref[:HALF, :]
    rims_ref[HALF:, :] = out_ref[rows - HALF :, :]


def fold(grid, table, even, odd):
    rows, columns = table.shape[0], PATCH * DEPTH
    return pl.pallas_call(
        fold_kernel,
        out_shape=(
            jax.ShapeDtypeStruct((rows, columns), F32),
            jax.ShapeDtypeStruct((2 * HALF, columns), F32),
        ),
        compiler_params=pltpu.CompilerParams(vmem_limit_bytes=16 << 20),
        cost_estimate=pl.CostEstimate(
            flops=200_000_000, bytes_accessed=8_000_000, transcendentals=0
        ),
        name="fold",
    )(grid, table, even, odd)


def edges_kernel(out_in, rims_ref, even_ref, odd_ref, out_ref, corners_ref, total, sems):
    del out_in
    gx, gy = parity("gx"), parity("gy")
    rows, columns = out_ref.shape
    band = corners_ref.shape[2]
    far = pl.ds(pl.multiple_of(gy * (columns - band), band), band)
    copies = []
    for k, (ref, side) in enumerate(((even_ref, 1 - gx), (odd_ref, gx))):
        at = pl.ds(pl.multiple_of(side * HALF, HALF), HALF)
        total[k] = rims_ref[at, :] + ref[...].astype(F32)
        first = pl.multiple_of(side * (rows - HALF), HALF)
        copies.append(
            pltpu.make_async_copy(total.at[k], out_ref.at[pl.ds(first, HALF), :], sems.at[k])
        )
        copies[-1].start()
        corners_ref[k] = total[k, :, far]
    for copy in copies:
        copy.wait()


def close_kernel(out_in, corners_ref, even_ref, odd_ref, out_ref, total, sems):
    del out_in
    gx, gy = parity("gx"), parity("gy")
    rows, columns = out_ref.shape
    band = even_ref.shape[1]
    far = pl.ds(pl.multiple_of(gy * (columns - band), band), band)
    copies = []
    for k, (ref, side) in enumerate(((even_ref, 1 - gx), (odd_ref, gx))):
        total[k] = corners_ref[k] + ref[...].astype(F32)
        at = pl.ds(pl.multiple_of(side * (rows - HALF), HALF), HALF)
        copies.append(pltpu.make_async_copy(total.at[k], out_ref.at[at, far], sems.at[k]))
        copies[-1].start()
    for copy in copies:
        copy.wait()


def close(kernel, name, width, out, kept, even, odd):
    vmem, anywhere = pl.BlockSpec(memory_space=pltpu.VMEM), pl.BlockSpec(memory_space=pl.ANY)
    corners = jax.ShapeDtypeStruct((2, HALF, HALF * DEPTH), F32)
    first = kernel is edges_kernel
    shape = jax.ShapeDtypeStruct(out.shape, F32)
    return pl.pallas_call(
        kernel,
        in_specs=[anywhere, vmem, vmem, vmem],
        out_specs=(anywhere, vmem) if first else anywhere,
        out_shape=(shape, corners) if first else shape,
        scratch_shapes=[
            pltpu.VMEM((2, HALF, width), F32),
            pltpu.SemaphoreType.DMA((2,)),
        ],
        input_output_aliases={0: 0},
        compiler_params=pltpu.CompilerParams(vmem_limit_bytes=16 << 20),
        name=name,
    )(out, kept, even, odd)


def swap_even(value, axis):
    count = lax.axis_size(axis)
    return lax.ppermute(value, axis, [(i, i ^ 1) for i in range(count) if i ^ 1 < count])


def swap_odd(value, axis):
    ends = [i + 1 if i % 2 else i - 1 for i in range(lax.axis_size(axis))]
    pairs = [(i, j) for i, j in enumerate(ends) if 0 <= j < len(ends)]
    return lax.ppermute(value, axis, pairs)


def body(image, psfs):
    patches = image.shape[0] // PATCH
    last = psfs.shape[0] - 1
    gx = parity("gx")
    to_odd = lax.dynamic_slice_in_dim(psfs, gx * last, 1, 0)
    to_even = lax.dynamic_slice_in_dim(psfs, (1 - gx) * last, 1, 0)
    even = swap_even(to_even, "gx")
    odd = swap_odd(to_odd, "gx")
    spectra = [image_forward(image, 0)]
    spectra[0], odd, even = lax.optimization_barrier((spectra[0], odd, even))
    to_even, to_odd = blend_x(psfs, odd, even)
    image, to_even, to_odd = lax.optimization_barrier((image, to_even, to_odd))
    even = swap_even(to_even, "gy")
    odd = swap_odd(to_odd, "gy")
    spectra += [image_forward(image, p) for p in range(1, patches)]
    bands, table, out_even, out_odd = respond(spectra, (even, to_even, to_odd, odd))
    odd_y = swap_odd(out_odd, "gy")
    even_y = swap_even(out_even, "gy")
    grid, band = bands()
    out_odd, out_even = x_rims(band, even_y)
    even_x = swap_even(out_even, "gx")
    odd_x = swap_odd(out_odd, "gx")
    out_odd, out_even = x_corners(odd_y)
    even_corner = swap_even(out_even, "gx")
    odd_corner = swap_odd(out_odd, "gx")
    out, rims = fold(grid, table, even_y, odd_y)
    out, corners = close(edges_kernel, "edges", out.shape[1], out, rims, even_x, odd_x)
    return close(close_kernel, "corners", HALF * DEPTH, out, corners, even_corner, odd_corner)


def solution(mesh):
    placed = (P("gx", "gy"), P("gx", "gy", None, None))
    return jax.shard_map(body, mesh=mesh, in_specs=placed, out_specs=P("gx", "gy"), check_vma=False)
```
